32 devices in a mesh: fsdp: 8 (over y, x, core), tp: 4 (over z).
Axes of the slice: x: 2, y: 2, z: 4, core: 2. Of those that a mesh axis runs over, the one named last changes fastest.
Arguments:
- inputs: bfloat16 [8192, 2048], P(('fsdp', 'tp')), may hold values from -6 to 6
- query_weight: bfloat16 [2048, 2048], P('fsdp', 'tp'), may hold values from -0.125 to 0.125
- query_bias: float32 [2048], P('tp'), may hold values from -3 to 3
- key_weight: bfloat16 [2048, 2048], P('fsdp', 'tp'), may hold values from -0.125 to 0.125
- value_weight: bfloat16 [2048, 2048], P('fsdp', 'tp'), may hold values from -0.125 to 0.125
- value_bias: float32 [2048], P('tp'), may hold values from -3 to 3
- output_weight: bfloat16 [2048, 2048], P('tp', 'fsdp'), may hold values from -0.75 to 0.75
- output_bias: float32 [2048], replicated, may hold values from -3 to 3
- first_gain: float32 [2048], replicated, may hold values from 0.5 to 1.5
- first_shift: float32 [2048], replicated, may hold values from -3 to 3
- up_weight: bfloat16 [2048, 8192], P('fsdp', 'tp'), may hold values from -0.125 to 0.125
- up_bias: float32 [8192], P('tp'), may hold values from -3 to 3
- down_weight: bfloat16 [8192, 2048], P('tp', 'fsdp'), may hold values from -0.125 to 0.125
- down_bias: float32 [2048], replicated, may hold values from -3 to 3
- second_gain: float32 [2048], replicated, may hold values from 0.5 to 1.5
- second_shift: float32 [2048], replicated, may hold values from -3 to 3
- segments: int32 [8, 1024], P('fsdp'), may hold values from 0 to 7, never falling along the last dimension, each value on 1 to 512 neighbouring positions
- cotangent: bfloat16 [8192, 2048], P(('fsdp', 'tp')), may hold values from -6 to 6
Outputs:
- layer_out: bfloat16 [8192, 2048], P(('fsdp', 'tp'))
- input_grad: bfloat16 [8192, 2048], P(('fsdp', 'tp'))
- query_weight_grad: float32 [2048, 2048], P('fsdp', 'tp')
- query_bias_grad: float32 [4, 512], P('tp', 'fsdp')
- key_weight_grad: float32 [2048, 2048], P('fsdp', 'tp')
- value_weight_grad: float32 [2048, 2048], P('fsdp', 'tp')
- value_bias_grad: float32 [4, 512], P('tp', 'fsdp')
- output_weight_grad: float32 [2048, 2048], P('tp', 'fsdp')
- output_bias_grad: float32 [2048], P(('fsdp', 'tp'))
- first_gain_grad: float32 [2048], P(('fsdp', 'tp'))
- first_shift_grad: float32 [2048], P(('fsdp', 'tp'))
- up_weight_grad: float32 [2048, 8192], P('fsdp', 'tp')
- up_bias_grad: float32 [4, 2048], P('tp', 'fsdp')
- down_weight_grad: float32 [8192, 2048], P('tp', 'fsdp')
- down_bias_grad: float32 [2048], P(('fsdp', 'tp'))
- second_gain_grad: float32 [2048], P(('fsdp', 'tp'))
- second_shift_grad: float32 [2048], P(('fsdp', 'tp'))
The draws below stay inside these ranges and needn't reach their ends.
Inputs may be any that keep to these rules, and one draw needn't show every extreme that they name: `segments`: within a sequence the numbers never fall; one number marks one document of 1 to 512 tokens, and one document of each sequence has exactly 512.
All inputs are finite; a program needn't handle non-finite values.
Results may differ from the reference program's by a relative error of at most 0.019.
Values may be sent and summed in bfloat16 or wider, within the bound.
A program may use at most 192 MiB of HBM per device.

```python
import math
import jax
import jax.numpy as jnp
import numpy as np
from jax import lax

D = 2048
HEADS = 16
HD = 128
FF = 8192
LEN = 1024
DOCS = 8
SEQS = 8
TOKENS = 8192
DOC_MOST = 512
N_TP = 4


def raised(drawn, key, source, target, parts, factor):
    def block_of(position):
        return (jnp.arange(drawn.shape[position]) // (drawn.shape[position] // parts)).reshape((-1,) + (1,) * (drawn.ndim - 1 - position))

    near = jax.random.permutation(key, parts)[block_of(target)]
    far = (block_of(target) + parts // 2) % parts
    return jnp.where((block_of(source) == near) | (block_of(source) == far), factor * drawn, drawn)


def block_levels(own_key, shape, shards, least, largest):
    loudness, own = 1.0, jax.random.fold_in(own_key, 6)
    for axis_at, parts in shards:
        heights = jnp.exp(jax.random.uniform(jax.random.fold_in(own, axis_at), (parts,), jnp.float32, least / len(shards), largest / len(shards)))
        loudness = loudness * jnp.repeat(heights, shape[axis_at] // parts).reshape([-1 if axis == axis_at else 1 for axis in range(len(shape))])
    return loudness


def profile(amount, total, most, lean):
    portions = [(1 << 20) // math.isqrt(rank ** lean) + 1 for rank in range(2, amount + 1)]
    spare, holding = total - most - (amount - 1), [1] * (amount - 1)
    while spare > 0:
        free = [i for i in range(amount - 1) if holding[i] < most]
        pool, budget = sum([portions[i] for i in free]), spare
        for i in free:
            addition = min(most - holding[i], max(1, budget * portions[i] // pool), spare)
            holding[i] = holding[i] + addition
            spare = spare - addition
    return np.array([most] + holding)


def uneven(key, count, total, bound, skew):
    if count == 2:
        one = jax.random.randint(key, (), max(1, total - bound), min(bound, total - 1) + 1)
        return jnp.stack([one, total - one])
    sizes = jnp.asarray(profile(count, total, bound, skew), jnp.int32)
    couples = (count - 1) // 2
    donor, sink = sizes[1:1 + 2 * couples:2], sizes[2:2 + 2 * couples:2]
    slack = jnp.minimum(donor - 1, bound - sink)
    passed = jax.random.randint(jax.random.fold_in(key, 1), (couples,), 0, 1 << 20) % (slack + 1)
    sizes = sizes.at[1:1 + 2 * couples:2].set(donor - passed).at[2:2 + 2 * couples:2].set(sink + passed)
    return sizes[jax.random.permutation(jax.random.fold_in(key, 2), count)]


def bell_draw(own_key, dims, scale, most, split=(), dtype=jnp.bfloat16):
    values = scale * jax.random.normal(own_key, dims, jnp.float32)
    if split:
        values = values * block_levels(own_key, dims, split, -0.22, 0.18)
    return jnp.clip(values, -most, most).astype(dtype)


def heavy_noise(rng, extent, width, bound, cuts, heavy, kind=jnp.bfloat16):
    values = width * jax.random.normal(rng, extent, jnp.float32)
    if cuts:
        values = values * block_levels(rng, extent, cuts, -0.22, 0.18)
    return jnp.clip(raised(values, jax.random.fold_in(rng, 3), *heavy), -bound, bound).astype(kind)


def setup_inputs(seed: int = 0) -> dict:
    key_list = jax.random.split(jax.random.key(seed), 19)
    inputs = bell_draw(key_list[0], (TOKENS, D), 1.0, 6.0, ((0, 32),))
    query_weight = bell_draw(key_list[1], (D, D), D ** -0.5, 0.125, ((0, 8), (1, 4)))
    query_bias = bell_draw(key_list[2], (D,), 0.5, 3.0, ((0, 4),), jnp.float32)
    key_weight = bell_draw(key_list[3], (D, D), D ** -0.5, 0.125, ((0, 8), (1, 4)))
    value_weight = bell_draw(key_list[4], (D, D), D ** -0.5, 0.125, ((0, 8), (1, 4)))
    value_bias = bell_draw(key_list[5], (D,), 0.5, 3.0, ((0, 4),), jnp.float32)
    output_weight = bell_draw(key_list[6], (D, D), (D // 32) ** -0.5, 0.75, ((0, 4), (1, 8)))
    output_bias = bell_draw(key_list[7], (D,), 0.5, 3.0, (), jnp.float32)
    first_gain = jnp.clip(1.0 + 0.1 * jax.random.normal(key_list[8], (D,), jnp.float32), 0.5, 1.5)
    first_shift = bell_draw(key_list[9], (D,), 0.5, 3.0, (), jnp.float32)
    up_weight = bell_draw(key_list[10], (D, FF), D ** -0.5, 0.125, ((0, 8), (1, 4)))
    up_bias = bell_draw(key_list[11], (FF,), 0.5, 3.0, ((0, 4),), jnp.float32)
    down_weight = bell_draw(key_list[12], (FF, D), (FF // 4) ** -0.5, 0.125, ((0, 4), (1, 8)))
    down_bias = bell_draw(key_list[13], (D,), 0.5, 3.0, (), jnp.float32)
    second_gain = jnp.clip(1.0 + 0.1 * jax.random.normal(key_list[14], (D,), jnp.float32), 0.5, 1.5)
    second_shift = bell_draw(key_list[15], (D,), 0.5, 3.0, (), jnp.float32)
    segments = jax.vmap(lambda own: jnp.searchsorted(jnp.cumsum(uneven(own, DOCS, LEN, DOC_MOST, 2)), jnp.arange(LEN), side="right"))(jax.random.split(key_list[16], SEQS)).reshape((SEQS, LEN)).astype(jnp.int32)
    cotangent = heavy_noise(key_list[17], (TOKENS, D), 1.0, 6.0, ((0, 32),), (0, 1, 32, 2.75))
    return dict(inputs=inputs, query_weight=query_weight, query_bias=query_bias, key_weight=key_weight, value_weight=value_weight, value_bias=value_bias, output_weight=output_weight, output_bias=output_bias, first_gain=first_gain, first_shift=first_shift, up_weight=up_weight, up_bias=up_bias, down_weight=down_weight, down_bias=down_bias, second_gain=second_gain, second_shift=second_shift, segments=segments, cotangent=cotangent)


EPS = 1e-06
NEG = -1000000000.0
HIGH = lax.Precision.HIGHEST

@jax.custom_vjp
def low(v):
    return lax.optimization_barrier(v.astype(jnp.bfloat16)).astype(jnp.float32)

@jax.custom_vjp
def low_back(v):
    return v

def low_keep(v):
    return (low(v), None)

def low_pass(kept, grad):
    return (grad,)

def back_keep(v):
    return (v, None)

def back_low(kept, grad):
    return (low(grad),)
low.defvjp(low_keep, low_pass)
low_back.defvjp(back_keep, back_low)

def matmul(left, right):
    return jnp.dot(left, right, precision=HIGH)

def layer_norm(total, gain, shift):
    center = total - lax.optimization_barrier(jnp.mean(total, axis=-1, keepdims=True))
    spread = lax.optimization_barrier(jnp.mean(center * center, axis=-1, keepdims=True))
    return center * lax.rsqrt(spread + EPS) * gain + shift

def attend(pieces):
    queries, keys, values, labels = pieces
    scores = low_back(jnp.einsum('qhd,khd->hqk', queries, keys, precision=HIGH) * HD ** (-0.5))
    same = labels[:, None] == labels[None, :]
    scores = jnp.where(same[None], scores, NEG)
    top = lax.optimization_barrier(jnp.max(scores, axis=-1, keepdims=True))
    weights = jnp.exp(scores - top)
    probs = low(weights / lax.optimization_barrier(jnp.sum(weights, axis=-1, keepdims=True)))
    return low(low_back(jnp.einsum('hqk,khd->qhd', probs, values, precision=HIGH)))

def layer(params, rows, labels):
    query_weight, query_bias, key_weight, value_weight, value_bias, output_weight, output_bias, first_gain, first_shift, up_weight, up_bias, down_weight, down_bias, second_gain, second_shift = params
    number = labels.shape[0]
    query = low(low_back(matmul(rows, query_weight) + query_bias))
    keys = low(low_back(matmul(rows, key_weight)))
    value = low(low_back(matmul(rows, value_weight) + value_bias))

    def heads(table):
        return table.reshape(number, LEN, HEADS, HD)
    context = lax.map(attend, (heads(query), heads(keys), heads(value), labels)).reshape(rows.shape[0], D)
    first_sum = rows + low_back(matmul(context, output_weight)) + output_bias
    first_out = layer_norm(first_sum, first_gain, first_shift)
    pre = low_back(matmul(low(first_out), up_weight) + up_bias)
    hidden = low(jax.nn.gelu(pre, approximate=True))
    second_sum = first_out + low_back(matmul(hidden, down_weight)) + down_bias
    return layer_norm(second_sum, second_gain, second_shift)

def reference(inputs, query_weight, query_bias, key_weight, value_weight, value_bias, output_weight, output_bias, first_gain, first_shift, up_weight, up_bias, down_weight, down_bias, second_gain, second_shift, segments, cotangent):
    per = math.gcd(SEQS, 4)
    params = tuple((item.astype(jnp.float32) for item in (query_weight, query_bias, key_weight, value_weight, value_bias, output_weight, output_bias, first_gain, first_shift, up_weight, up_bias, down_weight, down_bias, second_gain, second_shift)))

    def whole(weights, rows):

        def block(pieces):
            return layer(weights, pieces[0], pieces[1])
        result = lax.map(jax.checkpoint(block), (rows.reshape(SEQS // per, per * LEN, D), segments.reshape(SEQS // per, per, LEN)))
        return result.reshape(TOKENS, D)
    layer_out, pull = jax.vjp(whole, params, inputs.astype(jnp.float32))
    weight_grads, input_grad = pull(cotangent.astype(jnp.float32))
    query_weight_grad, query_bias_grad, key_weight_grad, value_weight_grad, value_bias_grad, output_weight_grad, output_bias_grad, first_gain_grad, first_shift_grad, up_weight_grad, up_bias_grad, down_weight_grad, down_bias_grad, second_gain_grad, second_shift_grad = weight_grads
    return (layer_out.astype(jnp.bfloat16), input_grad.astype(jnp.bfloat16), query_weight_grad, query_bias_grad.reshape(N_TP, D // N_TP), key_weight_grad, value_weight_grad, value_bias_grad.reshape(N_TP, D // N_TP), output_weight_grad, output_bias_grad, first_gain_grad, first_shift_grad, up_weight_grad, up_bias_grad.reshape(N_TP, FF // N_TP), down_weight_grad, down_bias_grad, second_gain_grad, second_shift_grad)
```

```python
import jax
import jax.numpy as jnp
from jax import lax
from jax.sharding import PartitionSpec as P

HD = 128
EPS = 1e-06
NEG = -1000000000.0
AXES = ("fsdp", "tp")
F32 = jnp.float32
BF16 = jnp.bfloat16


def project(left, right):
    return jnp.dot(left, right, preferred_element_type=F32)


def against(left, right):
    return lax.dot_general(left, right, (((1,), (1,)), ((), ())), preferred_element_type=F32)


def across(left, right):
    return lax.dot_general(left, right, (((0,), (0,)), ((), ())), preferred_element_type=F32)


def normalize(total):
    center = total - jnp.mean(total, axis=-1, keepdims=True)
    spread = jnp.mean(center * center, axis=-1, keepdims=True)
    scale_inv = lax.rsqrt(spread + EPS)
    return center * scale_inv, scale_inv


def norm_back(grad, normed, scale_inv, gain):
    scaled = grad * gain
    inner = (
        scaled
        - jnp.mean(scaled, axis=-1, keepdims=True)
        - normed * jnp.mean(scaled * normed, axis=-1, keepdims=True)
    )
    return (scale_inv * inner, jnp.sum(grad * normed, axis=0), jnp.sum(grad, axis=0))


def gelu_tanh(values):
    return jax.nn.gelu(values, approximate=True)


def scores_of(queries, keys, labels):
    scores = jnp.einsum("qhd,khd->hqk", queries, keys, preferred_element_type=F32) * HD ** (-0.5)
    same = labels[:, None] == labels[None, :]
    return jnp.where(same[None], scores, NEG)


def attend(queries, keys, values, labels):
    scores = scores_of(queries, keys, labels)
    top = jnp.max(scores, axis=-1, keepdims=True)
    weights = jnp.exp(scores - top)
    total = jnp.sum(weights, axis=-1, keepdims=True)
    probs = (weights / total).astype(BF16)
    context = jnp.einsum("hqk,khd->qhd", probs, values, preferred_element_type=F32).astype(BF16)
    return context, top[..., 0] + jnp.log(total[..., 0])


def attend_back(queries, keys, values, d_context, log_total, labels):
    probs = jnp.exp(scores_of(queries, keys, labels) - log_total[..., None])
    probs_low = probs.astype(BF16)
    d_value = jnp.einsum("hqk,qhd->khd", probs_low, d_context, preferred_element_type=F32).astype(
        BF16
    )
    d_probs = jnp.einsum("qhd,khd->hqk", d_context, values, preferred_element_type=F32)
    d_scores = (probs * (d_probs - jnp.sum(probs * d_probs, axis=-1, keepdims=True))).astype(BF16)
    d_query = (
        jnp.einsum("hqk,khd->qhd", d_scores, keys, preferred_element_type=F32) * HD ** (-0.5)
    ).astype(BF16)
    d_key = (
        jnp.einsum("hqk,qhd->khd", d_scores, queries, preferred_element_type=F32) * HD ** (-0.5)
    ).astype(BF16)
    return (d_query, d_key, d_value)


class Layout:
    def __init__(self, fsdp, tp):
        self.fsdp, self.tp = fsdp, tp
        self.planes, self.n = fsdp // 2, tp // 2
        f, t = lax.axis_index("fsdp"), lax.axis_index("tp")
        self.g, self.c = f // 2, f % 2
        self.h, self.l = t // self.n, t % self.n

    def move(self, value, rule):
        pairs = []
        for g in range(self.planes):
            for c in range(2):
                for h in range(2):
                    for l in range(self.n):
                        a, b, d, e = rule(g, c, h, l)
                        here = (g * 2 + c) * self.tp + h * self.n + l
                        there = (a * 2 + b) * self.tp + d * self.n + e
                        pairs.append((here, there))
        return lax.ppermute(value, AXES, pairs)

    def core(self, value):
        return self.move(value, lambda g, c, h, l: (g, 1 - c, h, l))

    def half(self, value):
        return self.move(value, lambda g, c, h, l: (g, c, 1 - h, l))

    def trade(self, value):
        return self.move(value, lambda g, c, h, l: (g, h, c, l))

    def plane(self, value, mask):
        return self.move(value, lambda g, c, h, l: (g ^ mask, c, h, l))

    def along(self, value, step):
        return self.move(value, lambda g, c, h, l: (g, c, h, (l + step) % self.n))

    def relative(self, value):
        size = value.shape[-1] // self.planes
        parts = [
            lax.dynamic_slice_in_dim(value, (self.g ^ m) * size, size, axis=value.ndim - 1)
            for m in range(self.planes)
        ]
        return jnp.concatenate(parts, axis=-1)

    def gather(self, own):
        pieces = []
        for step in range(self.n):
            piece = own if step == 0 else self.along(own, step)
            pieces += [piece, self.core(piece)]
        return jnp.concatenate(pieces, axis=0)

    def reduce(self, block):
        total, arrived = None, []
        for step in list(range(1, self.n)) + [0]:
            both = block((self.n - step) % self.n)
            size = both.shape[0] // 2
            mate = self.core(both[size:].astype(BF16))
            summed = both[:size] + mate.astype(F32)
            if step == 0:
                total = summed
            else:
                arrived.append(self.along(summed.astype(BF16), step))
        for piece in arrived:
            total = total + piece.astype(F32)
        return total

    def spread(self, shard, axis):
        other = 1 - axis
        width = shard.shape[other] // 2
        mine = lax.dynamic_slice_in_dim(shard, self.c * width, width, axis=other)
        give = lax.dynamic_slice_in_dim(shard, (1 - self.c) * width, width, axis=other)
        got = self.core(give)
        first = self.c == 0
        near = jnp.concatenate(
            [jnp.where(first, mine, got), jnp.where(first, got, mine)], axis=axis
        )
        near = jnp.concatenate([near, self.half(near)], axis=other)
        size = near.shape[axis] // 2

        def part(value, index):
            return lax.slice_in_dim(value, index * size, (index + 1) * size, axis=axis)

        pieces = {0: (part(near, 0), part(near, 1))}
        for m in sorted(range(1, self.planes), key=lambda v: bin(v).count("1")):
            if bin(m).count("1") == 1:
                whole = self.plane(near, m)
                pieces[m] = (part(whole, 0), part(whole, 1))
            else:
                top, low = 1 << (m.bit_length() - 1), m & -m
                pieces[m] = (
                    self.plane(pieces[m ^ top][0], top),
                    self.plane(pieces[m ^ low][1], low),
                )
        return jnp.concatenate([p for m in range(self.planes) for p in pieces[m]], axis=axis)

    def collect(self, grad, axis):
        other = 1 - axis
        size = grad.shape[axis] // (2 * self.planes)
        width = grad.shape[other] // 2
        total = {
            m: [
                lax.slice_in_dim(grad, (2 * m + k) * size, (2 * m + k + 1) * size, axis=axis)
                for k in range(2)
            ]
            for m in range(self.planes)
        }
        for m in sorted(range(1, self.planes), key=lambda v: -bin(v).count("1")):
            if bin(m).count("1") == 1:
                both = jnp.concatenate([v.astype(BF16) for v in total[m]], axis=axis)
                both = self.plane(both, m).astype(F32)
                for k in range(2):
                    piece = lax.slice_in_dim(both, k * size, (k + 1) * size, axis=axis)
                    total[0][k] = total[0][k] + piece
            else:
                top, low = 1 << (m.bit_length() - 1), m & -m
                first = self.plane(total[m][0].astype(BF16), top).astype(F32)
                total[m ^ top][0] = total[m ^ top][0] + first
                second = self.plane(total[m][1].astype(BF16), low).astype(F32)
                total[m ^ low][1] = total[m ^ low][1] + second
        near = jnp.concatenate(total[0], axis=axis)
        mine = lax.slice_in_dim(near, 0, width, axis=other)
        give = lax.slice_in_dim(near, width, 2 * width, axis=other)
        mine = mine + self.half(give.astype(BF16)).astype(F32)
        keep = lax.dynamic_slice_in_dim(mine, self.c * size, size, axis=axis)
        give = lax.dynamic_slice_in_dim(mine, (1 - self.c) * size, size, axis=axis)
        got = self.core(give.astype(BF16)).astype(F32)
        first = self.c == 0
        return jnp.concatenate(
            [jnp.where(first, keep, got), jnp.where(first, got, keep)], axis=other
        )

    def role(self, vector):
        width = vector.shape[0] // 2
        mine = lax.dynamic_slice_in_dim(vector, self.c * width, width)
        return jnp.concatenate([mine, self.half(mine)])

    def unrole(self, vector):
        width = vector.shape[0] // 2
        table = jnp.zeros((self.tp, 2, width), vector.dtype)
        for k, h in enumerate((self.h, 1 - self.h)):
            piece = vector[k * width : (k + 1) * width].reshape(1, 1, width)
            table = lax.dynamic_update_slice(table, piece, (h * self.n + self.l, self.c, 0))
        return table.reshape(self.tp * 2 * width)


def shards(
    fsdp,
    tp,
    inputs,
    query_weight,
    query_bias,
    key_weight,
    value_weight,
    value_bias,
    output_weight,
    output_bias,
    first_gain,
    first_shift,
    up_weight,
    up_bias,
    down_weight,
    down_bias,
    second_gain,
    second_shift,
    segments,
    cotangent,
):
    lay = Layout(fsdp, tp)
    length = segments.shape[1]
    local = query_weight.shape[1] // HD
    rows_own = inputs.shape[0]

    def heads(table):
        return table.reshape(length, local, HD)

    query_full = lay.spread(query_weight, 0)
    key_full = lay.spread(key_weight, 0)
    value_full = lay.spread(value_weight, 0)
    output_full = lay.spread(output_weight, 1)
    up_full = lay.spread(up_weight, 0)
    down_full = lay.spread(down_weight, 1)

    own = lay.trade(lay.relative(inputs))
    own_cot = lay.trade(lay.relative(cotangent)).astype(F32)
    labels = jnp.where(lay.c == lay.h, segments[0], lay.core(segments[0]))
    label_parts = []
    for step in range(lay.n):
        for core in (lay.c, 1 - lay.c):
            at = (core * lay.n + (lay.l + lay.n - step) % lay.n) * rows_own
            label_parts.append(lax.dynamic_slice_in_dim(labels, at, rows_own))
    labels = jnp.concatenate(label_parts)
    output_bias, first_gain, first_shift, down_bias, second_gain, second_shift = (
        lay.relative(v)
        for v in (output_bias, first_gain, first_shift, down_bias, second_gain, second_shift)
    )
    query_bias, value_bias, up_bias = (lay.role(v) for v in (query_bias, value_bias, up_bias))

    rows_all = lay.gather(own)
    query = (project(rows_all, query_full) + query_bias).astype(BF16)
    keys = project(rows_all, key_full).astype(BF16)
    value = (project(rows_all, value_full) + value_bias).astype(BF16)
    context, log_total = attend(heads(query), heads(keys), heads(value), labels)
    context = context.reshape(length, local * HD)

    def rows_at(table, step):
        return table[2 * rows_own * step : 2 * rows_own * (step + 1)]

    attn = lay.reduce(lambda step: project(rows_at(context, step), output_full))
    first_sum = own.astype(F32) + attn + output_bias
    first_normed, first_inv = normalize(first_sum)
    first_out = first_normed * first_gain + first_shift
    mid_all = lay.gather(first_out.astype(BF16))
    pre = project(mid_all, up_full) + up_bias
    active, gelu_back = jax.vjp(gelu_tanh, pre)
    hidden = active.astype(BF16)
    ffn = lay.reduce(lambda step: project(rows_at(hidden, step), down_full))
    second_sum = first_out + ffn + down_bias
    second_normed, second_inv = normalize(second_sum)
    final = second_normed * second_gain + second_shift
    layer_out = lay.relative(lay.trade(final.astype(BF16)))

    d_second, second_gain_term, second_shift_term = norm_back(
        own_cot, second_normed, second_inv, second_gain
    )
    down_bias_term = jnp.sum(d_second, axis=0)
    d_branch_all = lay.gather(d_second.astype(BF16))
    d_hidden = against(d_branch_all, down_full)
    d_pre = gelu_back(d_hidden)[0].astype(BF16)
    up_bias_term = jnp.sum(d_pre.astype(F32), axis=0)
    d_mid = lay.reduce(lambda step: against(rows_at(d_pre, step), up_full))
    down_term = across(hidden, d_branch_all)
    up_term = across(mid_all, d_pre)
    down_grad = lay.collect(down_term, 1)
    up_grad = lay.collect(up_term, 0)
    d_first = d_mid + d_second
    d_first_sum, first_gain_term, first_shift_term = norm_back(
        d_first, first_normed, first_inv, first_gain
    )
    output_bias_term = jnp.sum(d_first_sum, axis=0)
    d_attn_all = lay.gather(d_first_sum.astype(BF16))
    d_context = against(d_attn_all, output_full).astype(BF16)
    output_term = across(context, d_attn_all)
    output_grad = lay.collect(output_term, 1)
    d_query, d_key, d_value = (
        v.reshape(length, local * HD)
        for v in attend_back(
            heads(query), heads(keys), heads(value), heads(d_context), log_total, labels
        )
    )
    query_bias_term = jnp.sum(d_query.astype(F32), axis=0)
    value_bias_term = jnp.sum(d_value.astype(F32), axis=0)
    d_rows = lay.reduce(
        lambda step: against(rows_at(d_query, step), query_full)
        + against(rows_at(d_key, step), key_full)
        + against(rows_at(d_value, step), value_full)
    )
    input_grad = lay.relative(lay.trade((d_rows + d_first_sum).astype(BF16)))
    query_grad = lay.collect(across(rows_all, d_query), 0)
    key_grad = lay.collect(across(rows_all, d_key), 0)
    value_grad = lay.collect(across(rows_all, d_value), 0)

    def small(terms):
        total = lax.psum(jnp.concatenate(terms), AXES)
        result, at = [], 0
        for term in terms:
            result.append(total[at : at + term.shape[0]])
            at += term.shape[0]
        return result

    f, t = lax.axis_index("fsdp"), lax.axis_index("tp")

    def residual(vector):
        size = vector.shape[0] // (fsdp * tp)
        return lax.dynamic_slice_in_dim(vector, (f * tp + t) * size, size)

    def split(vector):
        size = vector.shape[0] // (fsdp * tp)
        return lax.dynamic_slice_in_dim(vector, (t * fsdp + f) * size, size)[None]

    early = small(
        [
            lay.relative(v)
            for v in (
                down_bias_term,
                second_gain_term,
                second_shift_term,
                output_bias_term,
                first_gain_term,
                first_shift_term,
            )
        ]
        + [lay.unrole(up_bias_term)]
    )
    late = small([lay.unrole(query_bias_term), lay.unrole(value_bias_term)])
    return (
        layer_out,
        input_grad,
        query_grad,
        split(late[0]),
        key_grad,
        value_grad,
        split(late[1]),
        output_grad,
        residual(early[3]),
        residual(early[4]),
        residual(early[5]),
        up_grad,
        split(early[6]),
        down_grad,
        residual(early[0]),
        residual(early[1]),
        residual(early[2]),
    )


def solution(mesh):
    fsdp, tp = mesh.shape["fsdp"], mesh.shape["tp"]

    def body(*arrays):
        return shards(fsdp, tp, *arrays)

    tokens, inner, outer = P(AXES, None), P("fsdp", "tp"), P("tp", "fsdp")
    placed = (
        tokens,
        inner,
        P("tp"),
        inner,
        inner,
        P("tp"),
        outer,
        P(),
        P(),
        P(),
        inner,
        P("tp"),
        outer,
        P(),
        P(),
        P(),
        P("fsdp", None),
        tokens,
    )
    return jax.shard_map(
        body,
        mesh=mesh,
        in_specs=placed,
        out_specs=(
            tokens,
            tokens,
            inner,
            outer,
            inner,
            inner,
            outer,
            outer,
            P(AXES),
            P(AXES),
            P(AXES),
            inner,
            outer,
            outer,
            P(AXES),
            P(AXES),
            P(AXES),
        ),
        check_vma=False,
    )
```

```python
import functools

import jax
import jax.numpy as jnp
from jax import lax
from jax.experimental import pallas as pl
from jax.experimental.pallas import tpu as pltpu
from jax.sharding import PartitionSpec as P

HD = 128
EPS = 1e-06
NEG = -1000000000.0
AXES = ("fsdp", "tp")
F32 = jnp.float32
BF16 = jnp.bfloat16
MESH = pl.DeviceIdType.MESH
VMEM = 60 * 2**20


def project(left, right):
    return jnp.dot(left, right, preferred_element_type=F32)


def against(left, right):
    return lax.dot_general(left, right, (((1,), (1,)), ((), ())), preferred_element_type=F32)


def across(left, right):
    return lax.dot_general(left, right, (((0,), (0,)), ((), ())), preferred_element_type=F32)


def normalize(total):
    center = total - jnp.mean(total, axis=-1, keepdims=True)
    spread = jnp.mean(center * center, axis=-1, keepdims=True)
    scale_inv = lax.rsqrt(spread + EPS)
    return center * scale_inv, scale_inv


def norm_back(grad, normed, scale_inv, gain):
    scaled = grad * gain
    inner = (
        scaled
        - jnp.mean(scaled, axis=-1, keepdims=True)
        - normed * jnp.mean(scaled * normed, axis=-1, keepdims=True)
    )
    return (scale_inv * inner, jnp.sum(grad * normed, axis=0), jnp.sum(grad, axis=0))


def gelu_tanh(values):
    return jax.nn.gelu(values, approximate=True)


def scores_of(queries, keys, labels):
    scores = jnp.einsum("qhd,khd->hqk", queries, keys, preferred_element_type=F32) * HD ** (-0.5)
    same = labels[:, None] == labels[None, :]
    return jnp.where(same[None], scores, NEG)


def attend(queries, keys, values, labels):
    scores = scores_of(queries, keys, labels)
    top = jnp.max(scores, axis=-1, keepdims=True)
    weights = jnp.exp(scores - top)
    total = jnp.sum(weights, axis=-1, keepdims=True)
    probs = (weights / total).astype(BF16)
    context = jnp.einsum("hqk,khd->qhd", probs, values, preferred_element_type=F32).astype(BF16)
    return context, top[..., 0] + jnp.log(total[..., 0])


def attend_back(queries, keys, values, d_context, log_total, labels):
    probs = jnp.exp(scores_of(queries, keys, labels) - log_total[..., None])
    probs_low = probs.astype(BF16)
    d_value = jnp.einsum("hqk,qhd->khd", probs_low, d_context, preferred_element_type=F32).astype(
        BF16
    )
    d_probs = jnp.einsum("qhd,khd->hqk", d_context, values, preferred_element_type=F32)
    d_scores = (probs * (d_probs - jnp.sum(probs * d_probs, axis=-1, keepdims=True))).astype(BF16)
    d_query = (
        jnp.einsum("hqk,khd->qhd", d_scores, keys, preferred_element_type=F32) * HD ** (-0.5)
    ).astype(BF16)
    d_key = (
        jnp.einsum("hqk,qhd->khd", d_scores, queries, preferred_element_type=F32) * HD ** (-0.5)
    ).astype(BF16)
    return (d_query, d_key, d_value)


class Layout:
    def __init__(self, fsdp, tp):
        self.fsdp, self.tp = fsdp, tp
        self.planes, self.n = fsdp // 2, tp // 2
        f, t = lax.axis_index("fsdp"), lax.axis_index("tp")
        self.g, self.c = f // 2, f % 2
        self.h, self.l = t // self.n, t % self.n

    def move(self, value, rule):
        pairs = []
        for g in range(self.planes):
            for c in range(2):
                for h in range(2):
                    for l in range(self.n):
                        a, b, d, e = rule(g, c, h, l)
                        here = (g * 2 + c) * self.tp + h * self.n + l
                        there = (a * 2 + b) * self.tp + d * self.n + e
                        pairs.append((here, there))
        return lax.ppermute(value, AXES, pairs)

    def core(self, value):
        return self.move(value, lambda g, c, h, l: (g, 1 - c, h, l))

    def half(self, value):
        return self.move(value, lambda g, c, h, l: (g, c, 1 - h, l))

    def trade(self, value):
        return self.move(value, lambda g, c, h, l: (g, h, c, l))

    def plane(self, value, mask):
        return self.move(value, lambda g, c, h, l: (g ^ mask, c, h, l))

    def along(self, value, step):
        return self.move(value, lambda g, c, h, l: (g, c, h, (l + step) % self.n))

    def relative(self, value):
        size = value.shape[-1] // self.planes
        parts = [
            lax.dynamic_slice_in_dim(value, (self.g ^ m) * size, size, axis=value.ndim - 1)
            for m in range(self.planes)
        ]
        return jnp.concatenate(parts, axis=-1)

    def gather(self, own):
        pieces = []
        for step in range(self.n):
            piece = own if step == 0 else self.along(own, step)
            pieces += [piece, self.core(piece)]
        return jnp.concatenate(pieces, axis=0)

    def reduce(self, block):
        total, arrived = None, []
        for step in list(range(1, self.n)) + [0]:
            both = block((self.n - step) % self.n)
            size = both.shape[0] // 2
            mate = self.core(both[size:].astype(BF16))
            summed = both[:size] + mate.astype(F32)
            if step == 0:
                total = summed
            else:
                arrived.append(self.along(summed.astype(BF16), step))
        for piece in arrived:
            total = total + piece.astype(F32)
        return total

    def spread(self, shard, axis):
        other = 1 - axis
        width = shard.shape[other] // 2
        mine = lax.dynamic_slice_in_dim(shard, self.c * width, width, axis=other)
        give = lax.dynamic_slice_in_dim(shard, (1 - self.c) * width, width, axis=other)
        got = self.core(give)
        first = self.c == 0
        near = jnp.concatenate(
            [jnp.where(first, mine, got), jnp.where(first, got, mine)], axis=axis
        )
        near = jnp.concatenate([near, self.half(near)], axis=other)
        size = near.shape[axis] // 2

        def part(value, index):
            return lax.slice_in_dim(value, index * size, (index + 1) * size, axis=axis)

        pieces = {0: (part(near, 0), part(near, 1))}
        for m in sorted(range(1, self.planes), key=lambda v: bin(v).count("1")):
            if bin(m).count("1") == 1:
                whole = self.plane(near, m)
                pieces[m] = (part(whole, 0), part(whole, 1))
            else:
                top, low = 1 << (m.bit_length() - 1), m & -m
                pieces[m] = (
                    self.plane(pieces[m ^ top][0], top),
                    self.plane(pieces[m ^ low][1], low),
                )
        return jnp.concatenate([p for m in range(self.planes) for p in pieces[m]], axis=axis)

    def collect(self, grad, axis):
        other = 1 - axis
        size = grad.shape[axis] // (2 * self.planes)
        width = grad.shape[other] // 2
        total = {
            m: [
                lax.slice_in_dim(grad, (2 * m + k) * size, (2 * m + k + 1) * size, axis=axis)
                for k in range(2)
            ]
            for m in range(self.planes)
        }
        for m in sorted(range(1, self.planes), key=lambda v: -bin(v).count("1")):
            if bin(m).count("1") == 1:
                both = jnp.concatenate([v.astype(BF16) for v in total[m]], axis=axis)
                both = self.plane(both, m).astype(F32)
                for k in range(2):
                    piece = lax.slice_in_dim(both, k * size, (k + 1) * size, axis=axis)
                    total[0][k] = total[0][k] + piece
            else:
                top, low = 1 << (m.bit_length() - 1), m & -m
                first = self.plane(total[m][0].astype(BF16), top).astype(F32)
                total[m ^ top][0] = total[m ^ top][0] + first
                second = self.plane(total[m][1].astype(BF16), low).astype(F32)
                total[m ^ low][1] = total[m ^ low][1] + second
        near = jnp.concatenate(total[0], axis=axis)
        mine = lax.slice_in_dim(near, 0, width, axis=other)
        give = lax.slice_in_dim(near, width, 2 * width, axis=other)
        mine = mine + self.half(give.astype(BF16)).astype(F32)
        keep = lax.dynamic_slice_in_dim(mine, self.c * size, size, axis=axis)
        give = lax.dynamic_slice_in_dim(mine, (1 - self.c) * size, size, axis=axis)
        got = self.core(give.astype(BF16)).astype(F32)
        first = self.c == 0
        return jnp.concatenate(
            [jnp.where(first, keep, got), jnp.where(first, got, keep)], axis=other
        )

    def role(self, vector):
        width = vector.shape[0] // 2
        mine = lax.dynamic_slice_in_dim(vector, self.c * width, width)
        return jnp.concatenate([mine, self.half(mine)])

    def unrole(self, vector):
        width = vector.shape[0] // 2
        table = jnp.zeros((self.tp, 2, width), vector.dtype)
        for k, h in enumerate((self.h, 1 - self.h)):
            piece = vector[k * width : (k + 1) * width].reshape(1, 1, width)
            table = lax.dynamic_update_slice(table, piece, (h * self.n + self.l, self.c, 0))
        return table.reshape(self.tp * 2 * width)


def dot(left, right, dims=((1,), (0,))):
    return lax.dot_general(left, right, (dims, ((), ())), preferred_element_type=F32)


NN, NT, TN = ((1,), (0,)), ((1,), (1,)), ((0,), (0,))


class Sizes:
    def __init__(self, fsdp, tp, inputs, query_weight, up_weight, segments):
        self.fsdp, self.tp = fsdp, tp
        self.planes, self.n = fsdp // 2, tp // 2
        self.rows, self.dim = inputs.shape
        self.length = segments.shape[1]
        self.fine = query_weight.shape[0]
        self.wide = 2 * self.fine
        self.heads = query_weight.shape[1]
        self.half = self.heads // 2
        self.units = up_weight.shape[1]
        self.uhalf = self.units // 2


INNER = (True, True, True, False, True, False)


class Links:
    def __init__(self, size, send, recv):
        self.size, self.send, self.recv = size, send, recv
        f, t = lax.axis_index("fsdp"), lax.axis_index("tp")
        self.g, self.c = f // 2, f % 2
        self.h, self.l = t // size.n, t % size.n
        self.done = set()
        self.sent = []
        self.next = 0

    def device(self, g, c, h, l):
        return (g * 2 + c, h * self.size.n + l)

    def mate(self):
        return self.device(self.g, 1 - self.c, self.h, self.l)

    def across(self):
        return self.device(self.g, self.c, 1 - self.h, self.l)

    def corner(self):
        return self.device(self.g, 1 - self.c, 1 - self.h, self.l)

    def plane(self, mask):
        return self.device(self.g ^ mask, self.c, self.h, self.l)

    def along(self, step):
        return self.device(self.g, self.c, self.h, (self.l + step) % self.size.n)

    def barrier(self):
        size = self.size
        peers = [self.mate(), self.across(), self.corner()]
        mask = 1
        while mask < size.planes:
            peers.append(self.plane(mask))
            mask *= 2
        peers += [self.along(step) for step in range(1, size.n)]
        semaphore = pltpu.get_barrier_semaphore()
        for peer in peers:
            pl.semaphore_signal(semaphore, inc=1, device_id=peer, device_id_type=MESH)
        pl.semaphore_wait(semaphore, len(peers))

    def slots(self, count=1):
        first = self.next
        self.next += count
        return first

    def copy(self, slot, source, target, device):
        return pltpu.make_async_remote_copy(
            src_ref=source,
            dst_ref=target,
            send_sem=self.send.at[slot],
            recv_sem=self.recv.at[slot],
            device_id=device,
            device_id_type=MESH,
        )

    def go(self, slot, source, target, device):
        copy = self.copy(slot, source, target, device)
        copy.start()
        self.sent.append(copy)
        return copy


class Local:
    def __init__(self, semaphores):
        self.semaphores, self.next = semaphores, 0

    def start(self, source, target):
        copy = pltpu.make_async_copy(source, target, self.semaphores.at[self.next])
        self.next += 1
        copy.start()
        return copy


class Spread:
    def __init__(self, links, local, shard, full, inner):
        self.links, self.local = links, local
        self.shard, self.full, self.inner = shard, full, inner
        self.base = links.slots(3 + 2 * (links.size.planes - 1))
        self.waited = set()

    def part(self, index):
        axis = 1 if self.inner else 0
        width = self.shard.shape[axis] // 2
        at = pl.multiple_of(index * width, width)
        return self.shard.at[:, pl.ds(at, width)] if self.inner else self.shard.at[pl.ds(at, width)]

    def home(self, e, c):
        fine = self.links.size.fine
        at = pl.ds(pl.multiple_of(c * fine, fine), fine)
        if self.inner:
            return self.full.at[e, at, :]
        width = self.full.shape[1] // 2
        return self.full.at[0, pl.ds(e * width, width), at]

    def block(self, m, e=None):
        wide = self.links.size.wide
        if self.inner:
            at = pl.ds(m * wide, wide)
            return self.full.at[:, at, :] if e is None else self.full.at[e, at, :]
        width = self.full.shape[1] // 2
        return self.full.at[m] if e is None else self.full.at[m, pl.ds(e * width, width)]

    def first(self):
        k = self.links
        mine, other = self.part(k.c), self.part(1 - k.c)
        self.own = self.local.start(mine, self.home(0, k.c))
        self.steps = [
            k.go(self.base, other, self.home(0, k.c), k.mate()),
            k.go(self.base + 1, mine, self.home(1, k.c), k.across()),
            k.go(self.base + 2, other, self.home(1, k.c), k.corner()),
        ]

    def second(self):
        k = self.links
        for step in self.steps:
            step.wait_recv()
        self.own.wait()
        self.pieces = {}
        mask = 1
        while mask < k.size.planes:
            copy = k.go(self.base + 1 + 2 * mask, self.block(0), self.block(mask), k.plane(mask))
            self.pieces[mask, 0] = self.pieces[mask, 1] = copy
            mask *= 2

    def arrive(self, m, e):
        copy = self.pieces[m, e]
        if id(copy) not in self.waited:
            self.waited.add(id(copy))
            copy.wait_recv()

    def third(self):
        k = self.links
        for m in sorted(range(1, k.size.planes), key=lambda v: bin(v).count("1")):
            if bin(m).count("1") > 1:
                top, low = 1 << (m.bit_length() - 1), m & -m
                for e, bit in ((0, top), (1, low)):
                    self.arrive(m ^ bit, e)
                    self.pieces[m, e] = k.go(
                        self.base + 1 + 2 * m + e,
                        self.block(m ^ bit, e),
                        self.block(m, e),
                        k.plane(bit),
                    )

    def finish(self):
        for m in range(1, self.links.size.planes):
            for e in range(2):
                self.arrive(m, e)


class Activations:
    def __init__(self, links, rows, give, take, out, came):
        self.links, self.rows = links, rows
        self.give, self.take, self.out, self.came = give, take, out, came
        size = links.size
        self.gather_slots = links.slots(2 * size.n)
        self.mate_slots = links.slots(size.n * size.planes)
        self.along_slots = links.slots(size.n * size.planes)

    def piece(self, index):
        size = self.links.size
        return self.rows.at[pl.ds(index * size.rows, size.rows)]

    def gather_start(self):
        k, base = self.links, self.gather_slots
        self.far = [
            k.go(base + step, self.piece(0), self.piece(2 * step), k.along(step))
            for step in range(1, k.size.n)
        ]
        self.near = [k.go(base + k.size.n, self.piece(0), self.piece(1), k.mate())]

    def gather_relay(self):
        k, base = self.links, self.gather_slots
        for step in range(1, k.size.n):
            self.far[step - 1].wait_recv()
            self.near.append(
                k.go(
                    base + k.size.n + step,
                    self.piece(2 * step),
                    self.piece(2 * step + 1),
                    k.mate(),
                )
            )

    def gather_wait(self, step):
        self.near[step].wait_recv()

    def gather_end(self):
        over = self.far + self.near
        for copy in over:
            copy.wait_send()
        self.links.sent = [c for c in self.links.sent if all(c is not o for o in over)]

    def reduce(self, tile, put):
        k = self.links
        size = k.size
        planes, n = size.planes, size.n

        def near(step, m):
            at = step * planes + m
            return k.copy(self.mate_slots + at, self.give.at[at], self.take.at[at], k.mate())

        def far(step, m):
            at = (step - 1) * planes + m
            return k.copy(self.along_slots + at, self.out.at[at], self.came.at[at], k.along(step))

        for step in list(range(1, n)) + [0]:
            index = 2 * ((n - step) % n)

            @pl.loop(0, planes)
            def _(m, step=step, index=index):
                self.give[step * planes + m] = tile(m, index + 1).astype(BF16)
                near(step, m).start()

            @pl.loop(0, planes)
            def _(m, step=step, index=index):
                total = tile(m, index)
                near(step, m).wait_recv()
                total = total + self.take[step * planes + m].astype(F32)
                if step:
                    self.out[(step - 1) * planes + m] = total.astype(BF16)
                    far(step, m).start()
                else:
                    for other in range(1, n):
                        far(other, m).wait_recv()
                        total = total + self.came[(other - 1) * planes + m].astype(F32)
                    put(m, total)

        @pl.loop(0, planes)
        def _(m):
            for step in range(n):
                near(step, m).wait_send()
            for step in range(1, n):
                far(step, m).wait_send()


def mean_of(value):
    return jnp.mean(value, axis=-1, keepdims=True)


def forward_kernel(size, *refs):
    (
        inputs,
        cotangent,
        label_row,
        label_column,
        role_bias,
        residual,
        *shards_,
    ) = refs[:12]
    (
        fulls_q,
        fulls_k,
        fulls_v,
        fulls_o,
        fulls_u,
        fulls_d,
        rows_out,
        qkv_out,
        context_out,
        lse_out,
        mid_out,
        pre_out,
        hidden_out,
        normed_out,
        inverse_out,
        final_out,
        d_second_out,
        sums_out,
    ) = refs[12:30]
    (
        rows,
        wq,
        qkv,
        context,
        lse,
        wo,
        wu,
        wd,
        hidden,
        pre,
        give,
        take,
        out,
        came,
        cot,
        labels_r,
        labels_c,
        bias,
        vectors,
        send,
        recv,
        near_sem,
    ) = refs[30:]
    k = Links(size, send, recv)
    local = Local(near_sem)
    R, D, L, wide, half, uhalf = (
        size.rows,
        size.dim,
        size.length,
        size.wide,
        size.half,
        size.uhalf,
    )
    planes, n = size.planes, size.n
    k.barrier()
    stay = k.c == k.h

    fulls = (fulls_q, fulls_k, fulls_v, fulls_o, fulls_u, fulls_d)
    spread = [Spread(k, local, s, w, i) for s, w, i in zip(shards_, fulls, INNER)]
    act = Activations(k, rows, give, take, out, came)

    def trade(source, target):
        base = k.slots(planes)
        first_local = local.next
        local.next += planes

        def pieces(m):
            at = pl.multiple_of((k.g ^ m) * wide, wide)
            return source.at[:, pl.ds(at, wide)], target(m)

        @pl.when(stay)
        def _():
            for m in range(planes):
                a, b = pieces(m)
                pltpu.make_async_copy(a, b, near_sem.at[first_local + m]).start()

        @pl.when(jnp.logical_not(stay))
        def _():
            for m in range(planes):
                a, b = pieces(m)
                k.copy(base + m, a, b, k.corner()).start()

        def wait():
            @pl.when(stay)
            def _():
                for m in range(planes):
                    a, b = pieces(m)
                    pltpu.make_async_copy(a, b, near_sem.at[first_local + m]).wait()

            @pl.when(jnp.logical_not(stay))
            def _():
                for m in range(planes):
                    a, b = pieces(m)
                    k.copy(base + m, a, b, k.corner()).wait()

        return wait

    rows_ready = trade(inputs, lambda m: rows.at[pl.ds(0, R), pl.ds(m * wide, wide)])
    for index in range(3):
        spread[index].first()

    label_slots = k.slots(2)
    label_pairs = ((label_row, labels_r), (label_column, labels_c))

    @pl.when(stay)
    def _():
        for index, (a, b) in enumerate(label_pairs):
            k.copy(label_slots + index, a, b, k.mate()).start()

    label_local = local.next
    local.next += 2

    @pl.when(stay)
    def _():
        for index, (a, b) in enumerate(label_pairs):
            pltpu.make_async_copy(a, b, near_sem.at[label_local + index]).start()

    bias_slot = k.slots()
    bias_copy = k.go(bias_slot, role_bias.at[k.c], bias.at[1], k.across())
    bias_local = local.start(role_bias.at[k.c], bias.at[0])

    for m in range(planes):
        vectors[:, pl.ds(m * wide, wide)] = residual[k.g ^ m]

    rows_ready()
    act.gather_start()
    spread[0].second()
    spread[3].first()
    spread[1].second()
    spread[2].second()
    spread[4].first()
    act.gather_relay()

    saved = []
    loads = {}

    def load(index, buffer):
        spread[index].finish()
        loads[index] = local.start(fulls[index], buffer)

    for index in range(3):
        spread[index].third()
    spread[3].second()
    for step in range(n):
        act.gather_wait(step)
    saved.append(local.start(rows, rows_out))
    bias_copy.wait_recv()
    bias_local.wait()

    @pl.when(stay)
    def _():
        for index, (a, b) in enumerate(label_pairs):
            pltpu.make_async_copy(a, b, near_sem.at[label_local + index]).wait()
            k.copy(label_slots + index, a, b, k.mate()).wait_send()

    @pl.when(jnp.logical_not(stay))
    def _():
        for index, (a, b) in enumerate(label_pairs):
            k.copy(label_slots + index, a, b, k.mate()).wait_recv()

    load(0, wq.at[0])
    load(1, wq.at[1])
    for index in range(3):
        loads[index].wait()
        for e in range(2):
            result = dot(rows[...], wq[index % 2, e])
            if index != 1:
                at = 0 if index == 0 else half
                result = result + bias[e, :, pl.ds(at, half)]
            qkv[index, :, pl.ds(e * half, half)] = result.astype(BF16)
        if index == 0:
            load(2, wq.at[0])
    saved.append(local.start(qkv, qkv_out))
    act.gather_end()

    spread[4].second()
    spread[5].first()
    cot_ready = trade(cotangent, lambda m: cot.at[:, pl.ds(m * wide, wide)])
    spread[3].third()

    order = []
    for step in range(n):
        for core in (k.c, 1 - k.c):
            order.append(core * n + (k.l + n - step) % n)
    row = jnp.concatenate([labels_r[q] for q in order], axis=-1)
    for piece, q in enumerate(order):
        column = labels_c[pl.ds(pl.multiple_of(q * R, R), R), :]
        same = column == row

        lane = lax.broadcasted_iota(jnp.int32, (R, HD), 1)
        where = pl.ds(piece * R, R)

        def one(head, kept, where=where, same=same):
            at = pl.ds(pl.multiple_of(head * HD, HD), HD)
            scores = dot(qkv[0, where, at], qkv[1, :, at], NT) * HD ** (-0.5)
            scores = jnp.where(same, scores, NEG)
            top = jnp.max(scores, axis=-1, keepdims=True)
            weights = jnp.exp(scores - top)
            summed = jnp.sum(weights, axis=-1, keepdims=True)
            probs = (weights * (1.0 / summed)).astype(BF16)
            context[where, at] = dot(probs, qkv[2, :, at]).astype(BF16)
            return jnp.where(lane == head, top + jnp.log(summed), kept)

        lse[where, :] = lax.fori_loop(0, size.heads // HD, one, jnp.zeros((R, HD), F32))

    saved.append(local.start(context, context_out))
    saved.append(local.start(lse, lse_out))

    load(3, wo)
    loads[3].wait()

    def attn_tile(m, index):
        return dot(context[pl.ds(index * R, R), :], wo[m])

    def attn_put(m, value):
        at = pl.ds(pl.multiple_of(m * wide, wide), wide)
        normed_out[:, at] = value + rows[pl.ds(0, R), at].astype(F32) + vectors[0:1, at]

    saved[0].wait()
    act.reduce(attn_tile, attn_put)
    center = normed_out[...] - mean_of(normed_out[...])
    inverse = lax.rsqrt(mean_of(center * center) + EPS)
    normed = center * inverse
    normed_out[...] = normed
    inverse_out[...] = inverse
    rows[pl.ds(0, R), :] = (normed * vectors[1:2, :] + vectors[2:3, :]).astype(BF16)
    act.gather_start()
    spread[4].third()
    spread[5].second()
    act.gather_relay()
    load(4, wu)
    loads[4].wait()
    tile = min(512, uhalf)
    for step in range(n):
        act.gather_wait(step)
        where = pl.ds(step * 2 * R, 2 * R)
        for e in range(2):

            @pl.loop(0, uhalf // tile)
            def _(j, e=e, where=where):
                at = pl.ds(pl.multiple_of(j * tile, tile), tile)
                to = pl.ds(pl.multiple_of(e * uhalf + j * tile, tile), tile)
                skip = pl.ds(pl.multiple_of(2 * half + j * tile, 128), tile)
                value = dot(rows[where, :], wu[e, :, at]) + bias[e, :, skip]
                pre[where, to] = value.astype(BF16)
                hidden[where, to] = gelu_tanh(value).astype(BF16)

    saved.append(local.start(rows, mid_out))
    saved.append(local.start(pre, pre_out))
    saved.append(local.start(hidden, hidden_out))
    act.gather_end()
    spread[5].third()
    load(5, wd)
    loads[5].wait()

    def ffn_tile(m, index):
        return dot(hidden[pl.ds(index * R, R), :], wd[m])

    def ffn_put(m, value):
        at = pl.ds(pl.multiple_of(m * wide, wide), wide)
        first = normed_out[:, at] * vectors[1:2, at] + vectors[2:3, at]
        d_second_out[:, at] = value + first + vectors[3:4, at]

    act.reduce(ffn_tile, ffn_put)
    cot_ready()
    center = d_second_out[...] - mean_of(d_second_out[...])
    inverse = lax.rsqrt(mean_of(center * center) + EPS)
    normed = center * inverse
    final_out[...] = (normed * vectors[4:5, :] + vectors[5:6, :]).astype(BF16)
    grad = cot[...].astype(F32)
    scaled = grad * vectors[4:5, :]
    inner = scaled - mean_of(scaled) - normed * mean_of(scaled * normed)
    d_second = inverse * inner
    d_second_out[...] = d_second
    sums_out[0:1, :] = jnp.sum(d_second, axis=0, keepdims=True)
    sums_out[1:2, :] = jnp.sum(grad * normed, axis=0, keepdims=True)
    sums_out[2:3, :] = jnp.sum(grad, axis=0, keepdims=True)
    for copy in saved[1:]:
        copy.wait()
    for copy in k.sent:
        copy.wait_send()


def forward(size, arrays):
    R, D, L, T = size.rows, size.dim, size.length, size.tp
    P_, n, wide, half, uhalf = size.planes, size.n, size.wide, size.half, size.uhalf
    C, U = size.heads, size.units
    whole = [jax.ShapeDtypeStruct((2, D, half), BF16)] * 3 + [
        jax.ShapeDtypeStruct((P_, C, wide), BF16),
        jax.ShapeDtypeStruct((2, D, uhalf), BF16),
        jax.ShapeDtypeStruct((P_, U, wide), BF16),
    ]
    kept = [
        jax.ShapeDtypeStruct((L, D), BF16),
        jax.ShapeDtypeStruct((3, L, C), BF16),
        jax.ShapeDtypeStruct((L, C), BF16),
        jax.ShapeDtypeStruct((L, HD), F32),
        jax.ShapeDtypeStruct((L, D), BF16),
        jax.ShapeDtypeStruct((L, U), BF16),
        jax.ShapeDtypeStruct((L, U), BF16),
    ]
    ends = [
        jax.ShapeDtypeStruct((R, D), F32),
        jax.ShapeDtypeStruct((R, 1), F32),
        jax.ShapeDtypeStruct((R, D), BF16),
        jax.ShapeDtypeStruct((R, D), F32),
        jax.ShapeDtypeStruct((3, D), F32),
    ]
    anywhere = pl.BlockSpec(memory_space=pl.ANY)
    vmem = pl.BlockSpec(memory_space=pltpu.VMEM)
    width = 2 * half + uhalf
    slots = 6 * (3 + 2 * (P_ - 1)) + 2 * P_ + 3 + 2 * n + 2 * n * P_
    scratch = [
        pltpu.VMEM((L, D), BF16),
        pltpu.VMEM((2, 2, D, half), BF16),
        pltpu.VMEM((3, L, C), BF16),
        pltpu.VMEM((L, C), BF16),
        pltpu.VMEM((L, HD), F32),
        pltpu.VMEM((P_, C, wide), BF16),
        pltpu.VMEM((2, D, uhalf), BF16),
        pltpu.VMEM((P_, U, wide), BF16),
        pltpu.VMEM((L, U), BF16),
        pltpu.VMEM((L, U), BF16),
        pltpu.VMEM((n * P_, R, wide), BF16),
        pltpu.VMEM((n * P_, R, wide), BF16),
        pltpu.VMEM((max(n - 1, 1) * P_, R, wide), BF16),
        pltpu.VMEM((max(n - 1, 1) * P_, R, wide), BF16),
        pltpu.VMEM((R, D), BF16),
        pltpu.VMEM((T, 1, R), jnp.int32),
        pltpu.VMEM((L, 1), jnp.int32),
        pltpu.VMEM((2, 1, width), F32),
        pltpu.VMEM((8, D), F32),
        pltpu.SemaphoreType.DMA((slots,)),
        pltpu.SemaphoreType.DMA((slots,)),
        pltpu.SemaphoreType.DMA((32 + 2 * P_,)),
    ]
    return pl.pallas_call(
        functools.partial(forward_kernel, size),
        out_shape=whole + kept + ends,
        in_specs=[anywhere, anywhere, vmem, vmem, vmem, vmem] + [anywhere] * 6,
        out_specs=[anywhere] * 13 + [vmem] * 5,
        scratch_shapes=scratch,
        compiler_params=pltpu.CompilerParams(
            collective_id=0, has_side_effects=True, vmem_limit_bytes=VMEM
        ),
        name="forward",
    )(*arrays)


def shards(
    fsdp,
    tp,
    inputs,
    query_weight,
    query_bias,
    key_weight,
    value_weight,
    value_bias,
    output_weight,
    output_bias,
    first_gain,
    first_shift,
    up_weight,
    up_bias,
    down_weight,
    down_bias,
    second_gain,
    second_shift,
    segments,
    cotangent,
):
    lay = Layout(fsdp, tp)
    length = segments.shape[1]
    local = query_weight.shape[1] // HD
    rows_own = inputs.shape[0]

    def heads(table):
        return table.reshape(length, local, HD)

    size = Sizes(fsdp, tp, inputs, query_weight, up_weight, segments)
    residual_vectors = jnp.stack(
        [output_bias, first_gain, first_shift, down_bias, second_gain, second_shift] + [output_bias] * 2
    )
    residual_vectors = residual_vectors.reshape(8, size.planes, size.wide).transpose(1, 0, 2)
    role_bias = jnp.concatenate(
        [v.reshape(2, -1) for v in (query_bias, value_bias, up_bias)], axis=1
    )[:, None]
    results = forward(
        size,
        (
            inputs,
            cotangent,
            segments.reshape(tp, 1, rows_own),
            segments.reshape(length, 1),
            role_bias,
            residual_vectors,
            query_weight,
            key_weight,
            value_weight,
            output_weight,
            up_weight,
            down_weight,
        ),
    )
    query_full, key_full, value_full, up_full = (
        jnp.concatenate([results[i][0], results[i][1]], axis=1) for i in (0, 1, 2, 4)
    )
    output_full, down_full = (
        results[i].transpose(1, 0, 2).reshape(results[i].shape[1], -1) for i in (3, 5)
    )
    rows_all, (query, keys, value), context, log_total, mid_all, pre, hidden = results[6:13]
    first_normed, first_inv, final, d_second, sums = results[13:]
    log_total = log_total[:, :local].T
    layer_out = lay.relative(lay.trade(final))
    down_bias_term, second_gain_term, second_shift_term = sums[0], sums[1], sums[2]
    first_gain = lay.relative(first_gain)
    gelu_back = jax.vjp(gelu_tanh, pre.astype(F32))[1]
    labels = jnp.where(lay.c == lay.h, segments[0], lay.core(segments[0]))
    label_parts = []
    for step in range(lay.n):
        for core in (lay.c, 1 - lay.c):
            at = (core * lay.n + (lay.l + lay.n - step) % lay.n) * rows_own
            label_parts.append(lax.dynamic_slice_in_dim(labels, at, rows_own))
    labels = jnp.concatenate(label_parts)

    def rows_at(table, step):
        return table[2 * rows_own * step : 2 * rows_own * (step + 1)]

    d_branch_all = lay.gather(d_second.astype(BF16))
    d_hidden = against(d_branch_all, down_full)
    d_pre = gelu_back(d_hidden)[0].astype(BF16)
    up_bias_term = jnp.sum(d_pre.astype(F32), axis=0)
    d_mid = lay.reduce(lambda step: against(rows_at(d_pre, step), up_full))
    down_term = across(hidden, d_branch_all)
    up_term = across(mid_all, d_pre)
    down_grad = lay.collect(down_term, 1)
    up_grad = lay.collect(up_term, 0)
    d_first = d_mid + d_second
    d_first_sum, first_gain_term, first_shift_term = norm_back(
        d_first, first_normed, first_inv, first_gain
    )
    output_bias_term = jnp.sum(d_first_sum, axis=0)
    d_attn_all = lay.gather(d_first_sum.astype(BF16))
    d_context = against(d_attn_all, output_full).astype(BF16)
    output_term = across(context, d_attn_all)
    output_grad = lay.collect(output_term, 1)
    d_query, d_key, d_value = (
        v.reshape(length, local * HD)
        for v in attend_back(
            heads(query), heads(keys), heads(value), heads(d_context), log_total, labels
        )
    )
    query_bias_term = jnp.sum(d_query.astype(F32), axis=0)
    value_bias_term = jnp.sum(d_value.astype(F32), axis=0)
    d_rows = lay.reduce(
        lambda step: against(rows_at(d_query, step), query_full)
        + against(rows_at(d_key, step), key_full)
        + against(rows_at(d_value, step), value_full)
    )
    input_grad = lay.relative(lay.trade((d_rows + d_first_sum).astype(BF16)))
    query_grad = lay.collect(across(rows_all, d_query), 0)
    key_grad = lay.collect(across(rows_all, d_key), 0)
    value_grad = lay.collect(across(rows_all, d_value), 0)

    def small(terms):
        total = lax.psum(jnp.concatenate(terms), AXES)
        result, at = [], 0
        for term in terms:
            result.append(total[at : at + term.shape[0]])
            at += term.shape[0]
        return result

    f, t = lax.axis_index("fsdp"), lax.axis_index("tp")

    def residual(vector):
        size = vector.shape[0] // (fsdp * tp)
        return lax.dynamic_slice_in_dim(vector, (f * tp + t) * size, size)

    def split(vector):
        size = vector.shape[0] // (fsdp * tp)
        return lax.dynamic_slice_in_dim(vector, (t * fsdp + f) * size, size)[None]

    early = small(
        [
            lay.relative(v)
            for v in (
                down_bias_term,
                second_gain_term,
                second_shift_term,
                output_bias_term,
                first_gain_term,
                first_shift_term,
            )
        ]
        + [lay.unrole(up_bias_term)]
    )
    late = small([lay.unrole(query_bias_term), lay.unrole(value_bias_term)])
    return (
        layer_out,
        input_grad,
        query_grad,
        split(late[0]),
        key_grad,
        value_grad,
        split(late[1]),
        output_grad,
        residual(early[3]),
        residual(early[4]),
        residual(early[5]),
        up_grad,
        split(early[6]),
        down_grad,
        residual(early[0]),
        residual(early[1]),
        residual(early[2]),
    )


def solution(mesh):
    fsdp, tp = mesh.shape["fsdp"], mesh.shape["tp"]

    def body(*arrays):
        return shards(fsdp, tp, *arrays)

    tokens, inner, outer = P(AXES, None), P("fsdp", "tp"), P("tp", "fsdp")
    placed = (
        tokens,
        inner,
        P("tp"),
        inner,
        inner,
        P("tp"),
        outer,
        P(),
        P(),
        P(),
        inner,
        P("tp"),
        outer,
        P(),
        P(),
        P(),
        P("fsdp", None),
        tokens,
    )
    return jax.shard_map(
        body,
        mesh=mesh,
        in_specs=placed,
        out_specs=(
            tokens,
            tokens,
            inner,
            outer,
            inner,
            inner,
            outer,
            outer,
            P(AXES),
            P(AXES),
            P(AXES),
            inner,
            outer,
            outer,
            P(AXES),
            P(AXES),
            P(AXES),
        ),
        check_vma=False,
    )
```

```python
import functools

import jax
import jax.numpy as jnp
from jax import lax
from jax.experimental import pallas as pl
from jax.experimental.pallas import tpu as pltpu
from jax.sharding import PartitionSpec as P

HD = 128
EPS = 1e-06
NEG = -1000000000.0
AXES = ("fsdp", "tp")
F32 = jnp.float32
BF16 = jnp.bfloat16
MESH = pl.DeviceIdType.MESH
VMEM = 62 * 2**20


def gelu_tanh(values):
    return jax.nn.gelu(values, approximate=True)


def dot(left, right, dims=((1,), (0,))):
    return lax.dot_general(left, right, (dims, ((), ())), preferred_element_type=F32)


NN, NT, TN = ((1,), (0,)), ((1,), (1,)), ((0,), (0,))


class Sizes:
    def __init__(self, fsdp, tp, inputs, query_weight, up_weight, segments):
        self.fsdp, self.tp = fsdp, tp
        self.planes, self.n = fsdp // 2, tp // 2
        self.rows, self.dim = inputs.shape
        self.length = segments.shape[1]
        self.fine = query_weight.shape[0]
        self.wide = 2 * self.fine
        self.heads = query_weight.shape[1]
        self.half = self.heads // 2
        self.units = up_weight.shape[1]
        self.uhalf = self.units // 2


INNER = (True, True, True, False, True, False)


class Links:
    def __init__(self, size, send, recv):
        self.size, self.send, self.recv = size, send, recv
        f, t = lax.axis_index("fsdp"), lax.axis_index("tp")
        self.g, self.c = f // 2, f % 2
        self.h, self.l = t // size.n, t % size.n
        self.done = set()
        self.sent = []
        self.next = 0

    def device(self, g, c, h, l):
        return (g * 2 + c, h * self.size.n + l)

    def mate(self):
        return self.device(self.g, 1 - self.c, self.h, self.l)

    def across(self):
        return self.device(self.g, self.c, 1 - self.h, self.l)

    def corner(self):
        return self.device(self.g, 1 - self.c, 1 - self.h, self.l)

    def plane(self, mask):
        return self.device(self.g ^ mask, self.c, self.h, self.l)

    def along(self, step):
        return self.device(self.g, self.c, self.h, (self.l + step) % self.size.n)

    def barrier(self):
        size = self.size
        peers = [self.mate(), self.across(), self.corner()]
        mask = 1
        while mask < size.planes:
            peers.append(self.plane(mask))
            mask *= 2
        peers += [self.along(step) for step in range(1, size.n)]
        semaphore = pltpu.get_barrier_semaphore()
        for peer in peers:
            pl.semaphore_signal(semaphore, inc=1, device_id=peer, device_id_type=MESH)
        pl.semaphore_wait(semaphore, len(peers))

    def slots(self, count=1):
        first = self.next
        self.next += count
        return first

    def copy(self, slot, source, target, device):
        return pltpu.make_async_remote_copy(
            src_ref=source,
            dst_ref=target,
            send_sem=self.send.at[slot],
            recv_sem=self.recv.at[slot],
            device_id=device,
            device_id_type=MESH,
        )

    def go(self, slot, source, target, device):
        copy = self.copy(slot, source, target, device)
        copy.start()
        self.sent.append(copy)
        return copy


class Local:
    def __init__(self, semaphores):
        self.semaphores, self.next = semaphores, 0

    def start(self, source, target):
        copy = pltpu.make_async_copy(source, target, self.semaphores.at[self.next])
        self.next += 1
        copy.start()
        return copy


class Spread:
    def __init__(self, links, local, shard, full, inner):
        self.links, self.local = links, local
        self.shard, self.full, self.inner = shard, full, inner
        self.base = links.slots(3 + 2 * (links.size.planes - 1))
        self.waited = set()

    def part(self, index):
        axis = 1 if self.inner else 0
        width = self.shard.shape[axis] // 2
        at = pl.multiple_of(index * width, width)
        return self.shard.at[:, pl.ds(at, width)] if self.inner else self.shard.at[pl.ds(at, width)]

    def home(self, e, c):
        fine = self.links.size.fine
        at = pl.ds(pl.multiple_of(c * fine, fine), fine)
        if self.inner:
            return self.full.at[e, at, :]
        width = self.full.shape[1] // 2
        return self.full.at[0, pl.ds(e * width, width), at]

    def block(self, m, e=None):
        wide = self.links.size.wide
        if self.inner:
            at = pl.ds(m * wide, wide)
            return self.full.at[:, at, :] if e is None else self.full.at[e, at, :]
        width = self.full.shape[1] // 2
        return self.full.at[m] if e is None else self.full.at[m, pl.ds(e * width, width)]

    def first(self):
        k = self.links
        mine, other = self.part(k.c), self.part(1 - k.c)
        self.own = self.local.start(mine, self.home(0, k.c))
        self.steps = [
            k.go(self.base, other, self.home(0, k.c), k.mate()),
            k.go(self.base + 1, mine, self.home(1, k.c), k.across()),
            k.go(self.base + 2, other, self.home(1, k.c), k.corner()),
        ]

    def second(self):
        k = self.links
        for step in self.steps:
            step.wait_recv()
        self.own.wait()
        self.pieces = {}
        mask = 1
        while mask < k.size.planes:
            copy = k.go(self.base + 1 + 2 * mask, self.block(0), self.block(mask), k.plane(mask))
            self.pieces[mask, 0] = self.pieces[mask, 1] = copy
            mask *= 2

    def arrive(self, m, e):
        copy = self.pieces[m, e]
        if id(copy) not in self.waited:
            self.waited.add(id(copy))
            copy.wait_recv()

    def third(self):
        k = self.links
        for m in sorted(range(1, k.size.planes), key=lambda v: bin(v).count("1")):
            if bin(m).count("1") > 1:
                top, low = 1 << (m.bit_length() - 1), m & -m
                for e, bit in ((0, top), (1, low)):
                    self.arrive(m ^ bit, e)
                    self.pieces[m, e] = k.go(
                        self.base + 1 + 2 * m + e,
                        self.block(m ^ bit, e),
                        self.block(m, e),
                        k.plane(bit),
                    )

    def finish(self):
        for m in range(1, self.links.size.planes):
            for e in range(2):
                self.arrive(m, e)


class Activations:
    def __init__(self, links, rows, give, take, out, came):
        self.links, self.rows = links, rows
        self.give, self.take, self.out, self.came = give, take, out, came
        size = links.size
        self.gather_slots = links.slots(2 * size.n)
        self.mate_slots = links.slots(size.n * size.planes)
        self.along_slots = links.slots(size.n * size.planes)

    def piece(self, index):
        size = self.links.size
        return self.rows.at[pl.ds(index * size.rows, size.rows)]

    def gather_start(self):
        k, base = self.links, self.gather_slots
        self.far = [
            k.go(base + step, self.piece(0), self.piece(2 * step), k.along(step))
            for step in range(1, k.size.n)
        ]
        self.near = [k.go(base + k.size.n, self.piece(0), self.piece(1), k.mate())]

    def gather_relay(self):
        k, base = self.links, self.gather_slots
        for step in range(1, k.size.n):
            self.far[step - 1].wait_recv()
            self.near.append(
                k.go(
                    base + k.size.n + step,
                    self.piece(2 * step),
                    self.piece(2 * step + 1),
                    k.mate(),
                )
            )

    def gather_wait(self, step):
        self.near[step].wait_recv()

    def gather_end(self):
        over = self.far + self.near
        for copy in over:
            copy.wait_send()
        self.links.sent = [c for c in self.links.sent if all(c is not o for o in over)]

    def near_copy(self, step, m):
        k = self.links
        at = step * k.size.planes + m
        return k.copy(self.mate_slots + at, self.give.at[m], self.take.at[at], k.mate())

    def far_copy(self, step, m):
        k = self.links
        at = (step - 1) * k.size.planes + m
        return k.copy(self.along_slots + at, self.out.at[at], self.came.at[at], k.along(step))

    def reduce_step(self, step, tile, put):
        planes, n = self.links.size.planes, self.links.size.n
        index = 2 * ((n - step) % n)

        @pl.loop(0, planes)
        def _(m):
            value = tile(m, index + 1).astype(BF16)
            if step != 1 and n > 1:
                self.near_copy(step - 1 if step else n - 1, m).wait_send()
            self.give[m] = value
            self.near_copy(step, m).start()

        @pl.loop(0, planes)
        def _(m):
            total = tile(m, index)
            self.near_copy(step, m).wait_recv()
            total = total + self.take[step * planes + m].astype(F32)
            if step:
                self.out[(step - 1) * planes + m] = total.astype(BF16)
                self.far_copy(step, m).start()
            else:
                for other in range(1, n):
                    self.far_copy(other, m).wait_recv()
                    total = total + self.came[(other - 1) * planes + m].astype(F32)
                put(m, total)

    def reduce_end(self):
        planes, n = self.links.size.planes, self.links.size.n

        @pl.loop(0, planes)
        def _(m):
            self.near_copy(0, m).wait_send()
            for step in range(1, n):
                self.far_copy(step, m).wait_send()

    def reduce(self, tile, put):
        for step in list(range(1, self.links.size.n)) + [0]:
            self.reduce_step(step, tile, put)
        self.reduce_end()


def mean_of(value):
    return jnp.mean(value, axis=-1, keepdims=True)


def forward_kernel(size, *refs):
    (
        inputs,
        cotangent,
        label_row,
        label_column,
        role_bias,
        residual,
        *shards_,
    ) = refs[:12]
    (
        fulls_q,
        fulls_k,
        fulls_v,
        fulls_o,
        fulls_u,
        fulls_d,
        rows_out,
        qkv_out,
        context_out,
        lse_out,
        mid_out,
        pre_out,
        hidden_out,
        normed_out,
        inverse_out,
        final_out,
        d_second_out,
        sums_out,
        label_row_out,
        label_column_out,
    ) = refs[12:32]
    (
        rows,
        wq,
        qkv,
        context,
        lse,
        wo,
        wu,
        wd,
        hidden,
        pre,
        give,
        take,
        out,
        came,
        cot,
        labels_r,
        labels_c,
        bias,
        vectors,
        send,
        recv,
        near_sem,
    ) = refs[32:]
    k = Links(size, send, recv)
    local = Local(near_sem)
    R, D, L, wide, half, uhalf = (
        size.rows,
        size.dim,
        size.length,
        size.wide,
        size.half,
        size.uhalf,
    )
    planes, n = size.planes, size.n
    k.barrier()
    stay = k.c == k.h

    fulls = (fulls_q, fulls_k, fulls_v, fulls_o, fulls_u, fulls_d)
    spread = [Spread(k, local, s, w, i) for s, w, i in zip(shards_, fulls, INNER)]
    act = Activations(k, rows, give, take, out, came)

    def trade(source, target):
        base = k.slots(planes)
        first_local = local.next
        local.next += planes

        def pieces(m):
            at = pl.multiple_of((k.g ^ m) * wide, wide)
            return source.at[:, pl.ds(at, wide)], target(m)

        @pl.when(stay)
        def _():
            for m in range(planes):
                a, b = pieces(m)
                pltpu.make_async_copy(a, b, near_sem.at[first_local + m]).start()

        @pl.when(jnp.logical_not(stay))
        def _():
            for m in range(planes):
                a, b = pieces(m)
                k.copy(base + m, a, b, k.corner()).start()

        def wait():
            @pl.when(stay)
            def _():
                for m in range(planes):
                    a, b = pieces(m)
                    pltpu.make_async_copy(a, b, near_sem.at[first_local + m]).wait()

            @pl.when(jnp.logical_not(stay))
            def _():
                for m in range(planes):
                    a, b = pieces(m)
                    k.copy(base + m, a, b, k.corner()).wait()

        return wait

    rows_ready = trade(inputs, lambda m: rows.at[pl.ds(0, R), pl.ds(m * wide, wide)])
    for index in range(3):
        spread[index].first()

    label_slots = k.slots(2)
    label_pairs = ((label_row, labels_r), (label_column, labels_c))

    @pl.when(stay)
    def _():
        for index, (a, b) in enumerate(label_pairs):
            k.copy(label_slots + index, a, b, k.mate()).start()

    label_local = local.next
    local.next += 2

    @pl.when(stay)
    def _():
        for index, (a, b) in enumerate(label_pairs):
            pltpu.make_async_copy(a, b, near_sem.at[label_local + index]).start()

    bias_slot = k.slots()
    bias_copy = k.go(bias_slot, role_bias.at[k.c], bias.at[1], k.across())
    bias_local = local.start(role_bias.at[k.c], bias.at[0])

    for m in range(planes):
        vectors[:, pl.ds(m * wide, wide)] = residual[k.g ^ m]

    rows_ready()
    act.gather_start()
    spread[0].second()
    spread[3].first()
    spread[1].second()
    spread[2].second()
    spread[4].first()
    act.gather_relay()

    saved = []
    loads = {}

    def load(index, buffer):
        spread[index].finish()
        loads[index] = local.start(fulls[index], buffer)

    for index in range(3):
        spread[index].third()
    spread[3].second()
    for step in range(n):
        act.gather_wait(step)
    saved.append(local.start(rows, rows_out))
    bias_copy.wait_recv()
    bias_local.wait()

    @pl.when(stay)
    def _():
        for index, (a, b) in enumerate(label_pairs):
            pltpu.make_async_copy(a, b, near_sem.at[label_local + index]).wait()
            k.copy(label_slots + index, a, b, k.mate()).wait_send()

    @pl.when(jnp.logical_not(stay))
    def _():
        for index, (a, b) in enumerate(label_pairs):
            k.copy(label_slots + index, a, b, k.mate()).wait_recv()

    load(0, wq.at[0])
    load(1, wq.at[1])
    for index in range(3):
        loads[index].wait()
        for e in range(2):
            result = dot(rows[...], wq[index % 2, e])
            if index != 1:
                at = 0 if index == 0 else half
                result = result + bias[e, :, pl.ds(at, half)]
            qkv[index, :, pl.ds(e * half, half)] = result.astype(BF16)
        if index == 0:
            load(2, wq.at[0])
    saved.append(local.start(qkv, qkv_out))
    act.gather_end()

    spread[4].second()
    spread[5].first()
    cot_ready = trade(cotangent, lambda m: cot.at[:, pl.ds(m * wide, wide)])
    spread[3].third()

    order = []
    for step in range(n):
        for core in (k.c, 1 - k.c):
            order.append(core * n + (k.l + n - step) % n)
    row = jnp.concatenate([labels_r[q] for q in order], axis=-1)
    label_row_out[...] = row
    for piece, q in enumerate(order):
        column = labels_c[pl.ds(pl.multiple_of(q * R, R), R), :]
        label_column_out[pl.ds(piece * R, R), :] = column
        same = column == row

        lane = lax.broadcasted_iota(jnp.int32, (R, HD), 1)
        where = pl.ds(piece * R, R)

        def one(head, kept, where=where, same=same):
            at = pl.ds(pl.multiple_of(head * HD, HD), HD)
            scores = dot(qkv[0, where, at], qkv[1, :, at], NT) * HD ** (-0.5)
            scores = jnp.where(same, scores, NEG)
            top = jnp.max(scores, axis=-1, keepdims=True)
            weights = jnp.exp(scores - top)
            summed = jnp.sum(weights, axis=-1, keepdims=True)
            probs = (weights * (1.0 / summed)).astype(BF16)
            context[where, at] = dot(probs, qkv[2, :, at]).astype(BF16)
            return jnp.where(lane == head, top + jnp.log(summed), kept)

        lse[where, :] = lax.fori_loop(0, size.heads // HD, one, jnp.zeros((R, HD), F32))

    saved.append(local.start(context, context_out))
    saved.append(local.start(lse, lse_out))

    load(3, wo)
    loads[3].wait()

    def attn_tile(m, index):
        return dot(context[pl.ds(index * R, R), :], wo[m])

    def attn_put(m, value):
        at = pl.ds(pl.multiple_of(m * wide, wide), wide)
        normed_out[:, at] = value + rows[pl.ds(0, R), at].astype(F32) + vectors[0:1, at]

    saved[0].wait()
    act.reduce(attn_tile, attn_put)

    @pl.loop(0, R // 16)
    def _(i):
        at = pl.ds(pl.multiple_of(i * 16, 16), 16)
        summed = normed_out[at, :]
        center = summed - mean_of(summed)
        scale = lax.rsqrt(mean_of(center * center) + EPS)
        normed = center * scale
        normed_out[at, :] = normed
        inverse_out[at, :] = scale
        rows[at, :] = (normed * vectors[1:2, :] + vectors[2:3, :]).astype(BF16)

    act.gather_start()
    spread[4].third()
    spread[5].second()
    act.gather_relay()
    load(4, wu)
    loads[4].wait()
    tile = min(512, uhalf)
    for step in range(n):
        act.gather_wait(step)
        where = pl.ds(step * 2 * R, 2 * R)
        for e in range(2):

            @pl.loop(0, uhalf // tile)
            def _(j, e=e, where=where):
                at = pl.ds(pl.multiple_of(j * tile, tile), tile)
                to = pl.ds(pl.multiple_of(e * uhalf + j * tile, tile), tile)
                skip = pl.ds(pl.multiple_of(2 * half + j * tile, 128), tile)
                value = dot(rows[where, :], wu[e, :, at]) + bias[e, :, skip]
                pre[where, to] = value.astype(BF16)
                hidden[where, to] = gelu_tanh(value).astype(BF16)

    saved.append(local.start(rows, mid_out))
    saved.append(local.start(pre, pre_out))
    saved.append(local.start(hidden, hidden_out))
    act.gather_end()
    spread[5].third()
    load(5, wd)
    loads[5].wait()

    def ffn_tile(m, index):
        return dot(hidden[pl.ds(index * R, R), :], wd[m])

    def ffn_put(m, value):
        at = pl.ds(pl.multiple_of(m * wide, wide), wide)
        first = normed_out[:, at] * vectors[1:2, at] + vectors[2:3, at]
        d_second_out[:, at] = value + first + vectors[3:4, at]

    act.reduce(ffn_tile, ffn_put)
    cot_ready()
    sums_out[...] = jnp.zeros_like(sums_out)

    @pl.loop(0, R // 16)
    def _(i):
        at = pl.ds(pl.multiple_of(i * 16, 16), 16)
        summed = d_second_out[at, :]
        center = summed - mean_of(summed)
        scale = lax.rsqrt(mean_of(center * center) + EPS)
        normed = center * scale
        final_out[at, :] = (normed * vectors[4:5, :] + vectors[5:6, :]).astype(BF16)
        grad = cot[at, :].astype(F32)
        scaled = grad * vectors[4:5, :]
        d_second = scale * (scaled - mean_of(scaled) - normed * mean_of(scaled * normed))
        d_second_out[at, :] = d_second
        for index, value in enumerate((d_second, grad * normed, grad)):
            sums_out[index : index + 1, :] += jnp.sum(value, axis=0, keepdims=True)

    for copy in saved[1:]:
        copy.wait()
    for copy in k.sent:
        copy.wait_send()


def forward(size, arrays):
    R, D, L, T = size.rows, size.dim, size.length, size.tp
    P_, n, wide, half, uhalf = size.planes, size.n, size.wide, size.half, size.uhalf
    C, U = size.heads, size.units
    whole = [jax.ShapeDtypeStruct((2, D, half), BF16)] * 3 + [
        jax.ShapeDtypeStruct((P_, C, wide), BF16),
        jax.ShapeDtypeStruct((2, D, uhalf), BF16),
        jax.ShapeDtypeStruct((P_, U, wide), BF16),
    ]
    kept = [
        jax.ShapeDtypeStruct((L, D), BF16),
        jax.ShapeDtypeStruct((3, L, C), BF16),
        jax.ShapeDtypeStruct((L, C), BF16),
        jax.ShapeDtypeStruct((L, HD), F32),
        jax.ShapeDtypeStruct((L, D), BF16),
        jax.ShapeDtypeStruct((L, U), BF16),
        jax.ShapeDtypeStruct((L, U), BF16),
    ]
    ends = [
        jax.ShapeDtypeStruct((R, D), F32),
        jax.ShapeDtypeStruct((R, 1), F32),
        jax.ShapeDtypeStruct((R, D), BF16),
        jax.ShapeDtypeStruct((R, D), F32),
        jax.ShapeDtypeStruct((3, D), F32),
        jax.ShapeDtypeStruct((1, L), jnp.int32),
        jax.ShapeDtypeStruct((L, 1), jnp.int32),
    ]
    anywhere = pl.BlockSpec(memory_space=pl.ANY)
    vmem = pl.BlockSpec(memory_space=pltpu.VMEM)
    width = 2 * half + uhalf
    slots = 6 * (3 + 2 * (P_ - 1)) + 2 * P_ + 3 + 2 * n + 2 * n * P_
    scratch = [
        pltpu.VMEM((L, D), BF16),
        pltpu.VMEM((2, 2, D, half), BF16),
        pltpu.VMEM((3, L, C), BF16),
        pltpu.VMEM((L, C), BF16),
        pltpu.VMEM((L, HD), F32),
        pltpu.VMEM((P_, C, wide), BF16),
        pltpu.VMEM((2, D, uhalf), BF16),
        pltpu.VMEM((P_, U, wide), BF16),
        pltpu.VMEM((L, U), BF16),
        pltpu.VMEM((L, U), BF16),
        pltpu.VMEM((P_, R, wide), BF16),
        pltpu.VMEM((n * P_, R, wide), BF16),
        pltpu.VMEM((max(n - 1, 1) * P_, R, wide), BF16),
        pltpu.VMEM((max(n - 1, 1) * P_, R, wide), BF16),
        pltpu.VMEM((R, D), BF16),
        pltpu.VMEM((T, 1, R), jnp.int32),
        pltpu.VMEM((L, 1), jnp.int32),
        pltpu.VMEM((2, 1, width), F32),
        pltpu.VMEM((8, D), F32),
        pltpu.SemaphoreType.DMA((slots,)),
        pltpu.SemaphoreType.DMA((slots,)),
        pltpu.SemaphoreType.DMA((32 + 2 * P_,)),
    ]
    return pl.pallas_call(
        functools.partial(forward_kernel, size),
        out_shape=whole + kept + ends,
        in_specs=[anywhere, anywhere, vmem, vmem, vmem, vmem] + [anywhere] * 6,
        out_specs=[anywhere] * 13 + [vmem] * 7,
        scratch_shapes=scratch,
        compiler_params=pltpu.CompilerParams(
            collective_id=0, has_side_effects=True, vmem_limit_bytes=VMEM
        ),
        name="forward",
    )(*arrays)


class Collect:
    def __init__(self, links, grad, came, last, inner):
        self.links, self.grad, self.came, self.last, self.inner = links, grad, came, last, inner
        self.planes = links.size.planes
        self.base = links.slots(2 * (self.planes - 1) + 3)
        self.flying = {}

    def block(self, m, e):
        wide = self.links.size.wide
        if self.inner:
            return self.grad.at[e, pl.ds(m * wide, wide), :]
        width = self.grad.shape[1] // 2
        return self.grad.at[m, pl.ds(e * width, width), :]

    def home(self, e, c):
        fine = self.links.size.fine
        at = pl.ds(pl.multiple_of(c * fine, fine), fine)
        if self.inner:
            return self.grad.at[e, at, :]
        width = self.grad.shape[1] // 2
        return self.grad.at[0, pl.ds(e * width, width), at]

    @staticmethod
    def bit(m, e):
        return m & -m if e else 1 << (m.bit_length() - 1)

    def sources(self, m, e):
        return [o for o in range(1, self.planes) if o != m and o ^ self.bit(o, e) == m]

    def order(self):
        count = lambda v: bin(v).count("1")
        pairs = [(m, e) for m in range(1, self.planes) for e in range(2)]
        return sorted(pairs, key=lambda p: (-count(p[0]), len(self.sources(*p))))

    def send(self, m, e):
        self.flying[m, e] = self.links.go(
            self.base + 2 * (m - 1) + e,
            self.block(m, e),
            self.came.at[m - 1, e],
            self.links.plane(self.bit(m, e)),
        )

    def ready(self, m):
        for e in range(2):
            if m and not self.sources(m, e):
                self.send(m, e)

    def levels(self):
        return sorted({bin(m).count("1") for m, e in self.order() if self.sources(m, e)}, reverse=True)

    def advance(self, adder, level):
        for m, e in self.order():
            if bin(m).count("1") == level and self.sources(m, e):
                adder(self, m, e)
                self.send(m, e)

    def finish(self, adder):
        k = self.links
        for e in range(2):
            adder(self, 0, e)
        k.go(self.base + 2 * (self.planes - 1), self.home(0, 1 - k.c), self.last.at[1], k.mate())
        k.go(self.base + 2 * (self.planes - 1) + 1, self.home(1, k.c), self.last.at[2], k.across())
        k.go(
            self.base + 2 * (self.planes - 1) + 2,
            self.home(1, 1 - k.c),
            self.last.at[3],
            k.corner(),
        )
        self.final = k.sent[-3:]

    def arrive(self):
        for copy in self.final:
            copy.wait_recv()


def gelu_slope(v):
    scale = 0.7978845608028654
    square = v * v
    t = jnp.tanh(scale * v * (1.0 + 0.044715 * square))
    return 0.5 * (1.0 + t) + 0.5 * v * (1.0 - t * t) * scale * (1.0 + 3 * 0.044715 * square)


def backward_kernel(size, *refs):
    (
        full_q,
        full_k,
        full_v,
        full_o,
        full_u,
        full_d,
        rows_in,
        qkv_in,
        context_in,
        lse_in,
        mid_in,
        pre_in,
        hidden_in,
        normed,
        inverse,
        final,
        d_second,
        sums,
        label_row,
        label_column,
        residual,
    ) = refs[:21]
    (
        layer_out,
        input_grad,
        grad_d,
        grad_u,
        grad_o,
        grad_x,
        came_d,
        came_u,
        came_o,
        came_x,
        last_d,
        last_u,
        last_o,
        last_x,
        small_d,
        small_q,
        small_u,
    ) = refs[21:38]
    (
        rows,
        wbuf,
        wu,
        wo,
        abuf,
        dp,
        qkv,
        dqkv,
        context,
        d_context,
        lse,
        give,
        take,
        out,
        came,
        dfs,
        dk,
        dv,
        stage,
        parts_inner,
        parts_outer,
        got_d,
        got_q,
        got_u,
        gain,
        ends_acc,
        send,
        recv,
        near_sem,
        stage_sem,
        part_sem,
        free_sem,
    ) = refs[38:]
    k = Links(size, send, recv)
    local = Local(near_sem)
    R, D, L, wide, half, uhalf, T = (
        size.rows,
        size.dim,
        size.length,
        size.wide,
        size.half,
        size.uhalf,
        size.tp,
    )
    planes, n, C, U = size.planes, size.n, size.heads, size.units
    width = 3 * half
    act = Activations(k, rows, give, take, out, came)
    down = Collect(k, grad_d, came_d, last_d, False)
    up = Collect(k, grad_u, came_u, last_u, True)
    outer = Collect(k, grad_o, came_o, last_o, False)
    inner = Collect(k, grad_x, came_x, last_x, True)
    k.barrier()
    stay = k.c == k.h

    def trade(source, target):
        base = k.slots(planes)
        first_local = local.next
        local.next += planes

        def pieces(m):
            at = pl.multiple_of((k.g ^ m) * wide, wide)
            return source.at[:, pl.ds(m * wide, wide)], target.at[:, pl.ds(at, wide)]

        def both(go):
            @pl.when(stay)
            def _():
                for m in range(planes):
                    copy = pltpu.make_async_copy(*pieces(m), near_sem.at[first_local + m])
                    copy.start() if go else copy.wait()

            @pl.when(jnp.logical_not(stay))
            def _():
                for m in range(planes):
                    copy = k.copy(base + m, *pieces(m), k.corner())
                    copy.start() if go else copy.wait()

        both(True)
        return lambda: both(False)

    loads = {}
    start = local.start(d_second, dfs)
    start.wait()
    rows[pl.ds(0, R), :] = dfs[...].astype(BF16)
    act.gather_start()
    loads["pre"] = [local.start(pre_in, dp)]
    loads["down"] = [
        local.start(full_d.at[m], wbuf.at[pl.ds(0, U), pl.ds(m * wide, wide)])
        for m in range(planes)
    ]
    loads["up"] = [local.start(full_u.at[e], wu.at[:, pl.ds(e * uhalf, uhalf)]) for e in range(2)]
    loads["hidden"] = [local.start(hidden_in, abuf.at[:, pl.ds(0, U)])]
    layer_done = trade(final, layer_out)
    loads["attention"] = [
        local.start(qkv_in, qkv),
        local.start(context_in, context),
        local.start(lse_in, lse),
        local.start(full_o, wo),
    ]
    for m in range(planes):
        gain[:, pl.ds(m * wide, wide)] = residual[k.g ^ m]

    def loaded(name):
        for copy in loads[name]:
            copy.wait()

    small_d[...] = jnp.zeros_like(small_d)
    small_q[...] = jnp.zeros_like(small_q)
    small_u[...] = jnp.zeros_like(small_u)
    places = [(k.h * n + k.l) * 2 + k.c, ((1 - k.h) * n + k.l) * 2 + k.c]

    tile = min(512, U)
    loaded("pre")
    loaded("down")
    for step in range(n):
        if step == 1:
            act.gather_relay()
        act.gather_wait(step)
        where = pl.ds(step * 2 * R, 2 * R)

        @pl.loop(0, U // tile)
        def _(j, where=where):
            at = pl.ds(pl.multiple_of(j * tile, tile), tile)
            d_hidden = dot(rows[where, :], wbuf[at, pl.ds(0, D)], NT)
            value = (d_hidden * gelu_slope(dp[where, at].astype(F32))).astype(BF16)
            dp[where, at] = value

    if n == 1:
        act.gather_relay()
    act.gather_end()
    loads["weights"] = [
        local.start(
            full.at[e], wbuf.at[pl.ds(0, D), pl.ds(e * width + index * half, half)]
        )
        for index, full in enumerate((full_q, full_k, full_v))
        for e in range(2)
    ]

    def mid_tile(m, index):
        at = pl.ds(pl.multiple_of(m * wide, wide), wide)
        return dot(dp[pl.ds(index * R, R), :], wu[at, :], NT)

    def mid_put(m, value):
        at = pl.ds(pl.multiple_of(m * wide, wide), wide)
        dfs[:, at] += value

    def store(count, value, target):
        def copy(i, slot):
            piece = target(i)
            a, b = piece.shape
            return pltpu.make_async_copy(
                stage.at[slot, pl.ds(0, a), pl.ds(0, b)], piece, stage_sem.at[slot]
            )

        @pl.loop(0, count)
        def _(i):
            slot = i % 2

            @pl.when(i >= 2)
            def _():
                copy(i - 2, slot).wait()

            result = value(i).astype(BF16)
            stage[slot, pl.ds(0, result.shape[0]), pl.ds(0, result.shape[1])] = result
            copy(i, slot).start()

        for i in range(max(count - 2, 0), count):
            copy(i, i % 2).wait()

    def adder(work, m, e):
        sources = work.sources(m, e)
        block = work.block(m, e)
        a, b = block.shape
        if work.inner:
            cols = min(256, half, uhalf)
            count, shape = b // cols, (a, cols)
        else:
            lines = min(256, half, uhalf)
            count, shape = a // lines, (lines, b)

        def piece(ref, i):
            if work.inner:
                return ref.at[:, pl.ds(pl.multiple_of(i * shape[1], 128), shape[1])]
            return ref.at[pl.ds(pl.multiple_of(i * shape[0], 16), shape[0]), :]

        parts = parts_inner if work.inner else parts_outer
        inputs = [block] + [work.came.at[o - 1, e] for o in sources]

        def fetch(i, slot):
            return [
                pltpu.make_async_copy(
                    piece(ref, i),
                    parts.at[slot, index, pl.ds(0, shape[0]), pl.ds(0, shape[1])],
                    part_sem.at[slot, index],
                )
                for index, ref in enumerate(inputs)
            ]

        def put(i, slot):
            return pltpu.make_async_copy(
                stage.at[slot, pl.ds(0, shape[0]), pl.ds(0, shape[1])],
                piece(block, i),
                stage_sem.at[slot],
            )

        for o in sources:
            work.flying[o, e].wait_recv()
        for copy in fetch(0, 0):
            copy.start()
        for i in range(count):
            slot = i % 2
            if i + 1 < count:
                for copy in fetch(i + 1, 1 - slot):
                    copy.start()
            for copy in fetch(i, slot):
                copy.wait()
            if i >= 2:
                put(i - 2, slot).wait()
            total = sum(
                parts[slot, index, pl.ds(0, shape[0]), pl.ds(0, shape[1])].astype(F32)
                for index in range(len(inputs))
            )
            stage[slot, pl.ds(0, shape[0]), pl.ds(0, shape[1])] = total.astype(BF16)
            put(i, slot).start()
        for i in range(max(count - 2, 0), count):
            put(i, i % 2).wait()

    def piece_order():
        return sorted(range(planes), key=lambda m: (-bin(m).count("1"), m))

    loaded("up")
    for step in range(1, n):
        act.reduce_step(step, mid_tile, mid_put)

    loaded("hidden")
    lines = min(512, U)
    for m in piece_order():
        store(
            U // lines,
            lambda i, m=m: dot(
                abuf[:, pl.ds(pl.multiple_of(i * lines, lines), lines)],
                rows[:, pl.ds(m * wide, wide)],
                TN,
            ),
            lambda i, m=m: grad_d.at[m, pl.ds(pl.multiple_of(i * lines, lines), lines), :],
        )
        down.ready(m)
    for step in range(1, n):
        pl.semaphore_signal(free_sem, inc=1, device_id=k.along(step), device_id_type=MESH)
    loads["mid"] = [local.start(mid_in, abuf.at[:, pl.ds(0, D)])]
    act.reduce_step(0, mid_tile, mid_put)
    act.reduce_end()

    ends_acc[...] = jnp.zeros_like(ends_acc)
    ends_acc[0:3, :] = sums[...]

    @pl.loop(0, R // 16)
    def _(i):
        at = pl.ds(pl.multiple_of(i * 16, 16), 16)
        grad = dfs[at, :]
        normal = normed[at, :]
        scaled = grad * gain[1:2, :]
        d_sum = inverse[at, :] * (
            scaled - mean_of(scaled) - normal * mean_of(scaled * normal)
        )
        rows[at, :] = d_sum.astype(BF16)
        dfs[at, :] = d_sum
        for index, value in enumerate((d_sum, grad * normal, grad)):
            ends_acc[3 + index : 4 + index, :] += jnp.sum(value, axis=0, keepdims=True)

    if n > 1:
        pl.semaphore_wait(free_sem, n - 1)
    act.gather_start()
    for m in range(planes):
        small_d[k.g ^ m] = ends_acc[:, m * wide : (m + 1) * wide]

    loaded("mid")
    columns = min(512, uhalf)
    per = uhalf // columns
    for m in piece_order():
        store(
            2 * per,
            lambda i, m=m: dot(
                abuf[:, pl.ds(m * wide, wide)],
                dp[:, pl.ds(pl.multiple_of(i * columns, columns), columns)],
                TN,
            ),
            lambda i, m=m: grad_u.at[
                i // per,
                pl.ds(m * wide, wide),
                pl.ds(pl.multiple_of((i % per) * columns, columns), columns),
            ],
        )
        up.ready(m)
        if m == piece_order()[0]:
            for level in down.levels():
                down.advance(adder, level)
    for e in range(2):
        value = jnp.sum(dp[:, pl.ds(e * uhalf, uhalf)].astype(F32), axis=0, keepdims=True)
        line = lax.broadcasted_iota(jnp.int32, small_u.shape, 0)
        small_u[...] = jnp.where(line == places[e], value, small_u[...])
    loads["rows"] = [local.start(rows_in, abuf.at[:, pl.ds(0, D)])]
    loaded("attention")
    for step in range(n):
        if step == 1:
            act.gather_relay()
        act.gather_wait(step)
        where = pl.ds(step * 2 * R, 2 * R)
        total = dot(rows[where, pl.ds(0, wide)], wo[0], NT)
        for m in range(1, planes):
            total = total + dot(rows[where, pl.ds(m * wide, wide)], wo[m], NT)
        d_context[where, :] = total.astype(BF16)
    if n == 1:
        act.gather_relay()
    for m in piece_order():
        store(
            1,
            lambda i, m=m: dot(context[...], rows[:, pl.ds(m * wide, wide)], TN),
            lambda i, m=m: grad_o.at[m],
        )
        outer.ready(m)
    act.gather_end()

    lane = lax.broadcasted_iota(jnp.int32, (R, HD), 1)
    per_half = half // HD

    def attend_head(head):
        at = pl.ds(pl.multiple_of(head * HD, HD), HD)
        base = (head // per_half) * width + (head % per_half) * HD
        ats = [pl.ds(pl.multiple_of(base + index * half, HD), HD) for index in range(3)]
        dk[...] = jnp.zeros_like(dk)
        dv[...] = jnp.zeros_like(dv)

        @pl.loop(0, T)
        def _(piece):
            where = pl.ds(pl.multiple_of(piece * R, R), R)
            queries, keys, values = qkv[0, where, at], qkv[1, :, at], qkv[2, :, at]
            grads = d_context[where, at]
            scores = dot(queries, keys, NT) * HD ** (-0.5)
            same = label_column[where, :] == label_row[...]
            log_total = jnp.sum(jnp.where(lane == head, lse[where, :], 0.0), axis=-1, keepdims=True)
            probs = jnp.exp(jnp.where(same, scores, NEG) - log_total)
            d_probs = dot(grads, values, NT)
            inner_sum = jnp.sum(probs * d_probs, axis=-1, keepdims=True)
            d_scores = (probs * (d_probs - inner_sum)).astype(BF16)
            dqkv[where, ats[0]] = (dot(d_scores, keys) * HD ** (-0.5)).astype(BF16)
            dk[...] += dot(d_scores, queries, TN)
            dv[...] += dot(probs.astype(BF16), grads, TN)

        dqkv[:, ats[1]] = (dk[...] * HD ** (-0.5)).astype(BF16)
        dqkv[:, ats[2]] = dv[...].astype(BF16)

    count = C // HD

    @pl.loop(0, count // 2)
    def _(head):
        attend_head(head)

    for level in up.levels():
        up.advance(adder, level)
    for level in outer.levels():
        outer.advance(adder, level)

    @pl.loop(count // 2, count)
    def _(head):
        attend_head(head)

    down.finish(adder)
    loaded("rows")
    loaded("weights")

    def rows_tile(m, index):
        at = pl.ds(pl.multiple_of(m * wide, wide), wide)
        return dot(dqkv[pl.ds(index * R, R), :], wbuf[at, pl.ds(0, 2 * width)], NT)

    def rows_put(m, value):
        at = pl.ds(pl.multiple_of(m * wide, wide), wide)
        rows[pl.ds(0, R), at] = (value + dfs[:, at]).astype(BF16)

    for step in range(1, n):
        act.reduce_step(step, rows_tile, rows_put)
    for m in piece_order():
        store(
            6,
            lambda i, m=m: dot(
                abuf[:, pl.ds(m * wide, wide)],
                dqkv[:, pl.ds(pl.multiple_of(i * half, half), half)],
                TN,
            ),
            lambda i, m=m: grad_x.at[
                i // 3, pl.ds(m * wide, wide), pl.ds(pl.multiple_of((i % 3) * half, half), half)
            ],
        )
        inner.ready(m)
    for e in range(2):
        for index, part in enumerate((0, 2)):
            at = pl.ds(e * width + part * half, half)
            value = jnp.sum(dqkv[:, at].astype(F32), axis=0, keepdims=True)
            to = pl.ds(index * half, half)
            line = lax.broadcasted_iota(jnp.int32, (2 * T, half), 0)
            small_q[:, to] = jnp.where(line == places[e], value, small_q[:, to])
    act.reduce_step(0, rows_tile, rows_put)
    act.reduce_end()
    input_done = trade(rows.at[pl.ds(0, R), :], input_grad)

    smalls = ((small_d, got_d), (small_q, got_q), (small_u, got_u))
    rounds = [[k.along(step) for step in range(1, n)]] if n > 1 else []
    rounds += [[k.mate()], [k.across()]]
    mask = 1
    while mask < planes:
        rounds.append([k.plane(mask)])
        mask *= 2
    small_slot = k.slots(3 * (n + 1 + planes))
    turn = [0]

    def small_round():
        if not rounds:
            return
        copies = []
        for peer in rounds.pop(0):
            group = []
            for index, (mine, other) in enumerate(smalls):
                copy = k.copy(small_slot + 3 * turn[0] + index, mine, other.at[turn[0]], peer)
                copy.start()
                group.append((copy, mine, other.at[turn[0]]))
            turn[0] += 1
            copies += group
        for copy, mine, other in copies:
            copy.wait()
        for copy, mine, other in copies:
            mine[...] += other[...]

    small_round()
    for level in inner.levels():
        inner.advance(adder, level)
    small_round()
    up.finish(adder)
    small_round()
    outer.finish(adder)
    while rounds:
        small_round()
    inner.finish(adder)
    homes = [
        local.start(work.home(0, k.c), work.last.at[0]) for work in (down, up, outer, inner)
    ]
    layer_done()
    input_done()
    for work in (down, up, outer, inner):
        work.arrive()
    for copy in homes:
        copy.wait()
    for copy in k.sent:
        copy.wait_send()


def backward(size, arrays):
    R, D, L, T = size.rows, size.dim, size.length, size.tp
    P_, n, wide, half, uhalf = size.planes, size.n, size.wide, size.half, size.uhalf
    C, U, fine = size.heads, size.units, size.fine
    width = 3 * half
    bits = P_.bit_length() - 1
    rounds = 2 + bits + n - 1
    shape = jax.ShapeDtypeStruct
    m = max(P_ - 1, 1)
    outs = [
        shape((R, D), BF16),
        shape((R, D), BF16),
        shape((P_, U, wide), BF16),
        shape((2, D, uhalf), BF16),
        shape((P_, C, wide), BF16),
        shape((2, D, width), BF16),
        shape((m, 2, uhalf, wide), BF16),
        shape((m, 2, wide, uhalf), BF16),
        shape((m, 2, half, wide), BF16),
        shape((m, 2, wide, width), BF16),
        shape((4, uhalf, fine), BF16),
        shape((4, fine, uhalf), BF16),
        shape((4, half, fine), BF16),
        shape((4, fine, width), BF16),
    ]
    smalls = [
        shape((P_, 8, wide), F32),
        shape((2 * T, 2 * half), F32),
        shape((2 * T, uhalf), F32),
    ]
    anywhere = pl.BlockSpec(memory_space=pl.ANY)
    vmem = pl.BlockSpec(memory_space=pltpu.VMEM)
    tall, broad = max(U, D), max(D, 2 * width)
    slots = 2 * n + 2 * n * P_ + 4 * (2 * P_ + 1) + 2 * P_ + 3 * (n + 1 + P_)
    far = max(n - 1, 1) * P_
    tile = (max(min(512, U), wide, C), max(wide, min(512, uhalf), half))
    scratch = [
        pltpu.VMEM((L, D), BF16),
        pltpu.VMEM((tall, broad), BF16),
        pltpu.VMEM((D, U), BF16),
        pltpu.VMEM((P_, C, wide), BF16),
        pltpu.VMEM((L, max(U, D)), BF16),
        pltpu.VMEM((L, U), BF16),
        pltpu.VMEM((3, L, C), BF16),
        pltpu.VMEM((L, 3 * C), BF16),
        pltpu.VMEM((L, C), BF16),
        pltpu.VMEM((L, C), BF16),
        pltpu.VMEM((L, HD), F32),
        pltpu.VMEM((P_, R, wide), BF16),
        pltpu.VMEM((n * P_, R, wide), BF16),
        pltpu.VMEM((far, R, wide), BF16),
        pltpu.VMEM((far, R, wide), BF16),
        pltpu.VMEM((R, D), F32),
        pltpu.VMEM((L, HD), F32),
        pltpu.VMEM((L, HD), F32),
        pltpu.VMEM((2,) + tile, BF16),
        pltpu.VMEM((2, bits + 1, wide, min(256, half, uhalf)), BF16),
        pltpu.VMEM((2, bits + 1, min(256, half, uhalf), wide), BF16),
        pltpu.VMEM((rounds, P_, 8, wide), F32),
        pltpu.VMEM((rounds, 2 * T, 2 * half), F32),
        pltpu.VMEM((rounds, 2 * T, uhalf), F32),
        pltpu.VMEM((8, D), F32),
        pltpu.VMEM((8, D), F32),
        pltpu.SemaphoreType.DMA((slots,)),
        pltpu.SemaphoreType.DMA((slots,)),
        pltpu.SemaphoreType.DMA((32 + 3 * P_,)),
        pltpu.SemaphoreType.DMA((2,)),
        pltpu.SemaphoreType.DMA((2, bits + 1)),
        pltpu.SemaphoreType.REGULAR,
    ]
    return pl.pallas_call(
        functools.partial(backward_kernel, size),
        out_shape=outs + smalls,
        in_specs=[anywhere] * 13 + [vmem, vmem, anywhere, anywhere] + [vmem] * 4,
        out_specs=[anywhere] * 14 + [vmem] * 3,
        scratch_shapes=scratch,
        compiler_params=pltpu.CompilerParams(
            collective_id=1, has_side_effects=True, vmem_limit_bytes=VMEM
        ),
        name="backward",
    )(*arrays)


def shards(
    fsdp,
    tp,
    inputs,
    query_weight,
    query_bias,
    key_weight,
    value_weight,
    value_bias,
    output_weight,
    output_bias,
    first_gain,
    first_shift,
    up_weight,
    up_bias,
    down_weight,
    down_bias,
    second_gain,
    second_shift,
    segments,
    cotangent,
):
    size = Sizes(fsdp, tp, inputs, query_weight, up_weight, segments)
    f, t = lax.axis_index("fsdp"), lax.axis_index("tp")
    c = f % 2
    residual = jnp.stack(
        [output_bias, first_gain, first_shift, down_bias, second_gain, second_shift]
        + [output_bias] * 2
    )
    residual = residual.reshape(8, size.planes, size.wide).transpose(1, 0, 2)
    role_bias = jnp.concatenate(
        [v.reshape(2, -1) for v in (query_bias, value_bias, up_bias)], axis=1
    )[:, None]
    kept = forward(
        size,
        (
            inputs,
            cotangent,
            segments.reshape(tp, 1, size.rows),
            segments.reshape(size.length, 1),
            role_bias,
            residual,
            query_weight,
            key_weight,
            value_weight,
            output_weight,
            up_weight,
            down_weight,
        ),
    )
    results = backward(size, tuple(kept) + (residual,))
    layer_out, input_grad = results[:2]
    last_d, last_u, last_o, last_x, small_d, small_q, small_u = results[10:]

    def owned(last, axis):
        mine = last[0].astype(F32) + last[2].astype(F32)
        other = last[1].astype(F32) + last[3].astype(F32)
        return jnp.where(
            c == 0,
            jnp.concatenate([mine, other], axis=axis),
            jnp.concatenate([other, mine], axis=axis),
        )

    half = size.half
    inner = [owned(last_x[:, :, i * half : (i + 1) * half], 1) for i in range(3)]
    small_d = small_d.transpose(1, 0, 2).reshape(8, size.dim)
    residual_size = size.dim // (fsdp * tp)
    ends = lax.dynamic_slice(small_d, (0, (f * tp + t) * residual_size), (8, residual_size))

    def split(table):
        row = lax.dynamic_slice_in_dim(table, 2 * t, 2).reshape(1, -1)
        part = row.shape[1] // fsdp
        return lax.dynamic_slice_in_dim(row, f * part, part, axis=1)

    return (
        layer_out,
        input_grad,
        inner[0],
        split(small_q[:, :half]),
        inner[1],
        inner[2],
        split(small_q[:, half:]),
        owned(last_o, 0),
        ends[3],
        ends[4],
        ends[5],
        owned(last_u, 1),
        split(small_u),
        owned(last_d, 0),
        ends[0],
        ends[1],
        ends[2],
    )


def solution(mesh):
    fsdp, tp = mesh.shape["fsdp"], mesh.shape["tp"]

    def body(*arrays):
        return shards(fsdp, tp, *arrays)

    tokens, inner, outer = P(AXES, None), P("fsdp", "tp"), P("tp", "fsdp")
    placed = (
        tokens,
        inner,
        P("tp"),
        inner,
        inner,
        P("tp"),
        outer,
        P(),
        P(),
        P(),
        inner,
        P("tp"),
        outer,
        P(),
        P(),
        P(),
        P("fsdp", None),
        tokens,
    )
    return jax.shard_map(
        body,
        mesh=mesh,
        in_specs=placed,
        out_specs=(
            tokens,
            tokens,
            inner,
            outer,
            inner,
            inner,
            outer,
            outer,
            P(AXES),
            P(AXES),
            P(AXES),
            inner,
            outer,
            outer,
            P(AXES),
            P(AXES),
            P(AXES),
        ),
        check_vma=False,
    )
```

```python
import functools

import jax
import jax.numpy as jnp
from jax import lax
from jax.experimental import pallas as pl
from jax.experimental.pallas import tpu as pltpu
from jax.sharding import PartitionSpec as P

HD = 128
EPS = 1e-06
NEG = -1000000000.0
AXES = ("fsdp", "tp")
F32 = jnp.float32
BF16 = jnp.bfloat16
MESH = pl.DeviceIdType.MESH
VMEM = 62 * 2**20


def gelu_tanh(values):
    return jax.nn.gelu(values, approximate=True)


def dot(left, right, dims=((1,), (0,))):
    return lax.dot_general(left, right, (dims, ((), ())), preferred_element_type=F32)


NN, NT, TN = ((1,), (0,)), ((1,), (1,)), ((0,), (0,))


class Sizes:
    def __init__(self, fsdp, tp, inputs, query_weight, up_weight, segments):
        self.fsdp, self.tp = fsdp, tp
        self.planes, self.n = fsdp // 2, tp // 2
        self.rows, self.dim = inputs.shape
        self.length = segments.shape[1]
        self.fine = query_weight.shape[0]
        self.wide = 2 * self.fine
        self.heads = query_weight.shape[1]
        self.half = self.heads // 2
        self.units = up_weight.shape[1]
        self.uhalf = self.units // 2


INNER = (True, True, True, False, True, False)


class Links:
    def __init__(self, size, send, recv):
        self.size, self.send, self.recv = size, send, recv
        f, t = lax.axis_index("fsdp"), lax.axis_index("tp")
        self.g, self.c = f // 2, f % 2
        self.h, self.l = t // size.n, t % size.n
        self.done = set()
        self.sent = []
        self.next = 0

    def device(self, g, c, h, l):
        return (g * 2 + c, h * self.size.n + l)

    def mate(self):
        return self.device(self.g, 1 - self.c, self.h, self.l)

    def across(self):
        return self.device(self.g, self.c, 1 - self.h, self.l)

    def corner(self):
        return self.device(self.g, 1 - self.c, 1 - self.h, self.l)

    def plane(self, mask):
        return self.device(self.g ^ mask, self.c, self.h, self.l)

    def along(self, step):
        return self.device(self.g, self.c, self.h, (self.l + step) % self.size.n)

    def barrier(self):
        size = self.size
        peers = [self.mate(), self.across(), self.corner()]
        mask = 1
        while mask < size.planes:
            peers.append(self.plane(mask))
            mask *= 2
        peers += [self.along(step) for step in range(1, size.n)]
        semaphore = pltpu.get_barrier_semaphore()
        for peer in peers:
            pl.semaphore_signal(semaphore, inc=1, device_id=peer, device_id_type=MESH)
        pl.semaphore_wait(semaphore, len(peers))

    def slots(self, count=1):
        first = self.next
        self.next += count
        return first

    def copy(self, slot, source, target, device):
        return pltpu.make_async_remote_copy(
            src_ref=source,
            dst_ref=target,
            send_sem=self.send.at[slot],
            recv_sem=self.recv.at[slot],
            device_id=device,
            device_id_type=MESH,
        )

    def go(self, slot, source, target, device):
        copy = self.copy(slot, source, target, device)
        copy.start()
        self.sent.append(copy)
        return copy


class Local:
    def __init__(self, semaphores):
        self.semaphores, self.next = semaphores, 0

    def start(self, source, target):
        copy = pltpu.make_async_copy(source, target, self.semaphores.at[self.next])
        self.next += 1
        copy.start()
        return copy


class Spread:
    def __init__(self, links, local, shard, full, inner, hold):
        self.links, self.local, self.hold = links, local, hold
        self.shard, self.full, self.inner = shard, full, inner
        self.base = links.slots(3 + 2 * (links.size.planes - 1))
        self.waited = set()

    def part(self, index):
        axis = 1 if self.inner else 0
        width = self.shard.shape[axis] // 2
        at = pl.multiple_of(index * width, width)
        return self.shard.at[:, pl.ds(at, width)] if self.inner else self.shard.at[pl.ds(at, width)]

    def home(self, e, c):
        fine = self.links.size.fine
        at = pl.ds(pl.multiple_of(c * fine, fine), fine)
        if self.inner:
            return self.full.at[e, at, :]
        width = self.full.shape[1] // 2
        return self.full.at[0, pl.ds(e * width, width), at]

    def block(self, m, e=None):
        wide = self.links.size.wide
        if self.inner:
            at = pl.ds(m * wide, wide)
            return self.full.at[:, at, :] if e is None else self.full.at[e, at, :]
        width = self.full.shape[1] // 2
        return self.full.at[m] if e is None else self.full.at[m, pl.ds(e * width, width)]

    def near(self):
        k = self.links
        self.own = self.local.start(self.part(k.c), self.hold)
        self.steps = [k.go(self.base, self.part(1 - k.c), self.home(0, k.c), k.mate())]
        self.pieces = {}

    def keep(self):
        self.own.wait()
        self.own = self.local.start(self.hold, self.home(0, self.links.c))

    def far(self):
        k = self.links
        self.steps += [
            k.go(self.base + 1, self.part(k.c), self.home(1, k.c), k.across()),
            k.go(self.base + 2, self.part(1 - k.c), self.home(1, k.c), k.corner()),
        ]

    def plane(self, e):
        k = self.links
        if e == 0:
            self.own.wait()
            self.steps[0].wait_recv()
        else:
            self.steps[1].wait_recv()
            self.steps[2].wait_recv()
        mask = 1
        while mask < k.size.planes:
            self.pieces[mask, e] = k.go(
                self.base + 1 + 2 * mask + e, self.block(0, e), self.block(mask, e), k.plane(mask)
            )
            mask *= 2

    def arrive(self, m, e):
        if m and (m, e) not in self.waited:
            self.waited.add((m, e))
            self.pieces[m, e].wait_recv()

    def relay(self, e):
        k = self.links
        for m in sorted(range(1, k.size.planes), key=lambda v: bin(v).count("1")):
            if bin(m).count("1") > 1:
                bit = m & -m if e else 1 << (m.bit_length() - 1)
                self.arrive(m ^ bit, e)
                self.pieces[m, e] = k.go(
                    self.base + 1 + 2 * m + e,
                    self.block(m ^ bit, e),
                    self.block(m, e),
                    k.plane(bit),
                )

    def finish(self):
        for m in range(1, self.links.size.planes):
            for e in range(2):
                self.arrive(m, e)


class Activations:
    def __init__(self, links, rows, give, take, out, came):
        self.links, self.rows = links, rows
        self.give, self.take, self.out, self.came = give, take, out, came
        size = links.size
        self.gather_slots = links.slots(2 * size.n)
        self.mate_slots = links.slots(size.n * size.planes)
        self.along_slots = links.slots(size.n * size.planes)

    def piece(self, index):
        size = self.links.size
        return self.rows.at[pl.ds(index * size.rows, size.rows)]

    def gather_start(self):
        k, base = self.links, self.gather_slots
        self.far = [
            k.go(base + step, self.piece(0), self.piece(2 * step), k.along(step))
            for step in range(1, k.size.n)
        ]
        self.near = [k.go(base + k.size.n, self.piece(0), self.piece(1), k.mate())]

    def gather_relay(self):
        k, base = self.links, self.gather_slots
        for step in range(1, k.size.n):
            self.far[step - 1].wait_recv()
            self.near.append(
                k.go(
                    base + k.size.n + step,
                    self.piece(2 * step),
                    self.piece(2 * step + 1),
                    k.mate(),
                )
            )

    def gather_wait(self, step):
        self.near[step].wait_recv()

    def gather_end(self):
        over = self.far + self.near
        for copy in over:
            copy.wait_send()
        self.links.sent = [c for c in self.links.sent if all(c is not o for o in over)]

    def near_copy(self, step, m):
        k = self.links
        at = step * k.size.planes + m
        return k.copy(self.mate_slots + at, self.give.at[m], self.take.at[at], k.mate())

    def far_copy(self, step, m):
        k = self.links
        at = (step - 1) * k.size.planes + m
        return k.copy(self.along_slots + at, self.out.at[at], self.came.at[at], k.along(step))

    def reduce_near(self, step, tile, low, high):
        n = self.links.size.n
        index = 2 * ((n - step) % n)

        @pl.loop(low, high)
        def _(m):
            value = tile(m, index + 1).astype(BF16)
            if step != 1 and n > 1:
                self.near_copy(step - 1 if step else n - 1, m).wait_send()
            self.give[m] = value
            self.near_copy(step, m).start()

    def reduce_far(self, step, tile, low, high):
        planes, n = self.links.size.planes, self.links.size.n
        index = 2 * ((n - step) % n)

        @pl.loop(low, high)
        def _(m):
            total = tile(m, index)
            self.near_copy(step, m).wait_recv()
            total = total + self.take[step * planes + m].astype(F32)
            self.out[(step - 1) * planes + m] = total.astype(BF16)
            self.far_copy(step, m).start()

    def reduce_begin(self, tile, low, high):
        for step in range(1, self.links.size.n):
            self.reduce_near(step, tile, low, high)
            self.reduce_far(step, tile, low, high)
        self.reduce_near(0, tile, low, high)

    def reduce_finish(self, base, put):
        planes, n = self.links.size.planes, self.links.size.n

        @pl.loop(0, planes)
        def _(m):
            total = base(m)
            self.near_copy(0, m).wait_recv()
            total = total + self.take[m].astype(F32)
            for other in range(1, n):
                self.far_copy(other, m).wait_recv()
                total = total + self.came[(other - 1) * planes + m].astype(F32)
            put(m, total)

        @pl.loop(0, planes)
        def _(m):
            self.near_copy(0, m).wait_send()
            for step in range(1, n):
                self.far_copy(step, m).wait_send()


def mean_of(value):
    return jnp.mean(value, axis=-1, keepdims=True)


def forward_kernel(size, *refs):
    (
        inputs,
        cotangent,
        label_row,
        label_column,
        role_bias,
        residual,
        *shards_,
    ) = refs[:12]
    (
        fulls_q,
        fulls_k,
        fulls_v,
        fulls_o,
        fulls_u,
        fulls_d,
        rows_out,
        qkv_out,
        context_out,
        lse_out,
        mid_out,
        pre_out,
        hidden_out,
        normed_out,
        inverse_out,
        final_out,
        d_second_out,
        sums_out,
        label_row_out,
        label_column_out,
    ) = refs[12:32]
    (
        rows,
        wq,
        qkv,
        context,
        lse,
        wo,
        wu,
        wd,
        hidden,
        pre,
        give,
        take,
        out,
        came,
        cot,
        labels_r,
        labels_c,
        bias,
        vectors,
        send,
        recv,
        near_sem,
        *holds,
    ) = refs[32:]
    k = Links(size, send, recv)
    local = Local(near_sem)
    R, D, L, wide, half, uhalf = (
        size.rows,
        size.dim,
        size.length,
        size.wide,
        size.half,
        size.uhalf,
    )
    planes, n = size.planes, size.n
    k.barrier()
    stay = k.c == k.h

    fulls = (fulls_q, fulls_k, fulls_v, fulls_o, fulls_u, fulls_d)
    spread = [
        Spread(k, local, shard, full, inner, hold)
        for shard, full, inner, hold in zip(shards_, fulls, INNER, holds)
    ]
    act = Activations(k, rows, give, take, out, came)

    def trade(source, target):
        base = k.slots(planes)
        first_local = local.next
        local.next += planes

        def pieces(m):
            at = pl.multiple_of((k.g ^ m) * wide, wide)
            return source.at[:, pl.ds(at, wide)], target(m)

        @pl.when(stay)
        def _():
            for m in range(planes):
                a, b = pieces(m)
                pltpu.make_async_copy(a, b, near_sem.at[first_local + m]).start()

        @pl.when(jnp.logical_not(stay))
        def _():
            for m in range(planes):
                a, b = pieces(m)
                k.copy(base + m, a, b, k.corner()).start()

        def wait():
            @pl.when(stay)
            def _():
                for m in range(planes):
                    a, b = pieces(m)
                    pltpu.make_async_copy(a, b, near_sem.at[first_local + m]).wait()

            @pl.when(jnp.logical_not(stay))
            def _():
                for m in range(planes):
                    a, b = pieces(m)
                    k.copy(base + m, a, b, k.corner()).wait()

        return wait

    for index in range(3):
        spread[index].near()
    spread[0].far()
    spread[1].far()
    for index in range(3, 6):
        spread[index].near()
    for index in range(6):
        spread[index].keep()
    for index in range(3):
        spread[index].plane(0)
    rows_ready = trade(inputs, lambda m: rows.at[pl.ds(0, R), pl.ds(m * wide, wide)])

    label_slots = k.slots(2)
    label_pairs = ((label_row, labels_r), (label_column, labels_c))

    @pl.when(stay)
    def _():
        for index, (a, b) in enumerate(label_pairs):
            k.copy(label_slots + index, a, b, k.mate()).start()

    label_local = local.next
    local.next += 2

    @pl.when(stay)
    def _():
        for index, (a, b) in enumerate(label_pairs):
            pltpu.make_async_copy(a, b, near_sem.at[label_local + index]).start()

    bias_slot = k.slots()
    bias_copy = k.go(bias_slot, role_bias.at[k.c], bias.at[1], k.across())
    bias_local = local.start(role_bias.at[k.c], bias.at[0])

    for m in range(planes):
        vectors[:, pl.ds(m * wide, wide)] = residual[k.g ^ m]

    saved = []
    loads = {}

    def load(index, buffer):
        spread[index].finish()
        loads[index] = local.start(fulls[index], buffer)

    spread[0].plane(1)
    spread[2].far()
    for index in range(3):
        spread[index].relay(0)
    spread[1].plane(1)
    spread[3].far()
    spread[0].relay(1)
    rows_ready()
    act.gather_start()
    spread[2].plane(1)
    spread[4].far()
    spread[1].relay(1)
    spread[3].plane(0)
    act.gather_relay()
    spread[2].relay(1)
    spread[3].plane(1)
    spread[4].plane(0)
    for step in range(n):
        act.gather_wait(step)
    saved.append(local.start(rows, rows_out))
    bias_copy.wait_recv()
    bias_local.wait()

    @pl.when(stay)
    def _():
        for index, (a, b) in enumerate(label_pairs):
            pltpu.make_async_copy(a, b, near_sem.at[label_local + index]).wait()
            k.copy(label_slots + index, a, b, k.mate()).wait_send()

    @pl.when(jnp.logical_not(stay))
    def _():
        for index, (a, b) in enumerate(label_pairs):
            k.copy(label_slots + index, a, b, k.mate()).wait_recv()

    load(0, wq.at[0])
    load(1, wq.at[1])
    for index in range(3):
        loads[index].wait()
        for e in range(2):
            result = dot(rows[...], wq[index % 2, e])
            if index != 1:
                at = 0 if index == 0 else half
                result = result + bias[e, :, pl.ds(at, half)]
            qkv[index, :, pl.ds(e * half, half)] = result.astype(BF16)
        if index == 0:
            load(2, wq.at[0])
    saved.append(local.start(qkv, qkv_out))
    act.gather_end()

    spread[3].relay(0)
    spread[3].relay(1)
    order = []
    for step in range(n):
        for core in (k.c, 1 - k.c):
            order.append(core * n + (k.l + n - step) % n)
    row = jnp.concatenate([labels_r[q] for q in order], axis=-1)
    label_row_out[...] = row
    for piece, q in enumerate(order):
        column = labels_c[pl.ds(pl.multiple_of(q * R, R), R), :]
        label_column_out[pl.ds(piece * R, R), :] = column
        same = column == row

        lane = lax.broadcasted_iota(jnp.int32, (R, HD), 1)
        where = pl.ds(piece * R, R)

        def one(head, kept, where=where, same=same):
            at = pl.ds(pl.multiple_of(head * HD, HD), HD)
            scores = dot(qkv[0, where, at], qkv[1, :, at], NT) * HD ** (-0.5)
            scores = jnp.where(same, scores, NEG)
            top = jnp.max(scores, axis=-1, keepdims=True)
            weights = jnp.exp(scores - top)
            summed = jnp.sum(weights, axis=-1, keepdims=True)
            probs = (weights * (1.0 / summed)).astype(BF16)
            context[where, at] = dot(probs, qkv[2, :, at]).astype(BF16)
            return jnp.where(lane == head, top + jnp.log(summed), kept)

        lse[where, :] = lax.fori_loop(0, size.heads // HD, one, jnp.zeros((R, HD), F32))
        if piece == size.tp // 2 - 1:
            spread[4].relay(0)
            spread[5].plane(0)

    saved.append(local.start(context, context_out))
    saved.append(local.start(lse, lse_out))

    load(3, wo)
    loads[3].wait()

    def attn_tile(m, index):
        return dot(context[pl.ds(index * R, R), :], wo[m])

    def attn_put(m, value):
        at = pl.ds(pl.multiple_of(m * wide, wide), wide)
        normed_out[:, at] = value + rows[pl.ds(0, R), at].astype(F32) + vectors[0:1, at]

    saved[0].wait()
    act.reduce_begin(attn_tile, 0, planes)
    spread[4].plane(1)
    spread[5].far()
    act.reduce_finish(lambda m: attn_tile(m, 0), attn_put)

    @pl.loop(0, R // 16)
    def _(i):
        at = pl.ds(pl.multiple_of(i * 16, 16), 16)
        summed = normed_out[at, :]
        center = summed - mean_of(summed)
        scale = lax.rsqrt(mean_of(center * center) + EPS)
        normed = center * scale
        normed_out[at, :] = normed
        inverse_out[at, :] = scale
        rows[at, :] = (normed * vectors[1:2, :] + vectors[2:3, :]).astype(BF16)

    act.gather_start()
    spread[4].relay(1)
    spread[5].relay(0)
    act.gather_relay()
    load(4, wu)
    loads[4].wait()
    tile = min(512, uhalf)
    for step in range(n):
        act.gather_wait(step)
        if step == n - 1:
            spread[5].plane(1)
            cot_ready = trade(cotangent, lambda m: cot.at[:, pl.ds(m * wide, wide)])
        where = pl.ds(step * 2 * R, 2 * R)
        for e in range(2):

            @pl.loop(0, uhalf // tile)
            def _(j, e=e, where=where):
                at = pl.ds(pl.multiple_of(j * tile, tile), tile)
                to = pl.ds(pl.multiple_of(e * uhalf + j * tile, tile), tile)
                skip = pl.ds(pl.multiple_of(2 * half + j * tile, 128), tile)
                value = dot(rows[where, :], wu[e, :, at]) + bias[e, :, skip]
                pre[where, to] = value.astype(BF16)
                hidden[where, to] = gelu_tanh(value).astype(BF16)

    saved.append(local.start(rows, mid_out))
    saved.append(local.start(pre, pre_out))
    saved.append(local.start(hidden, hidden_out))
    act.gather_end()

    def ffn_tile(m, index):
        return dot(hidden[pl.ds(index * R, R), :], wd[m])

    def ffn_put(m, value):
        at = pl.ds(pl.multiple_of(m * wide, wide), wide)
        first = normed_out[:, at] * vectors[1:2, at] + vectors[2:3, at]
        d_second_out[:, at] = value + first + vectors[3:4, at]

    counts = [bin(m).count("1") for m in range(planes)]
    low = 0
    while low < planes:
        high = low + 1
        while high < planes and (counts[high] > 1) == (counts[low] > 1) and low:
            high += 1
        if low == 1:
            spread[5].relay(1)
        pieces = []
        for m in range(low, high):
            spread[5].arrive(m, 0)
            spread[5].arrive(m, 1)
            pieces.append(local.start(fulls[5].at[m], wd.at[m]))
        for piece in pieces:
            piece.wait()
        act.reduce_begin(ffn_tile, low, high)
        low = high
    act.reduce_finish(lambda m: ffn_tile(m, 0), ffn_put)
    cot_ready()
    sums_out[...] = jnp.zeros_like(sums_out)

    @pl.loop(0, R // 16)
    def _(i):
        at = pl.ds(pl.multiple_of(i * 16, 16), 16)
        summed = d_second_out[at, :]
        center = summed - mean_of(summed)
        scale = lax.rsqrt(mean_of(center * center) + EPS)
        normed = center * scale
        final_out[at, :] = (normed * vectors[4:5, :] + vectors[5:6, :]).astype(BF16)
        grad = cot[at, :].astype(F32)
        scaled = grad * vectors[4:5, :]
        d_second = scale * (scaled - mean_of(scaled) - normed * mean_of(scaled * normed))
        d_second_out[at, :] = d_second
        for index, value in enumerate((d_second, grad * normed, grad)):
            sums_out[index : index + 1, :] += jnp.sum(value, axis=0, keepdims=True)

    for copy in saved[1:]:
        copy.wait()
    for copy in k.sent:
        copy.wait_send()


def forward(size, arrays):
    R, D, L, T = size.rows, size.dim, size.length, size.tp
    P_, n, wide, half, uhalf = size.planes, size.n, size.wide, size.half, size.uhalf
    C, U = size.heads, size.units
    whole = [jax.ShapeDtypeStruct((2, D, half), BF16)] * 3 + [
        jax.ShapeDtypeStruct((P_, C, wide), BF16),
        jax.ShapeDtypeStruct((2, D, uhalf), BF16),
        jax.ShapeDtypeStruct((P_, U, wide), BF16),
    ]
    kept = [
        jax.ShapeDtypeStruct((L, D), BF16),
        jax.ShapeDtypeStruct((3, L, C), BF16),
        jax.ShapeDtypeStruct((L, C), BF16),
        jax.ShapeDtypeStruct((L, HD), F32),
        jax.ShapeDtypeStruct((L, D), BF16),
        jax.ShapeDtypeStruct((L, U), BF16),
        jax.ShapeDtypeStruct((L, U), BF16),
    ]
    ends = [
        jax.ShapeDtypeStruct((R, D), F32),
        jax.ShapeDtypeStruct((R, 1), F32),
        jax.ShapeDtypeStruct((R, D), BF16),
        jax.ShapeDtypeStruct((R, D), F32),
        jax.ShapeDtypeStruct((3, D), F32),
        jax.ShapeDtypeStruct((1, L), jnp.int32),
        jax.ShapeDtypeStruct((L, 1), jnp.int32),
    ]
    anywhere = pl.BlockSpec(memory_space=pl.ANY)
    vmem = pl.BlockSpec(memory_space=pltpu.VMEM)
    width = 2 * half + uhalf
    slots = 6 * (3 + 2 * (P_ - 1)) + 2 * P_ + 3 + 2 * n + 2 * n * P_
    scratch = [
        pltpu.VMEM((L, D), BF16),
        pltpu.VMEM((2, 2, D, half), BF16),
        pltpu.VMEM((3, L, C), BF16),
        pltpu.VMEM((L, C), BF16),
        pltpu.VMEM((L, HD), F32),
        pltpu.VMEM((P_, C, wide), BF16),
        pltpu.VMEM((2, D, uhalf), BF16),
        pltpu.VMEM((P_, U, wide), BF16),
        pltpu.VMEM((L, U), BF16),
        pltpu.VMEM((L, U), BF16),
        pltpu.VMEM((P_, R, wide), BF16),
        pltpu.VMEM((n * P_, R, wide), BF16),
        pltpu.VMEM((max(n - 1, 1) * P_, R, wide), BF16),
        pltpu.VMEM((max(n - 1, 1) * P_, R, wide), BF16),
        pltpu.VMEM((R, D), BF16),
        pltpu.VMEM((T, 1, R), jnp.int32),
        pltpu.VMEM((L, 1), jnp.int32),
        pltpu.VMEM((2, 1, width), F32),
        pltpu.VMEM((8, D), F32),
        pltpu.SemaphoreType.DMA((slots,)),
        pltpu.SemaphoreType.DMA((slots,)),
        pltpu.SemaphoreType.DMA((32 + 2 * P_,)),
        *[pltpu.VMEM((size.fine, half), BF16)] * 3,
        pltpu.VMEM((half, size.fine), BF16),
        pltpu.VMEM((size.fine, uhalf), BF16),
        pltpu.VMEM((uhalf, size.fine), BF16),
    ]
    return pl.pallas_call(
        functools.partial(forward_kernel, size),
        out_shape=whole + kept + ends,
        in_specs=[anywhere, anywhere, vmem, vmem, vmem, vmem] + [anywhere] * 6,
        out_specs=[anywhere] * 13 + [vmem] * 7,
        scratch_shapes=scratch,
        compiler_params=pltpu.CompilerParams(
            collective_id=0, has_side_effects=True, vmem_limit_bytes=VMEM
        ),
        name="forward",
    )(*arrays)


class Collect:
    def __init__(self, links, grad, came, last, inner):
        self.links, self.grad, self.came, self.last, self.inner = links, grad, came, last, inner
        self.planes = links.size.planes
        self.base = links.slots(2 * (self.planes - 1) + 3)
        self.flying, self.final = {}, []

    def block(self, m, e):
        wide = self.links.size.wide
        if self.inner:
            return self.grad.at[e, pl.ds(m * wide, wide), :]
        width = self.grad.shape[1] // 2
        return self.grad.at[m, pl.ds(e * width, width), :]

    def home(self, e, c):
        fine = self.links.size.fine
        at = pl.ds(pl.multiple_of(c * fine, fine), fine)
        if self.inner:
            return self.grad.at[e, at, :]
        width = self.grad.shape[1] // 2
        return self.grad.at[0, pl.ds(e * width, width), at]

    @staticmethod
    def bit(m, e):
        return m & -m if e else 1 << (m.bit_length() - 1)

    def sources(self, m, e):
        return [o for o in range(1, self.planes) if o != m and o ^ self.bit(o, e) == m]

    def send(self, m, e):
        self.flying[m, e] = self.links.go(
            self.base + 2 * (m - 1) + e,
            self.block(m, e),
            self.came.at[m - 1, e],
            self.links.plane(self.bit(m, e)),
        )

    def finish(self, e):
        k = self.links
        base = self.base + 2 * (self.planes - 1)
        if e == 0:
            self.final.append(k.go(base, self.home(0, 1 - k.c), self.last.at[0], k.mate()))
            return
        self.final += [
            k.go(base + 1, self.home(1, k.c), self.last.at[1], k.across()),
            k.go(base + 2, self.home(1, 1 - k.c), self.last.at[2], k.corner()),
        ]

    def arrive(self):
        for copy in self.final:
            copy.wait_recv()


def column_tile(width):
    for tile in (512, 384):
        if width % tile == 0:
            return tile
    return width


def gelu_slope(v):
    scale = 0.7978845608028654
    square = v * v
    t = jnp.tanh(scale * v * (1.0 + 0.044715 * square))
    return 0.5 * (1.0 + t) + 0.5 * v * (1.0 - t * t) * scale * (1.0 + 3 * 0.044715 * square)


def backward_kernel(size, *refs):
    (
        full_q,
        full_k,
        full_v,
        full_o,
        full_u,
        full_d,
        rows_in,
        qkv_in,
        context_in,
        lse_in,
        mid_in,
        pre_in,
        hidden_in,
        normed,
        inverse,
        final,
        d_second,
        sums,
        label_row,
        label_column,
        residual,
    ) = refs[:21]
    (
        layer_out,
        input_grad,
        grad_d,
        grad_u,
        grad_o,
        grad_x,
        came_d,
        came_u,
        came_o,
        came_x,
        last_d,
        last_u,
        last_o,
        last_x,
        small_d,
        small_q,
        small_u,
    ) = refs[21:38]
    (
        rows,
        wbuf,
        wbig,
        wo,
        abuf,
        dp,
        qkv,
        dqkv,
        context,
        d_context,
        lse,
        give,
        take,
        out,
        came,
        dfs,
        dk,
        dv,
        stage,
        parts,
        final_rows,
        got_d,
        got_q,
        got_u,
        gain,
        ends_acc,
        send,
        recv,
        near_sem,
        stage_sem,
        part_sem,
    ) = refs[38:]
    k = Links(size, send, recv)
    local = Local(near_sem)
    R, D, L, wide, half, uhalf, T = (
        size.rows,
        size.dim,
        size.length,
        size.wide,
        size.half,
        size.uhalf,
        size.tp,
    )
    planes, n, C, U = size.planes, size.n, size.heads, size.units
    width = 3 * half
    act = Activations(k, rows, give, take, out, came)
    down = Collect(k, grad_d, came_d, last_d, False)
    up = Collect(k, grad_u, came_u, last_u, True)
    outer = Collect(k, grad_o, came_o, last_o, False)
    inner = Collect(k, grad_x, came_x, last_x, True)
    k.barrier()
    stay = k.c == k.h

    def trade(source, target):
        base = k.slots(planes)
        first_local = local.next
        local.next += planes

        def pieces(m):
            at = pl.multiple_of((k.g ^ m) * wide, wide)
            return source.at[:, pl.ds(m * wide, wide)], target.at[:, pl.ds(at, wide)]

        def both(go):
            @pl.when(stay)
            def _():
                for m in range(planes):
                    copy = pltpu.make_async_copy(*pieces(m), near_sem.at[first_local + m])
                    copy.start() if go else copy.wait()

            @pl.when(jnp.logical_not(stay))
            def _():
                for m in range(planes):
                    copy = k.copy(base + m, *pieces(m), k.corner())
                    copy.start() if go else copy.wait()

        both(True)
        return lambda: both(False)

    loads = {}
    start = local.start(d_second, dfs)
    loads["pre"] = [local.start(pre_in, dp)]
    loads["down"] = [
        local.start(full_d.at[m], wbuf.at[pl.ds(0, U), pl.ds(m * wide, wide)])
        for m in range(planes)
    ]
    start.wait()
    rows[pl.ds(0, R), :] = dfs[...].astype(BF16)
    act.gather_start()
    loads["hidden"] = [local.start(hidden_in, abuf.at[:, pl.ds(0, U)])]
    loads["up"] = [
        local.start(full_u.at[e], wbig.at[pl.ds(0, D), pl.ds(e * uhalf, uhalf)]) for e in range(2)
    ]
    loads["final"] = [local.start(final, final_rows)]
    loads["attention"] = [
        local.start(qkv_in, qkv),
        local.start(context_in, context),
        local.start(lse_in, lse),
        local.start(full_o, wo),
    ]
    for m in range(planes):
        gain[:, pl.ds(m * wide, wide)] = residual[k.g ^ m]

    def loaded(name):
        for copy in loads[name]:
            copy.wait()

    small_d[...] = jnp.zeros_like(small_d)
    small_q[...] = jnp.zeros_like(small_q)
    small_u[...] = jnp.zeros_like(small_u)
    places = [(k.h * n + k.l) * 2 + k.c, ((1 - k.h) * n + k.l) * 2 + k.c]

    loaded("final")
    layer_done = trade(final_rows, layer_out)
    tile = min(512, U)
    loaded("pre")
    loaded("down")
    for step in range(n):
        if step == 1:
            act.gather_relay()
        act.gather_wait(step)
        where = pl.ds(step * 2 * R, 2 * R)

        @pl.loop(0, U // tile)
        def _(j, where=where):
            at = pl.ds(pl.multiple_of(j * tile, tile), tile)
            d_hidden = dot(rows[where, :], wbuf[at, pl.ds(0, D)], NT)
            value = (d_hidden * gelu_slope(dp[where, at].astype(F32))).astype(BF16)
            dp[where, at] = value

    if n == 1:
        act.gather_relay()
    act.gather_end()
    loads["weights"] = [
        local.start(
            full.at[e], wbuf.at[pl.ds(0, D), pl.ds(e * width + index * half, half)]
        )
        for index, full in enumerate((full_q, full_k, full_v))
        for e in range(2)
    ]

    def mid_tile(m, index):
        at = pl.ds(pl.multiple_of(m * wide, wide), wide)
        return dot(dp[pl.ds(index * R, R), :], wbig[at, pl.ds(0, U)], NT)

    pending = []
    turn = [0]

    def flush():
        for copies, work, m, e in pending:
            for copy in copies:
                copy.wait()
            if m:
                work.send(m, e)
        pending.clear()

    def unit(work, m, e, value, alone=False):
        block = work.block(m, e)
        a, b = block.shape
        if work.inner:
            cols = column_tile(b)
            count, shape = b // cols, (a, cols)
        else:
            lines = 512 if a % 512 == 0 else a
            count, shape = a // lines, (lines, b)

        def piece(ref, i):
            if work.inner:
                return ref.at[:, pl.ds(i * shape[1], shape[1])]
            return ref.at[pl.ds(i * shape[0], shape[0]), :]

        sources = [] if alone else work.sources(m, e)
        origins = [work.came.at[o - 1, e] for o in sources] + ([] if value else [block])

        def fetch(i):
            return [
                pltpu.make_async_copy(
                    piece(origin, i),
                    parts.at[i % 2, index, pl.ds(0, shape[0]), pl.ds(0, shape[1])],
                    part_sem.at[i % 2, index],
                )
                for index, origin in enumerate(origins)
            ]

        for o in sources:
            work.flying[o, e].wait_recv()
        for i in range(min(count, 2)):
            for copy in fetch(i):
                copy.start()
        copies = []
        for i in range(count):
            result = value(m, e, i, shape) if value else 0.0
            for index, copy in enumerate(fetch(i)):
                copy.wait()
                result = result + parts[
                    i % 2, index, pl.ds(0, shape[0]), pl.ds(0, shape[1])
                ].astype(F32)
            if i + 2 < count:
                for copy in fetch(i + 2):
                    copy.start()
            if i == 0:
                flush()
            slot = turn[0] % 2
            turn[0] += 1
            if len(copies) > 1:
                copies.pop(0).wait()
            stage[slot, pl.ds(0, shape[0]), pl.ds(0, shape[1])] = result.astype(BF16)
            copy = pltpu.make_async_copy(
                stage.at[slot, pl.ds(0, shape[0]), pl.ds(0, shape[1])],
                piece(block, i),
                stage_sem.at[slot],
            )
            copy.start()
            copies.append(copy)
        pending.append((copies, work, m, e))

    def units(work, pairs, value, alone=False):
        for m, e in pairs:
            unit(work, m, e, value, alone)

    def close(work, value):
        for e in (1, 0):
            unit(work, 0, e, value)
            flush()
            work.finish(e)

    def down_value(m, e, i, shape):
        at = pl.ds(e * uhalf + i * shape[0], shape[0])
        return dot(hidden_ref[0][:, at], rows[:, pl.ds(m * wide, wide)], TN)

    def up_value(m, e, i, shape):
        at = pl.ds(e * uhalf + i * shape[1], shape[1])
        return dot(wbig[pl.ds(L, L), pl.ds(m * wide, wide)], dp[:, at], TN)

    def outer_value(m, e, i, shape):
        at = pl.ds(e * half + i * shape[0], shape[0])
        return dot(context[:, at], abuf[:, pl.ds(m * wide, wide)], TN)

    def inner_value(m, e, i, shape):
        at = pl.ds(e * width + i * shape[1], shape[1])
        return dot(rows[:, pl.ds(m * wide, wide)], dqkv[:, at], TN)

    everything = [(m, e) for m in range(planes) for e in range(2)]
    weight_of = lambda m: bin(m).count("1")
    free = sorted(
        [p for p in everything if p[0] and not down.sources(*p)], key=lambda p: (-weight_of(p[0]), -p[1])
    )
    first_free = [p for p in free if weight_of(p[0]) == weight_of(planes - 1)]
    more_free = [p for p in free if p not in first_free]
    later = sorted(
        [p for p in everything if p[0] and down.sources(*p)],
        key=lambda p: (-weight_of(p[0]), -p[1]),
    )
    last = [(0, 0), (0, 1)]
    hidden_ref = [abuf.at[:, pl.ds(0, U)]]

    loaded("hidden")
    units(down, first_free, down_value)

    loaded("up")
    act.reduce_begin(mid_tile, 0, planes)

    @pl.loop(0, planes)
    def _(m):
        at = pl.ds(pl.multiple_of(m * wide, wide), wide)
        dfs[:, at] += mid_tile(m, 0)

    flush()
    again = [
        local.start(hidden_in, wbig.at[pl.ds(0, L), pl.ds(0, U)]),
        local.start(mid_in, wbig.at[pl.ds(L, L), pl.ds(0, D)]),
    ]
    for copy in again:
        copy.wait()
    hidden_ref[0] = wbig.at[pl.ds(0, L), pl.ds(0, U)]
    units(up, first_free, up_value)
    units(down, more_free, down_value)

    def mid_base(m):
        return dfs[:, pl.ds(pl.multiple_of(m * wide, wide), wide)]

    def mid_put(m, value):
        dfs[:, pl.ds(pl.multiple_of(m * wide, wide), wide)] = value

    act.reduce_finish(mid_base, mid_put)
    ends_acc[...] = jnp.zeros_like(ends_acc)
    ends_acc[0:3, :] = sums[...]

    @pl.loop(0, R // 16)
    def _(i):
        at = pl.ds(pl.multiple_of(i * 16, 16), 16)
        grad = dfs[at, :]
        normal = normed[at, :]
        scaled = grad * gain[1:2, :]
        d_sum = inverse[at, :] * (
            scaled - mean_of(scaled) - normal * mean_of(scaled * normal)
        )
        abuf[at, :] = d_sum.astype(BF16)
        dfs[at, :] = d_sum
        for index, value in enumerate((d_sum, grad * normal, grad)):
            ends_acc[3 + index : 4 + index, :] += jnp.sum(value, axis=0, keepdims=True)

    act.rows = abuf
    act.gather_start()
    flush()
    for m in range(planes):
        small_d[k.g ^ m] = ends_acc[:, m * wide : (m + 1) * wide]

    units(up, more_free, up_value)
    units(down, later, down_value)
    units(down, last, down_value, True)
    units(up, last, up_value, True)
    flush()
    loads["rows"] = [local.start(rows_in, rows)]
    for e in range(2):
        value = jnp.sum(dp[:, pl.ds(e * uhalf, uhalf)].astype(F32), axis=0, keepdims=True)
        line = lax.broadcasted_iota(jnp.int32, small_u.shape, 0)
        small_u[...] = jnp.where(line == places[e], value, small_u[...])
    loaded("attention")
    for step in range(n):
        if step == 1:
            act.gather_relay()
        act.gather_wait(step)
        where = pl.ds(step * 2 * R, 2 * R)
        total = dot(abuf[where, pl.ds(0, wide)], wo[0], NT)
        for m in range(1, planes):
            total = total + dot(abuf[where, pl.ds(m * wide, wide)], wo[m], NT)
        d_context[where, :] = total.astype(BF16)
    if n == 1:
        act.gather_relay()
    flush()
    units(outer, first_free + more_free, outer_value)
    units(outer, last, outer_value, True)
    act.gather_end()

    lane = lax.broadcasted_iota(jnp.int32, (R, HD), 1)
    per_half = half // HD

    def attend_head(head):
        at = pl.ds(pl.multiple_of(head * HD, HD), HD)
        base = (head // per_half) * width + (head % per_half) * HD
        ats = [pl.ds(pl.multiple_of(base + index * half, HD), HD) for index in range(3)]
        dk[...] = jnp.zeros_like(dk)
        dv[...] = jnp.zeros_like(dv)

        @pl.loop(0, T)
        def _(piece):
            where = pl.ds(pl.multiple_of(piece * R, R), R)
            queries, keys, values = qkv[0, where, at], qkv[1, :, at], qkv[2, :, at]
            grads = d_context[where, at]
            scores = dot(queries, keys, NT) * HD ** (-0.5)
            same = label_column[where, :] == label_row[...]
            log_total = jnp.sum(jnp.where(lane == head, lse[where, :], 0.0), axis=-1, keepdims=True)
            probs = jnp.exp(jnp.where(same, scores, NEG) - log_total)
            d_probs = dot(grads, values, NT)
            inner_sum = jnp.sum(probs * d_probs, axis=-1, keepdims=True)
            d_scores = (probs * (d_probs - inner_sum)).astype(BF16)
            dqkv[where, ats[0]] = (dot(d_scores, keys) * HD ** (-0.5)).astype(BF16)
            dk[...] += dot(d_scores, queries, TN)
            dv[...] += dot(probs.astype(BF16), grads, TN)

        dqkv[:, ats[1]] = (dk[...] * HD ** (-0.5)).astype(BF16)
        dqkv[:, ats[2]] = dv[...].astype(BF16)

    count = C // HD

    @pl.loop(0, count // 2)
    def _(head):
        attend_head(head)

    units(up, later, up_value)
    flush()

    @pl.loop(count // 2, count)
    def _(head):
        attend_head(head)

    loaded("weights")

    def rows_tile(m, index):
        at = pl.ds(pl.multiple_of(m * wide, wide), wide)
        return dot(dqkv[pl.ds(index * R, R), :], wbuf[at, pl.ds(0, 2 * width)], NT)

    act.reduce_begin(rows_tile, 0, planes)
    loaded("rows")
    units(inner, sorted(first_free + more_free, key=lambda p: (-p[1], -weight_of(p[0]))), inner_value)
    flush()

    def rows_base(m):
        return rows_tile(m, 0) + dfs[:, pl.ds(pl.multiple_of(m * wide, wide), wide)]

    def rows_put(m, value):
        final_rows[:, pl.ds(pl.multiple_of(m * wide, wide), wide)] = value.astype(BF16)

    for e in range(2):
        for index, part in enumerate((0, 2)):
            at = pl.ds(e * width + part * half, half)
            value = jnp.sum(dqkv[:, at].astype(F32), axis=0, keepdims=True)
            to = pl.ds(index * half, half)
            line = lax.broadcasted_iota(jnp.int32, (2 * T, half), 0)
            small_q[:, to] = jnp.where(line == places[e], value, small_q[:, to])
    units(outer, later, outer_value)
    close(down, None)
    layer_done()
    act.reduce_finish(rows_base, rows_put)
    flush()
    input_done = trade(final_rows, input_grad)

    smalls = ((small_d, got_d), (small_q, got_q), (small_u, got_u))
    rounds = [[k.along(step) for step in range(1, n)]] if n > 1 else []
    rounds += [[k.mate()], [k.across()]]
    mask = 1
    while mask < planes:
        rounds.append([k.plane(mask)])
        mask *= 2
    small_slot = k.slots(3 * (n + 1 + planes))
    small_turn = [0]

    flying = []

    def small_start():
        for peer in rounds.pop(0) if rounds else []:
            for index, (mine, other) in enumerate(smalls):
                at = small_turn[0]
                copy = k.copy(small_slot + 3 * at + index, mine, other.at[at], peer)
                copy.start()
                flying.append((copy, mine, other.at[at]))
            small_turn[0] += 1

    def small_finish():
        for copy, mine, other in flying:
            copy.wait()
        for copy, mine, other in flying:
            mine[...] += other[...]
        flying.clear()

    small_start()
    close(up, None)
    small_finish()
    small_start()
    units(inner, later, inner_value)
    flush()
    small_finish()
    small_start()
    close(outer, None)
    small_finish()
    while rounds:
        small_start()
        small_finish()
    close(inner, inner_value)
    input_done()
    for work in (down, up, outer, inner):
        work.arrive()
    for copy in k.sent:
        copy.wait_send()


def backward(size, arrays):
    R, D, L, T = size.rows, size.dim, size.length, size.tp
    P_, n, wide, half, uhalf = size.planes, size.n, size.wide, size.half, size.uhalf
    C, U, fine = size.heads, size.units, size.fine
    width = 3 * half
    bits = P_.bit_length() - 1
    rounds = 2 + bits + n - 1
    shape = jax.ShapeDtypeStruct
    m = max(P_ - 1, 1)
    outs = [
        shape((R, D), BF16),
        shape((R, D), BF16),
        shape((P_, U, wide), BF16),
        shape((2, D, uhalf), BF16),
        shape((P_, C, wide), BF16),
        shape((2, D, width), BF16),
        shape((m, 2, uhalf, wide), BF16),
        shape((m, 2, wide, uhalf), BF16),
        shape((m, 2, half, wide), BF16),
        shape((m, 2, wide, width), BF16),
        shape((3, uhalf, fine), BF16),
        shape((3, fine, uhalf), BF16),
        shape((3, half, fine), BF16),
        shape((3, fine, width), BF16),
    ]
    smalls = [
        shape((P_, 8, wide), F32),
        shape((2 * T, 2 * half), F32),
        shape((2 * T, uhalf), F32),
    ]
    anywhere = pl.BlockSpec(memory_space=pl.ANY)
    vmem = pl.BlockSpec(memory_space=pltpu.VMEM)
    tall, broad = max(U, D), max(D, 2 * width)
    slots = 2 * n + 2 * n * P_ + 4 * (2 * P_ + 1) + 2 * P_ + 3 * (n + 1 + P_)
    far = max(n - 1, 1) * P_
    tile = (
        max(min(512, uhalf), wide, half),
        max(wide, column_tile(uhalf), column_tile(width)),
    )
    scratch = [
        pltpu.VMEM((L, D), BF16),
        pltpu.VMEM((tall, broad), BF16),
        pltpu.VMEM((max(D, 2 * L), max(U, D)), BF16),
        pltpu.VMEM((P_, C, wide), BF16),
        pltpu.VMEM((L, max(U, D)), BF16),
        pltpu.VMEM((L, U), BF16),
        pltpu.VMEM((3, L, C), BF16),
        pltpu.VMEM((L, 3 * C), BF16),
        pltpu.VMEM((L, C), BF16),
        pltpu.VMEM((L, C), BF16),
        pltpu.VMEM((L, HD), F32),
        pltpu.VMEM((P_, R, wide), BF16),
        pltpu.VMEM((n * P_, R, wide), BF16),
        pltpu.VMEM((far, R, wide), BF16),
        pltpu.VMEM((far, R, wide), BF16),
        pltpu.VMEM((R, D), F32),
        pltpu.VMEM((L, HD), F32),
        pltpu.VMEM((L, HD), F32),
        pltpu.VMEM((2,) + tile, BF16),
        pltpu.VMEM((2, bits + 1) + tile, BF16),
        pltpu.VMEM((R, D), BF16),
        pltpu.VMEM((rounds, P_, 8, wide), F32),
        pltpu.VMEM((rounds, 2 * T, 2 * half), F32),
        pltpu.VMEM((rounds, 2 * T, uhalf), F32),
        pltpu.VMEM((8, D), F32),
        pltpu.VMEM((8, D), F32),
        pltpu.SemaphoreType.DMA((slots,)),
        pltpu.SemaphoreType.DMA((slots,)),
        pltpu.SemaphoreType.DMA((32 + 3 * P_,)),
        pltpu.SemaphoreType.DMA((2,)),
        pltpu.SemaphoreType.DMA((2, bits + 1)),
    ]
    return pl.pallas_call(
        functools.partial(backward_kernel, size),
        out_shape=outs + smalls,
        in_specs=[anywhere] * 13 + [vmem, vmem, anywhere, anywhere] + [vmem] * 4,
        out_specs=[anywhere] * 14 + [vmem] * 3,
        scratch_shapes=scratch,
        compiler_params=pltpu.CompilerParams(
            collective_id=1, has_side_effects=True, vmem_limit_bytes=VMEM
        ),
        name="backward",
    )(*arrays)


def shards(
    fsdp,
    tp,
    inputs,
    query_weight,
    query_bias,
    key_weight,
    value_weight,
    value_bias,
    output_weight,
    output_bias,
    first_gain,
    first_shift,
    up_weight,
    up_bias,
    down_weight,
    down_bias,
    second_gain,
    second_shift,
    segments,
    cotangent,
):
    size = Sizes(fsdp, tp, inputs, query_weight, up_weight, segments)
    f, t = lax.axis_index("fsdp"), lax.axis_index("tp")
    c = f % 2
    residual = jnp.stack(
        [output_bias, first_gain, first_shift, down_bias, second_gain, second_shift]
        + [output_bias] * 2
    )
    residual = residual.reshape(8, size.planes, size.wide).transpose(1, 0, 2)
    role_bias = jnp.concatenate(
        [v.reshape(2, -1) for v in (query_bias, value_bias, up_bias)], axis=1
    )[:, None]
    kept = forward(
        size,
        (
            inputs,
            cotangent,
            segments.reshape(tp, 1, size.rows),
            segments.reshape(size.length, 1),
            role_bias,
            residual,
            query_weight,
            key_weight,
            value_weight,
            output_weight,
            up_weight,
            down_weight,
        ),
    )
    results = backward(size, tuple(kept) + (residual,))
    layer_out, input_grad = results[:2]
    grad_d, grad_u, grad_o, grad_x = results[2:6]
    last_d, last_u, last_o, last_x, small_d, small_q, small_u = results[10:]

    def home(grad, axis):
        if axis == 1:
            return lax.dynamic_slice_in_dim(grad[0], c * size.fine, size.fine, axis=0)
        return lax.dynamic_slice_in_dim(
            grad[0, : grad.shape[1] // 2], c * size.fine, size.fine, axis=1
        )

    def owned(own, last, axis):
        mine = own.astype(F32) + last[1].astype(F32)
        other = last[0].astype(F32) + last[2].astype(F32)
        return jnp.where(
            c == 0,
            jnp.concatenate([mine, other], axis=axis),
            jnp.concatenate([other, mine], axis=axis),
        )

    half = size.half
    home_x = home(grad_x, 1)
    inner = []
    for i in range(3):
        at = slice(i * half, (i + 1) * half)
        inner.append(owned(home_x[:, at], last_x[:, :, at], 1))
    small_d = small_d.transpose(1, 0, 2).reshape(8, size.dim)
    residual_size = size.dim // (fsdp * tp)
    ends = lax.dynamic_slice(small_d, (0, (f * tp + t) * residual_size), (8, residual_size))

    def split(table):
        row = lax.dynamic_slice_in_dim(table, 2 * t, 2).reshape(1, -1)
        part = row.shape[1] // fsdp
        return lax.dynamic_slice_in_dim(row, f * part, part, axis=1)

    return (
        layer_out,
        input_grad,
        inner[0],
        split(small_q[:, :half]),
        inner[1],
        inner[2],
        split(small_q[:, half:]),
        owned(home(grad_o, 0), last_o, 0),
        ends[3],
        ends[4],
        ends[5],
        owned(home(grad_u, 1), last_u, 1),
        split(small_u),
        owned(home(grad_d, 0), last_d, 0),
        ends[0],
        ends[1],
        ends[2],
    )


def solution(mesh):
    fsdp, tp = mesh.shape["fsdp"], mesh.shape["tp"]

    def body(*arrays):
        return shards(fsdp, tp, *arrays)

    tokens, inner, outer = P(AXES, None), P("fsdp", "tp"), P("tp", "fsdp")
    placed = (
        tokens,
        inner,
        P("tp"),
        inner,
        inner,
        P("tp"),
        outer,
        P(),
        P(),
        P(),
        inner,
        P("tp"),
        outer,
        P(),
        P(),
        P(),
        P("fsdp", None),
        tokens,
    )
    return jax.shard_map(
        body,
        mesh=mesh,
        in_specs=placed,
        out_specs=(
            tokens,
            tokens,
            inner,
            outer,
            inner,
            inner,
            outer,
            outer,
            P(AXES),
            P(AXES),
            P(AXES),
            inner,
            outer,
            outer,
            P(AXES),
            P(AXES),
            P(AXES),
        ),
        check_vma=False,
    )
```

```python
import functools

import jax
import jax.numpy as jnp
from jax import lax
from jax.experimental import pallas as pl
from jax.experimental.pallas import tpu as pltpu
from jax.sharding import PartitionSpec as P

HD = 128
EPS = 1e-06
NEG = -1000000000.0
AXES = ("fsdp", "tp")
F32 = jnp.float32
BF16 = jnp.bfloat16
MESH = pl.DeviceIdType.MESH
VMEM = 62 * 2**20


def gelu_tanh(values):
    return jax.nn.gelu(values, approximate=True)


def dot(left, right, dims=((1,), (0,))):
    return lax.dot_general(left, right, (dims, ((), ())), preferred_element_type=F32)


NN, NT, TN = ((1,), (0,)), ((1,), (1,)), ((0,), (0,))


class Sizes:
    def __init__(self, fsdp, tp, inputs, query_weight, up_weight, segments):
        self.fsdp, self.tp = fsdp, tp
        self.planes, self.n = fsdp // 2, tp // 2
        self.rows, self.dim = inputs.shape
        self.length = segments.shape[1]
        self.fine = query_weight.shape[0]
        self.wide = 2 * self.fine
        self.heads = query_weight.shape[1]
        self.half = self.heads // 2
        self.units = up_weight.shape[1]
        self.uhalf = self.units // 2


INNER = (True, True, True, False, True, False)


class Links:
    def __init__(self, size, send, recv):
        self.size, self.send, self.recv = size, send, recv
        f, t = lax.axis_index("fsdp"), lax.axis_index("tp")
        self.g, self.c = f // 2, f % 2
        self.h, self.l = t // size.n, t % size.n
        self.done = set()
        self.sent = []
        self.next = 0

    def device(self, g, c, h, l):
        return (g * 2 + c, h * self.size.n + l)

    def mate(self):
        return self.device(self.g, 1 - self.c, self.h, self.l)

    def across(self):
        return self.device(self.g, self.c, 1 - self.h, self.l)

    def corner(self):
        return self.device(self.g, 1 - self.c, 1 - self.h, self.l)

    def plane(self, mask):
        return self.device(self.g ^ mask, self.c, self.h, self.l)

    def along(self, step):
        return self.device(self.g, self.c, self.h, (self.l + step) % self.size.n)

    def barrier(self):
        size = self.size
        peers = [self.mate(), self.across(), self.corner()]
        mask = 1
        while mask < size.planes:
            peers.append(self.plane(mask))
            mask *= 2
        peers += [self.along(step) for step in range(1, size.n)]
        semaphore = pltpu.get_barrier_semaphore()
        for peer in peers:
            pl.semaphore_signal(semaphore, inc=1, device_id=peer, device_id_type=MESH)
        pl.semaphore_wait(semaphore, len(peers))

    def slots(self, count=1):
        first = self.next
        self.next += count
        return first

    def copy(self, slot, source, target, device):
        return pltpu.make_async_remote_copy(
            src_ref=source,
            dst_ref=target,
            send_sem=self.send.at[slot],
            recv_sem=self.recv.at[slot],
            device_id=device,
            device_id_type=MESH,
        )

    def go(self, slot, source, target, device):
        copy = self.copy(slot, source, target, device)
        copy.start()
        self.sent.append(copy)
        return copy


class Local:
    def __init__(self, semaphores):
        self.semaphores, self.next = semaphores, 0

    def start(self, source, target):
        copy = pltpu.make_async_copy(source, target, self.semaphores.at[self.next])
        self.next += 1
        copy.start()
        return copy


class Spread:
    def __init__(self, links, local, shard, full, inner, hold):
        self.links, self.local, self.hold = links, local, hold
        self.shard, self.full, self.inner = shard, full, inner
        self.base = links.slots(3 + 2 * (links.size.planes - 1))
        self.waited = set()

    def part(self, index):
        axis = 1 if self.inner else 0
        width = self.shard.shape[axis] // 2
        at = pl.multiple_of(index * width, width)
        return self.shard.at[:, pl.ds(at, width)] if self.inner else self.shard.at[pl.ds(at, width)]

    def home(self, e, c):
        fine = self.links.size.fine
        at = pl.ds(pl.multiple_of(c * fine, fine), fine)
        if self.inner:
            return self.full.at[e, at, :]
        width = self.full.shape[1] // 2
        return self.full.at[0, pl.ds(e * width, width), at]

    def block(self, m, e=None):
        wide = self.links.size.wide
        if self.inner:
            at = pl.ds(m * wide, wide)
            return self.full.at[:, at, :] if e is None else self.full.at[e, at, :]
        width = self.full.shape[1] // 2
        return self.full.at[m] if e is None else self.full.at[m, pl.ds(e * width, width)]

    def near(self):
        k = self.links
        self.own = self.local.start(self.part(k.c), self.hold)
        self.steps = [k.go(self.base, self.part(1 - k.c), self.home(0, k.c), k.mate())]
        self.pieces = {}

    def keep(self):
        self.own.wait()
        self.own = self.local.start(self.hold, self.home(0, self.links.c))

    def far(self):
        k = self.links
        self.steps += [
            k.go(self.base + 1, self.part(k.c), self.home(1, k.c), k.across()),
            k.go(self.base + 2, self.part(1 - k.c), self.home(1, k.c), k.corner()),
        ]

    def plane(self, e):
        k = self.links
        if e == 0:
            self.own.wait()
            self.steps[0].wait_recv()
        else:
            self.steps[1].wait_recv()
            self.steps[2].wait_recv()
        mask = 1
        while mask < k.size.planes:
            self.pieces[mask, e] = k.go(
                self.base + 1 + 2 * mask + e, self.block(0, e), self.block(mask, e), k.plane(mask)
            )
            mask *= 2

    def arrive(self, m, e):
        if m and (m, e) not in self.waited:
            self.waited.add((m, e))
            self.pieces[m, e].wait_recv()

    def relay(self, e):
        k = self.links
        for m in sorted(range(1, k.size.planes), key=lambda v: bin(v).count("1")):
            if bin(m).count("1") > 1:
                bit = m & -m if e else 1 << (m.bit_length() - 1)
                self.arrive(m ^ bit, e)
                self.pieces[m, e] = k.go(
                    self.base + 1 + 2 * m + e,
                    self.block(m ^ bit, e),
                    self.block(m, e),
                    k.plane(bit),
                )

    def finish(self):
        for m in range(1, self.links.size.planes):
            for e in range(2):
                self.arrive(m, e)


class Activations:
    def __init__(self, links, rows, give, take, out, came):
        self.links, self.rows = links, rows
        self.give, self.take, self.out, self.came = give, take, out, came
        size = links.size
        self.gather_slots = links.slots(2 * size.n)
        self.mate_slots = links.slots(size.n * size.planes)
        self.along_slots = links.slots(size.n * size.planes)

    def piece(self, index):
        size = self.links.size
        return self.rows.at[pl.ds(index * size.rows, size.rows)]

    def gather_start(self):
        k, base = self.links, self.gather_slots
        self.far = [
            k.go(base + step, self.piece(0), self.piece(2 * step), k.along(step))
            for step in range(1, k.size.n)
        ]
        self.near = [k.go(base + k.size.n, self.piece(0), self.piece(1), k.mate())]

    def gather_relay(self):
        k, base = self.links, self.gather_slots
        for step in range(1, k.size.n):
            self.far[step - 1].wait_recv()
            self.near.append(
                k.go(
                    base + k.size.n + step,
                    self.piece(2 * step),
                    self.piece(2 * step + 1),
                    k.mate(),
                )
            )

    def gather_wait(self, step):
        self.near[step].wait_recv()

    def gather_end(self):
        over = self.far + self.near
        for copy in over:
            copy.wait_send()
        self.links.sent = [c for c in self.links.sent if all(c is not o for o in over)]

    def near_copy(self, step, m):
        k = self.links
        at = step * k.size.planes + m
        return k.copy(self.mate_slots + at, self.give.at[m], self.take.at[at], k.mate())

    def far_copy(self, step, m):
        k = self.links
        at = (step - 1) * k.size.planes + m
        return k.copy(self.along_slots + at, self.out.at[at], self.came.at[at], k.along(step))

    def reduce_near(self, step, tile, low, high):
        n = self.links.size.n
        index = 2 * ((n - step) % n)

        @pl.loop(low, high)
        def _(m):
            value = tile(m, index + 1).astype(BF16)
            if step != 1 and n > 1:
                self.near_copy(step - 1 if step else n - 1, m).wait_send()
            self.give[m] = value
            self.near_copy(step, m).start()

    def reduce_far(self, step, tile, low, high):
        planes, n = self.links.size.planes, self.links.size.n
        index = 2 * ((n - step) % n)

        @pl.loop(low, high)
        def _(m):
            total = tile(m, index)
            self.near_copy(step, m).wait_recv()
            total = total + self.take[step * planes + m].astype(F32)
            self.out[(step - 1) * planes + m] = total.astype(BF16)
            self.far_copy(step, m).start()

    def reduce_begin(self, tile, low, high):
        for step in range(1, self.links.size.n):
            self.reduce_near(step, tile, low, high)
            self.reduce_far(step, tile, low, high)
        self.reduce_near(0, tile, low, high)

    def reduce_finish(self, base, put):
        planes, n = self.links.size.planes, self.links.size.n

        @pl.loop(0, planes)
        def _(m):
            total = base(m)
            self.near_copy(0, m).wait_recv()
            total = total + self.take[m].astype(F32)
            for other in range(1, n):
                self.far_copy(other, m).wait_recv()
                total = total + self.came[(other - 1) * planes + m].astype(F32)
            put(m, total)

        @pl.loop(0, planes)
        def _(m):
            self.near_copy(0, m).wait_send()
            for step in range(1, n):
                self.far_copy(step, m).wait_send()


class Chunked:
    def __init__(self, links, rows):
        self.links, self.rows = links, rows
        self.base = links.slots(2 * links.size.n * links.size.planes)
        self.far, self.near = {}, {}

    def piece(self, index, m):
        size = self.links.size
        return self.rows.at[pl.ds(index * size.rows, size.rows), pl.ds(m * size.wide, size.wide)]

    def start(self, m):
        k = self.links
        n = k.size.n
        base = self.base + 2 * n * m
        for step in range(1, n):
            self.far[step, m] = k.go(
                base + step, self.piece(0, m), self.piece(2 * step, m), k.along(step)
            )
        self.near[0, m] = k.go(base + n, self.piece(0, m), self.piece(1, m), k.mate())

    def relay(self, m):
        k = self.links
        n = k.size.n
        base = self.base + 2 * n * m
        for step in range(1, n):
            self.far[step, m].wait_recv()
            self.near[step, m] = k.go(
                base + n + step, self.piece(2 * step, m), self.piece(2 * step + 1, m), k.mate()
            )

    def wait(self):
        for copy in self.near.values():
            copy.wait_recv()

    def end(self):
        over = list(self.far.values()) + list(self.near.values())
        for copy in over:
            copy.wait_send()
        self.links.sent = [c for c in self.links.sent if all(c is not o for o in over)]


def mean_of(value):
    return jnp.mean(value, axis=-1, keepdims=True)


def forward_kernel(size, *refs):
    (
        inputs,
        cotangent,
        label_row,
        label_column,
        role_bias,
        residual,
        *shards_,
    ) = refs[:12]
    (
        fulls_q,
        fulls_k,
        fulls_v,
        fulls_o,
        fulls_u,
        fulls_d,
        rows_out,
        qkv_out,
        context_out,
        lse_out,
        mid_out,
        pre_out,
        hidden_out,
        normed_out,
        inverse_out,
        final_out,
        d_second_out,
        sums_out,
        label_row_out,
        label_column_out,
    ) = refs[12:32]
    (
        rows,
        wq,
        qkv,
        context,
        lse,
        wo,
        wu,
        wd,
        hidden,
        pre,
        give,
        take,
        out,
        came,
        cot,
        labels_r,
        labels_c,
        bias,
        vectors,
        send,
        recv,
        near_sem,
        *holds,
    ) = refs[32:]
    k = Links(size, send, recv)
    local = Local(near_sem)
    R, D, L, wide, half, uhalf = (
        size.rows,
        size.dim,
        size.length,
        size.wide,
        size.half,
        size.uhalf,
    )
    planes, n = size.planes, size.n
    k.barrier()
    stay = k.c == k.h

    fulls = (fulls_q, fulls_k, fulls_v, fulls_o, fulls_u, fulls_d)
    spread = [
        Spread(k, local, shard, full, inner, hold)
        for shard, full, inner, hold in zip(shards_, fulls, INNER, holds)
    ]
    act = Activations(k, rows, give, take, out, came)
    begin = Chunked(k, rows)

    def trade(source, target):
        base = k.slots(planes)
        first_local = local.next
        local.next += planes

        def pieces(m):
            at = pl.multiple_of((k.g ^ m) * wide, wide)
            return source.at[:, pl.ds(at, wide)], target(m)

        @pl.when(stay)
        def _():
            for m in range(planes):
                a, b = pieces(m)
                pltpu.make_async_copy(a, b, near_sem.at[first_local + m]).start()

        @pl.when(jnp.logical_not(stay))
        def _():
            for m in range(planes):
                a, b = pieces(m)
                k.copy(base + m, a, b, k.corner()).start()

        def wait(blocks=range(planes)):
            @pl.when(stay)
            def _():
                for m in blocks:
                    a, b = pieces(m)
                    pltpu.make_async_copy(a, b, near_sem.at[first_local + m]).wait()

            @pl.when(jnp.logical_not(stay))
            def _():
                for m in blocks:
                    a, b = pieces(m)
                    k.copy(base + m, a, b, k.corner()).wait()

        return wait

    for index in range(3):
        spread[index].near()
    spread[0].far()
    spread[1].far()
    for index in range(3, 6):
        spread[index].near()
    for index in range(6):
        spread[index].keep()
    for index in range(3):
        spread[index].plane(0)
    rows_ready = trade(inputs, lambda m: rows.at[pl.ds(0, R), pl.ds(m * wide, wide)])

    label_slots = k.slots(2)
    label_pairs = ((label_row, labels_r), (label_column, labels_c))

    @pl.when(stay)
    def _():
        for index, (a, b) in enumerate(label_pairs):
            k.copy(label_slots + index, a, b, k.mate()).start()

    label_local = local.next
    local.next += 2

    @pl.when(stay)
    def _():
        for index, (a, b) in enumerate(label_pairs):
            pltpu.make_async_copy(a, b, near_sem.at[label_local + index]).start()

    bias_slot = k.slots()
    bias_copy = k.go(bias_slot, role_bias.at[k.c], bias.at[1], k.across())
    bias_local = local.start(role_bias.at[k.c], bias.at[0])

    for m in range(planes):
        vectors[:, pl.ds(m * wide, wide)] = residual[k.g ^ m]

    saved = []
    loads = {}

    def load(index, buffer):
        spread[index].finish()
        loads[index] = local.start(fulls[index], buffer)

    spread[0].plane(1)
    spread[2].far()
    for index in range(3):
        spread[index].relay(0)
    spread[1].plane(1)
    spread[3].far()
    spread[0].relay(1)
    for m in range(planes):
        rows_ready([m])
        begin.start(m)
    spread[2].plane(1)
    spread[4].far()
    spread[1].relay(1)
    spread[4].plane(0)
    for m in range(planes):
        begin.relay(m)
    spread[2].relay(1)
    spread[3].plane(0)
    spread[3].plane(1)
    begin.wait()
    saved.append(local.start(rows, rows_out))
    bias_copy.wait_recv()
    bias_local.wait()

    @pl.when(stay)
    def _():
        for index, (a, b) in enumerate(label_pairs):
            pltpu.make_async_copy(a, b, near_sem.at[label_local + index]).wait()
            k.copy(label_slots + index, a, b, k.mate()).wait_send()

    @pl.when(jnp.logical_not(stay))
    def _():
        for index, (a, b) in enumerate(label_pairs):
            k.copy(label_slots + index, a, b, k.mate()).wait_recv()

    load(0, wq.at[0])
    load(1, wq.at[1])
    for index in range(3):
        loads[index].wait()
        for e in range(2):
            result = dot(rows[...], wq[index % 2, e])
            if index != 1:
                at = 0 if index == 0 else half
                result = result + bias[e, :, pl.ds(at, half)]
            qkv[index, :, pl.ds(e * half, half)] = result.astype(BF16)
        if index == 0:
            load(2, wq.at[0])
    saved.append(local.start(qkv, qkv_out))
    begin.end()

    spread[4].relay(0)
    spread[3].relay(0)
    spread[3].relay(1)
    spread[4].plane(1)
    spread[5].far()
    order = []
    for step in range(n):
        for core in (k.c, 1 - k.c):
            order.append(core * n + (k.l + n - step) % n)
    row = jnp.concatenate([labels_r[q] for q in order], axis=-1)
    label_row_out[...] = row
    for piece, q in enumerate(order):
        column = labels_c[pl.ds(pl.multiple_of(q * R, R), R), :]
        label_column_out[pl.ds(piece * R, R), :] = column
        same = column == row

        lane = lax.broadcasted_iota(jnp.int32, (R, HD), 1)
        where = pl.ds(piece * R, R)

        def one(head, kept, where=where, same=same):
            at = pl.ds(pl.multiple_of(head * HD, HD), HD)
            scores = dot(qkv[0, where, at], qkv[1, :, at], NT) * HD ** (-0.5)
            scores = jnp.where(same, scores, NEG)
            top = jnp.max(scores, axis=-1, keepdims=True)
            weights = jnp.exp(scores - top)
            summed = jnp.sum(weights, axis=-1, keepdims=True)
            probs = (weights * (1.0 / summed)).astype(BF16)
            context[where, at] = dot(probs, qkv[2, :, at]).astype(BF16)
            return jnp.where(lane == head, top + jnp.log(summed), kept)

        lse[where, :] = lax.fori_loop(0, size.heads // HD, one, jnp.zeros((R, HD), F32))
        if piece == size.tp // 2 - 1:
            spread[5].plane(0)

    saved.append(local.start(context, context_out))
    saved.append(local.start(lse, lse_out))

    load(3, wo)
    loads[3].wait()

    def attn_tile(m, index):
        return dot(context[pl.ds(index * R, R), :], wo[m])

    def attn_put(m, value):
        at = pl.ds(pl.multiple_of(m * wide, wide), wide)
        normed_out[:, at] = value + rows[pl.ds(0, R), at].astype(F32) + vectors[0:1, at]

    saved[0].wait()
    act.reduce_begin(attn_tile, 0, planes)
    spread[4].relay(1)
    act.reduce_finish(lambda m: attn_tile(m, 0), attn_put)

    @pl.loop(0, R // 16)
    def _(i):
        at = pl.ds(pl.multiple_of(i * 16, 16), 16)
        summed = normed_out[at, :]
        center = summed - mean_of(summed)
        scale = lax.rsqrt(mean_of(center * center) + EPS)
        normed = center * scale
        normed_out[at, :] = normed
        inverse_out[at, :] = scale
        rows[at, :] = (normed * vectors[1:2, :] + vectors[2:3, :]).astype(BF16)

    act.gather_start()
    spread[5].relay(0)
    spread[5].plane(1)
    act.gather_relay()
    load(4, wu)
    loads[4].wait()
    tile = min(512, uhalf)
    for step in range(n):
        act.gather_wait(step)
        if step == n - 1:
            cot_ready = trade(cotangent, lambda m: cot.at[:, pl.ds(m * wide, wide)])
        where = pl.ds(step * 2 * R, 2 * R)
        for e in range(2):

            @pl.loop(0, uhalf // tile)
            def _(j, e=e, where=where):
                at = pl.ds(pl.multiple_of(j * tile, tile), tile)
                to = pl.ds(pl.multiple_of(e * uhalf + j * tile, tile), tile)
                skip = pl.ds(pl.multiple_of(2 * half + j * tile, 128), tile)
                value = dot(rows[where, :], wu[e, :, at]) + bias[e, :, skip]
                pre[where, to] = value.astype(BF16)
                hidden[where, to] = gelu_tanh(value).astype(BF16)

    saved.append(local.start(rows, mid_out))
    saved.append(local.start(pre, pre_out))
    saved.append(local.start(hidden, hidden_out))
    act.gather_end()

    def ffn_tile(m, index):
        return dot(hidden[pl.ds(index * R, R), :], wd[m])

    def ffn_put(m, value):
        at = pl.ds(pl.multiple_of(m * wide, wide), wide)
        first = normed_out[:, at] * vectors[1:2, at] + vectors[2:3, at]
        d_second_out[:, at] = value + first + vectors[3:4, at]

    counts = [bin(m).count("1") for m in range(planes)]
    low = 0
    while low < planes:
        high = low + 1
        while high < planes and (counts[high] > 1) == (counts[low] > 1) and low:
            high += 1
        if low == 1:
            spread[5].relay(1)
        pieces = []
        for m in range(low, high):
            spread[5].arrive(m, 0)
            spread[5].arrive(m, 1)
            pieces.append(local.start(fulls[5].at[m], wd.at[m]))
        for piece in pieces:
            piece.wait()
        act.reduce_begin(ffn_tile, low, high)
        low = high
    act.reduce_finish(lambda m: ffn_tile(m, 0), ffn_put)
    cot_ready()
    sums_out[...] = jnp.zeros_like(sums_out)

    @pl.loop(0, R // 16)
    def _(i):
        at = pl.ds(pl.multiple_of(i * 16, 16), 16)
        summed = d_second_out[at, :]
        center = summed - mean_of(summed)
        scale = lax.rsqrt(mean_of(center * center) + EPS)
        normed = center * scale
        final_out[at, :] = (normed * vectors[4:5, :] + vectors[5:6, :]).astype(BF16)
        grad = cot[at, :].astype(F32)
        scaled = grad * vectors[4:5, :]
        d_second = scale * (scaled - mean_of(scaled) - normed * mean_of(scaled * normed))
        d_second_out[at, :] = d_second
        for index, value in enumerate((d_second, grad * normed, grad)):
            sums_out[index : index + 1, :] += jnp.sum(value, axis=0, keepdims=True)

    for copy in saved[1:]:
        copy.wait()
    for copy in k.sent:
        copy.wait_send()


def forward(size, arrays):
    R, D, L, T = size.rows, size.dim, size.length, size.tp
    P_, n, wide, half, uhalf = size.planes, size.n, size.wide, size.half, size.uhalf
    C, U = size.heads, size.units
    whole = [jax.ShapeDtypeStruct((2, D, half), BF16)] * 3 + [
        jax.ShapeDtypeStruct((P_, C, wide), BF16),
        jax.ShapeDtypeStruct((2, D, uhalf), BF16),
        jax.ShapeDtypeStruct((P_, U, wide), BF16),
    ]
    kept = [
        jax.ShapeDtypeStruct((L, D), BF16),
        jax.ShapeDtypeStruct((3, L, C), BF16),
        jax.ShapeDtypeStruct((L, C), BF16),
        jax.ShapeDtypeStruct((L, HD), F32),
        jax.ShapeDtypeStruct((L, D), BF16),
        jax.ShapeDtypeStruct((L, U), BF16),
        jax.ShapeDtypeStruct((L, U), BF16),
    ]
    ends = [
        jax.ShapeDtypeStruct((R, D), F32),
        jax.ShapeDtypeStruct((R, 1), F32),
        jax.ShapeDtypeStruct((R, D), BF16),
        jax.ShapeDtypeStruct((R, D), F32),
        jax.ShapeDtypeStruct((3, D), F32),
        jax.ShapeDtypeStruct((1, L), jnp.int32),
        jax.ShapeDtypeStruct((L, 1), jnp.int32),
    ]
    anywhere = pl.BlockSpec(memory_space=pl.ANY)
    vmem = pl.BlockSpec(memory_space=pltpu.VMEM)
    width = 2 * half + uhalf
    slots = 6 * (3 + 2 * (P_ - 1)) + 2 * P_ + 3 + 2 * n + 4 * n * P_
    scratch = [
        pltpu.VMEM((L, D), BF16),
        pltpu.VMEM((2, 2, D, half), BF16),
        pltpu.VMEM((3, L, C), BF16),
        pltpu.VMEM((L, C), BF16),
        pltpu.VMEM((L, HD), F32),
        pltpu.VMEM((P_, C, wide), BF16),
        pltpu.VMEM((2, D, uhalf), BF16),
        pltpu.VMEM((P_, U, wide), BF16),
        pltpu.VMEM((L, U), BF16),
        pltpu.VMEM((L, U), BF16),
        pltpu.VMEM((P_, R, wide), BF16),
        pltpu.VMEM((n * P_, R, wide), BF16),
        pltpu.VMEM((max(n - 1, 1) * P_, R, wide), BF16),
        pltpu.VMEM((max(n - 1, 1) * P_, R, wide), BF16),
        pltpu.VMEM((R, D), BF16),
        pltpu.VMEM((T, 1, R), jnp.int32),
        pltpu.VMEM((L, 1), jnp.int32),
        pltpu.VMEM((2, 1, width), F32),
        pltpu.VMEM((8, D), F32),
        pltpu.SemaphoreType.DMA((slots,)),
        pltpu.SemaphoreType.DMA((slots,)),
        pltpu.SemaphoreType.DMA((32 + 2 * P_,)),
        *[pltpu.VMEM((size.fine, half), BF16)] * 3,
        pltpu.VMEM((half, size.fine), BF16),
        pltpu.VMEM((size.fine, uhalf), BF16),
        pltpu.VMEM((uhalf, size.fine), BF16),
    ]
    return pl.pallas_call(
        functools.partial(forward_kernel, size),
        out_shape=whole + kept + ends,
        in_specs=[anywhere, anywhere, vmem, vmem, vmem, vmem] + [anywhere] * 6,
        out_specs=[anywhere] * 13 + [vmem] * 7,
        scratch_shapes=scratch,
        compiler_params=pltpu.CompilerParams(
            collective_id=0, has_side_effects=True, vmem_limit_bytes=VMEM
        ),
        name="forward",
    )(*arrays)


class Collect:
    def __init__(self, links, grad, came, last, inner):
        self.links, self.grad, self.came, self.last, self.inner = links, grad, came, last, inner
        self.planes = links.size.planes
        self.base = links.slots(2 * (self.planes - 1) + 3)
        self.flying, self.final = {}, []

    def block(self, m, e):
        wide = self.links.size.wide
        if self.inner:
            return self.grad.at[e, pl.ds(m * wide, wide), :]
        width = self.grad.shape[1] // 2
        return self.grad.at[m, pl.ds(e * width, width), :]

    def home(self, e, c):
        fine = self.links.size.fine
        at = pl.ds(pl.multiple_of(c * fine, fine), fine)
        if self.inner:
            return self.grad.at[e, at, :]
        width = self.grad.shape[1] // 2
        return self.grad.at[0, pl.ds(e * width, width), at]

    @staticmethod
    def bit(m, e):
        return m & -m if e else 1 << (m.bit_length() - 1)

    def sources(self, m, e):
        return [o for o in range(1, self.planes) if o != m and o ^ self.bit(o, e) == m]

    def send(self, m, e):
        self.flying[m, e] = self.links.go(
            self.base + 2 * (m - 1) + e,
            self.block(m, e),
            self.came.at[m - 1, e],
            self.links.plane(self.bit(m, e)),
        )

    def finish(self, e):
        k = self.links
        base = self.base + 2 * (self.planes - 1)
        if e == 0:
            self.final.append(k.go(base, self.home(0, 1 - k.c), self.last.at[0], k.mate()))
            return
        self.final += [
            k.go(base + 1, self.home(1, k.c), self.last.at[1], k.across()),
            k.go(base + 2, self.home(1, 1 - k.c), self.last.at[2], k.corner()),
        ]

    def arrive(self):
        for copy in self.final:
            copy.wait_recv()


def column_tile(width):
    for tile in (512, 384):
        if width % tile == 0:
            return tile
    return width


def gelu_slope(v):
    scale = 0.7978845608028654
    square = v * v
    t = jnp.tanh(scale * v * (1.0 + 0.044715 * square))
    return 0.5 * (1.0 + t) + 0.5 * v * (1.0 - t * t) * scale * (1.0 + 3 * 0.044715 * square)


def backward_kernel(size, *refs):
    (
        full_q,
        full_k,
        full_v,
        full_o,
        full_u,
        full_d,
        rows_in,
        qkv_in,
        context_in,
        lse_in,
        mid_in,
        pre_in,
        hidden_in,
        normed,
        inverse,
        final,
        d_second,
        sums,
        label_row,
        label_column,
        residual,
    ) = refs[:21]
    (
        layer_out,
        input_grad,
        grad_d,
        grad_u,
        grad_o,
        grad_x,
        came_d,
        came_u,
        came_o,
        came_x,
        last_d,
        last_u,
        last_o,
        last_x,
        small_d,
        small_q,
        small_u,
    ) = refs[21:38]
    (
        rows,
        wbuf,
        wbig,
        wo,
        abuf,
        dp,
        qkv,
        dqkv,
        context,
        d_context,
        lse,
        give,
        take,
        out,
        came,
        dfs,
        dk,
        dv,
        stage,
        parts,
        final_rows,
        got_d,
        got_q,
        got_u,
        gain,
        ends_acc,
        send,
        recv,
        near_sem,
        stage_sem,
        part_sem,
    ) = refs[38:]
    k = Links(size, send, recv)
    local = Local(near_sem)
    R, D, L, wide, half, uhalf, T = (
        size.rows,
        size.dim,
        size.length,
        size.wide,
        size.half,
        size.uhalf,
        size.tp,
    )
    planes, n, C, U = size.planes, size.n, size.heads, size.units
    width = 3 * half
    act = Activations(k, rows, give, take, out, came)
    down = Collect(k, grad_d, came_d, last_d, False)
    up = Collect(k, grad_u, came_u, last_u, True)
    outer = Collect(k, grad_o, came_o, last_o, False)
    inner = Collect(k, grad_x, came_x, last_x, True)
    k.barrier()
    stay = k.c == k.h

    def trade(source, target):
        base = k.slots(planes)
        first_local = local.next
        local.next += planes

        def pieces(m):
            at = pl.multiple_of((k.g ^ m) * wide, wide)
            return source.at[:, pl.ds(m * wide, wide)], target.at[:, pl.ds(at, wide)]

        def both(go):
            @pl.when(stay)
            def _():
                for m in range(planes):
                    copy = pltpu.make_async_copy(*pieces(m), near_sem.at[first_local + m])
                    copy.start() if go else copy.wait()

            @pl.when(jnp.logical_not(stay))
            def _():
                for m in range(planes):
                    copy = k.copy(base + m, *pieces(m), k.corner())
                    copy.start() if go else copy.wait()

        both(True)
        return lambda: both(False)

    loads = {}
    start = local.start(d_second, dfs)
    loads["pre"] = [local.start(pre_in, dp)]
    loads["down"] = [
        local.start(full_d.at[m], wbuf.at[pl.ds(0, U), pl.ds(m * wide, wide)])
        for m in range(planes)
    ]
    start.wait()
    rows[pl.ds(0, R), :] = dfs[...].astype(BF16)
    act.gather_start()
    loads["hidden"] = [local.start(hidden_in, abuf.at[:, pl.ds(0, U)])]
    loads["up"] = [
        local.start(full_u.at[e], wbig.at[pl.ds(0, D), pl.ds(e * uhalf, uhalf)]) for e in range(2)
    ]
    loads["final"] = [local.start(final, final_rows)]
    loads["attention"] = [
        local.start(qkv_in, qkv),
        local.start(context_in, context),
        local.start(lse_in, lse),
        local.start(full_o, wo),
    ]
    for m in range(planes):
        gain[:, pl.ds(m * wide, wide)] = residual[k.g ^ m]

    def loaded(name):
        for copy in loads[name]:
            copy.wait()

    small_d[...] = jnp.zeros_like(small_d)
    small_q[...] = jnp.zeros_like(small_q)
    small_u[...] = jnp.zeros_like(small_u)
    places = [(k.h * n + k.l) * 2 + k.c, ((1 - k.h) * n + k.l) * 2 + k.c]

    tile = min(512, U)
    loaded("pre")
    loaded("down")
    for step in range(n):
        if step == 1:
            act.gather_relay()
        if step == n - 1:
            loaded("final")
            layer_done = trade(final_rows, layer_out)
        act.gather_wait(step)
        where = pl.ds(step * 2 * R, 2 * R)

        @pl.loop(0, U // tile)
        def _(j, where=where):
            at = pl.ds(pl.multiple_of(j * tile, tile), tile)
            d_hidden = dot(rows[where, :], wbuf[at, pl.ds(0, D)], NT)
            value = (d_hidden * gelu_slope(dp[where, at].astype(F32))).astype(BF16)
            dp[where, at] = value

    if n == 1:
        act.gather_relay()
    act.gather_end()
    loads["weights"] = [
        local.start(
            full.at[e], wbuf.at[pl.ds(0, D), pl.ds(e * width + index * half, half)]
        )
        for index, full in enumerate((full_q, full_k, full_v))
        for e in range(2)
    ]

    def mid_tile(m, index):
        at = pl.ds(pl.multiple_of(m * wide, wide), wide)
        return dot(dp[pl.ds(index * R, R), :], wbig[at, pl.ds(0, U)], NT)

    pending = []
    turn = [0]

    def flush():
        for copies, work, m, e in pending:
            for copy in copies:
                copy.wait()
            if m:
                work.send(m, e)
        pending.clear()

    def unit(work, m, e, value, alone=False):
        block = work.block(m, e)
        a, b = block.shape
        if work.inner:
            cols = column_tile(b)
            count, shape = b // cols, (a, cols)
        else:
            lines = 512 if a % 512 == 0 else a
            count, shape = a // lines, (lines, b)

        def piece(ref, i):
            if work.inner:
                return ref.at[:, pl.ds(i * shape[1], shape[1])]
            return ref.at[pl.ds(i * shape[0], shape[0]), :]

        sources = [] if alone else work.sources(m, e)
        origins = [work.came.at[o - 1, e] for o in sources] + ([] if value else [block])

        def fetch(i):
            return [
                pltpu.make_async_copy(
                    piece(origin, i),
                    parts.at[i % 2, index, pl.ds(0, shape[0]), pl.ds(0, shape[1])],
                    part_sem.at[i % 2, index],
                )
                for index, origin in enumerate(origins)
            ]

        for o in sources:
            work.flying[o, e].wait_recv()
        for i in range(min(count, 2)):
            for copy in fetch(i):
                copy.start()
        copies = []
        for i in range(count):
            result = value(m, e, i, shape) if value else 0.0
            for index, copy in enumerate(fetch(i)):
                copy.wait()
                result = result + parts[
                    i % 2, index, pl.ds(0, shape[0]), pl.ds(0, shape[1])
                ].astype(F32)
            if i + 2 < count:
                for copy in fetch(i + 2):
                    copy.start()
            if i == 0:
                flush()
            slot = turn[0] % 2
            turn[0] += 1
            if len(copies) > 1:
                copies.pop(0).wait()
            stage[slot, pl.ds(0, shape[0]), pl.ds(0, shape[1])] = result.astype(BF16)
            copy = pltpu.make_async_copy(
                stage.at[slot, pl.ds(0, shape[0]), pl.ds(0, shape[1])],
                piece(block, i),
                stage_sem.at[slot],
            )
            copy.start()
            copies.append(copy)
        pending.append((copies, work, m, e))

    def units(work, pairs, value, alone=False):
        for m, e in pairs:
            unit(work, m, e, value, alone)

    def close(work, value):
        for e in (1, 0):
            unit(work, 0, e, value)
            flush()
            work.finish(e)

    def down_value(m, e, i, shape):
        at = pl.ds(e * uhalf + i * shape[0], shape[0])
        return dot(hidden_ref[0][:, at], rows[:, pl.ds(m * wide, wide)], TN)

    def up_value(m, e, i, shape):
        at = pl.ds(e * uhalf + i * shape[1], shape[1])
        return dot(wbig[pl.ds(L, L), pl.ds(m * wide, wide)], dp[:, at], TN)

    def outer_value(m, e, i, shape):
        at = pl.ds(e * half + i * shape[0], shape[0])
        return dot(context[:, at], abuf[:, pl.ds(m * wide, wide)], TN)

    def inner_value(m, e, i, shape):
        at = pl.ds(e * width + i * shape[1], shape[1])
        return dot(rows[:, pl.ds(m * wide, wide)], dqkv[:, at], TN)

    everything = [(m, e) for m in range(planes) for e in range(2)]
    weight_of = lambda m: bin(m).count("1")
    free = sorted(
        [p for p in everything if p[0] and not down.sources(*p)], key=lambda p: (-weight_of(p[0]), -p[1])
    )
    first_free = [p for p in free if weight_of(p[0]) == weight_of(planes - 1)]
    more_free = [p for p in free if p not in first_free]
    later = sorted(
        [p for p in everything if p[0] and down.sources(*p)],
        key=lambda p: (-weight_of(p[0]), -p[1]),
    )
    last = [(0, 0), (0, 1)]
    hidden_ref = [abuf.at[:, pl.ds(0, U)]]

    loaded("hidden")
    units(down, first_free, down_value)

    loaded("up")
    act.reduce_begin(mid_tile, 0, planes)

    @pl.loop(0, planes)
    def _(m):
        at = pl.ds(pl.multiple_of(m * wide, wide), wide)
        dfs[:, at] += mid_tile(m, 0)

    flush()
    again = [
        local.start(hidden_in, wbig.at[pl.ds(0, L), pl.ds(0, U)]),
        local.start(mid_in, wbig.at[pl.ds(L, L), pl.ds(0, D)]),
    ]
    for copy in again:
        copy.wait()
    hidden_ref[0] = wbig.at[pl.ds(0, L), pl.ds(0, U)]
    units(down, more_free, down_value)

    def mid_base(m):
        return dfs[:, pl.ds(pl.multiple_of(m * wide, wide), wide)]

    def mid_put(m, value):
        dfs[:, pl.ds(pl.multiple_of(m * wide, wide), wide)] = value

    act.reduce_finish(mid_base, mid_put)
    ends_acc[...] = jnp.zeros_like(ends_acc)
    ends_acc[0:3, :] = sums[...]

    @pl.loop(0, R // 16)
    def _(i):
        at = pl.ds(pl.multiple_of(i * 16, 16), 16)
        grad = dfs[at, :]
        normal = normed[at, :]
        scaled = grad * gain[1:2, :]
        d_sum = inverse[at, :] * (
            scaled - mean_of(scaled) - normal * mean_of(scaled * normal)
        )
        abuf[at, :] = d_sum.astype(BF16)
        dfs[at, :] = d_sum
        for index, value in enumerate((d_sum, grad * normal, grad)):
            ends_acc[3 + index : 4 + index, :] += jnp.sum(value, axis=0, keepdims=True)

    act.rows = abuf
    act.gather_start()
    flush()
    for m in range(planes):
        small_d[k.g ^ m] = ends_acc[:, m * wide : (m + 1) * wide]

    units(down, later, down_value)
    units(down, last, down_value, True)
    units(up, last, up_value, True)
    flush()
    loads["rows"] = [local.start(rows_in, rows)]
    for e in range(2):
        value = jnp.sum(dp[:, pl.ds(e * uhalf, uhalf)].astype(F32), axis=0, keepdims=True)
        line = lax.broadcasted_iota(jnp.int32, small_u.shape, 0)
        small_u[...] = jnp.where(line == places[e], value, small_u[...])
    loaded("attention")
    for step in range(n):
        if step == 1:
            act.gather_relay()
        act.gather_wait(step)
        where = pl.ds(step * 2 * R, 2 * R)
        total = dot(abuf[where, pl.ds(0, wide)], wo[0], NT)
        for m in range(1, planes):
            total = total + dot(abuf[where, pl.ds(m * wide, wide)], wo[m], NT)
        d_context[where, :] = total.astype(BF16)
    if n == 1:
        act.gather_relay()
    flush()
    units(up, first_free, up_value)
    units(outer, first_free + more_free, outer_value)
    units(outer, last, outer_value, True)
    act.gather_end()
    close(down, None)

    lane = lax.broadcasted_iota(jnp.int32, (R, HD), 1)
    per_half = half // HD

    def attend_head(head):
        at = pl.ds(pl.multiple_of(head * HD, HD), HD)
        base = (head // per_half) * width + (head % per_half) * HD
        ats = [pl.ds(pl.multiple_of(base + index * half, HD), HD) for index in range(3)]
        dk[...] = jnp.zeros_like(dk)
        dv[...] = jnp.zeros_like(dv)

        @pl.loop(0, T)
        def _(piece):
            where = pl.ds(pl.multiple_of(piece * R, R), R)
            queries, keys, values = qkv[0, where, at], qkv[1, :, at], qkv[2, :, at]
            grads = d_context[where, at]
            scores = dot(queries, keys, NT) * HD ** (-0.5)
            same = label_column[where, :] == label_row[...]
            log_total = jnp.sum(jnp.where(lane == head, lse[where, :], 0.0), axis=-1, keepdims=True)
            probs = jnp.exp(jnp.where(same, scores, NEG) - log_total)
            d_probs = dot(grads, values, NT)
            inner_sum = jnp.sum(probs * d_probs, axis=-1, keepdims=True)
            d_scores = (probs * (d_probs - inner_sum)).astype(BF16)
            dqkv[where, ats[0]] = (dot(d_scores, keys) * HD ** (-0.5)).astype(BF16)
            dk[...] += dot(d_scores, queries, TN)
            dv[...] += dot(probs.astype(BF16), grads, TN)

        dqkv[:, ats[1]] = (dk[...] * HD ** (-0.5)).astype(BF16)
        dqkv[:, ats[2]] = dv[...].astype(BF16)

    count = C // HD

    @pl.loop(0, count // 2)
    def _(head):
        attend_head(head)

    units(up, more_free, up_value)
    flush()

    @pl.loop(count // 2, count)
    def _(head):
        attend_head(head)

    units(up, later, up_value)
    loaded("weights")

    def rows_tile(m, index):
        at = pl.ds(pl.multiple_of(m * wide, wide), wide)
        return dot(dqkv[pl.ds(index * R, R), :], wbuf[at, pl.ds(0, 2 * width)], NT)

    act.reduce_begin(rows_tile, 0, planes)
    loaded("rows")
    early = first_free + [p for p in more_free if p[1] == 1]
    units(inner, early, inner_value)
    flush()

    def rows_base(m):
        return rows_tile(m, 0) + dfs[:, pl.ds(pl.multiple_of(m * wide, wide), wide)]

    def rows_put(m, value):
        final_rows[:, pl.ds(pl.multiple_of(m * wide, wide), wide)] = value.astype(BF16)

    for e in range(2):
        for index, part in enumerate((0, 2)):
            at = pl.ds(e * width + part * half, half)
            value = jnp.sum(dqkv[:, at].astype(F32), axis=0, keepdims=True)
            to = pl.ds(index * half, half)
            line = lax.broadcasted_iota(jnp.int32, (2 * T, half), 0)
            small_q[:, to] = jnp.where(line == places[e], value, small_q[:, to])
    units(outer, later, outer_value)
    layer_done()
    act.reduce_finish(rows_base, rows_put)
    flush()
    input_done = trade(final_rows, input_grad)

    smalls = ((small_d, got_d), (small_q, got_q), (small_u, got_u))
    rounds = [[k.along(step) for step in range(1, n)]] if n > 1 else []
    rounds += [[k.mate()], [k.across()]]
    mask = 1
    while mask < planes:
        rounds.append([k.plane(mask)])
        mask *= 2
    small_slot = k.slots(3 * (n + 1 + planes))
    small_turn = [0]

    flying = []

    def small_start():
        for peer in rounds.pop(0) if rounds else []:
            for index, (mine, other) in enumerate(smalls):
                at = small_turn[0]
                copy = k.copy(small_slot + 3 * at + index, mine, other.at[at], peer)
                copy.start()
                flying.append((copy, mine, other.at[at]))
            small_turn[0] += 1

    def small_finish():
        for copy, mine, other in flying:
            copy.wait()
        for copy, mine, other in flying:
            mine[...] += other[...]
        flying.clear()

    small_start()
    close(up, None)
    small_finish()
    small_start()
    late = [p for p in later if p[1] == 1] + [p for p in more_free if p[1] == 0]
    late += [p for p in later if p[1] == 0]
    for m, e in late:
        unit(inner, m, e, inner_value)
        flush()
    small_finish()
    small_start()
    close(outer, None)
    small_finish()
    while rounds:
        small_start()
        small_finish()
    close(inner, inner_value)
    input_done()
    for work in (down, up, outer, inner):
        work.arrive()
    for copy in k.sent:
        copy.wait_send()


def backward(size, arrays):
    R, D, L, T = size.rows, size.dim, size.length, size.tp
    P_, n, wide, half, uhalf = size.planes, size.n, size.wide, size.half, size.uhalf
    C, U, fine = size.heads, size.units, size.fine
    width = 3 * half
    bits = P_.bit_length() - 1
    rounds = 2 + bits + n - 1
    shape = jax.ShapeDtypeStruct
    m = max(P_ - 1, 1)
    outs = [
        shape((R, D), BF16),
        shape((R, D), BF16),
        shape((P_, U, wide), BF16),
        shape((2, D, uhalf), BF16),
        shape((P_, C, wide), BF16),
        shape((2, D, width), BF16),
        shape((m, 2, uhalf, wide), BF16),
        shape((m, 2, wide, uhalf), BF16),
        shape((m, 2, half, wide), BF16),
        shape((m, 2, wide, width), BF16),
        shape((3, uhalf, fine), BF16),
        shape((3, fine, uhalf), BF16),
        shape((3, half, fine), BF16),
        shape((3, fine, width), BF16),
    ]
    smalls = [
        shape((P_, 8, wide), F32),
        shape((2 * T, 2 * half), F32),
        shape((2 * T, uhalf), F32),
    ]
    anywhere = pl.BlockSpec(memory_space=pl.ANY)
    vmem = pl.BlockSpec(memory_space=pltpu.VMEM)
    tall, broad = max(U, D), max(D, 2 * width)
    slots = 2 * n + 2 * n * P_ + 4 * (2 * P_ + 1) + 2 * P_ + 3 * (n + 1 + P_)
    far = max(n - 1, 1) * P_
    tile = (
        max(min(512, uhalf), wide, half),
        max(wide, column_tile(uhalf), column_tile(width)),
    )
    scratch = [
        pltpu.VMEM((L, D), BF16),
        pltpu.VMEM((tall, broad), BF16),
        pltpu.VMEM((max(D, 2 * L), max(U, D)), BF16),
        pltpu.VMEM((P_, C, wide), BF16),
        pltpu.VMEM((L, max(U, D)), BF16),
        pltpu.VMEM((L, U), BF16),
        pltpu.VMEM((3, L, C), BF16),
        pltpu.VMEM((L, 3 * C), BF16),
        pltpu.VMEM((L, C), BF16),
        pltpu.VMEM((L, C), BF16),
        pltpu.VMEM((L, HD), F32),
        pltpu.VMEM((P_, R, wide), BF16),
        pltpu.VMEM((n * P_, R, wide), BF16),
        pltpu.VMEM((far, R, wide), BF16),
        pltpu.VMEM((far, R, wide), BF16),
        pltpu.VMEM((R, D), F32),
        pltpu.VMEM((L, HD), F32),
        pltpu.VMEM((L, HD), F32),
        pltpu.VMEM((2,) + tile, BF16),
        pltpu.VMEM((2, bits + 1) + tile, BF16),
        pltpu.VMEM((R, D), BF16),
        pltpu.VMEM((rounds, P_, 8, wide), F32),
        pltpu.VMEM((rounds, 2 * T, 2 * half), F32),
        pltpu.VMEM((rounds, 2 * T, uhalf), F32),
        pltpu.VMEM((8, D), F32),
        pltpu.VMEM((8, D), F32),
        pltpu.SemaphoreType.DMA((slots,)),
        pltpu.SemaphoreType.DMA((slots,)),
        pltpu.SemaphoreType.DMA((32 + 3 * P_,)),
        pltpu.SemaphoreType.DMA((2,)),
        pltpu.SemaphoreType.DMA((2, bits + 1)),
    ]
    return pl.pallas_call(
        functools.partial(backward_kernel, size),
        out_shape=outs + smalls,
        in_specs=[anywhere] * 13 + [vmem, vmem, anywhere, anywhere] + [vmem] * 4,
        out_specs=[anywhere] * 14 + [vmem] * 3,
        scratch_shapes=scratch,
        compiler_params=pltpu.CompilerParams(
            collective_id=1, has_side_effects=True, vmem_limit_bytes=VMEM
        ),
        name="backward",
    )(*arrays)


def shards(
    fsdp,
    tp,
    inputs,
    query_weight,
    query_bias,
    key_weight,
    value_weight,
    value_bias,
    output_weight,
    output_bias,
    first_gain,
    first_shift,
    up_weight,
    up_bias,
    down_weight,
    down_bias,
    second_gain,
    second_shift,
    segments,
    cotangent,
):
    size = Sizes(fsdp, tp, inputs, query_weight, up_weight, segments)
    f, t = lax.axis_index("fsdp"), lax.axis_index("tp")
    c = f % 2
    residual = jnp.stack(
        [output_bias, first_gain, first_shift, down_bias, second_gain, second_shift]
        + [output_bias] * 2
    )
    residual = residual.reshape(8, size.planes, size.wide).transpose(1, 0, 2)
    role_bias = jnp.concatenate(
        [v.reshape(2, -1) for v in (query_bias, value_bias, up_bias)], axis=1
    )[:, None]
    kept = forward(
        size,
        (
            inputs,
            cotangent,
            segments.reshape(tp, 1, size.rows),
            segments.reshape(size.length, 1),
            role_bias,
            residual,
            query_weight,
            key_weight,
            value_weight,
            output_weight,
            up_weight,
            down_weight,
        ),
    )
    results = backward(size, tuple(kept) + (residual,))
    layer_out, input_grad = results[:2]
    grad_d, grad_u, grad_o, grad_x = results[2:6]
    last_d, last_u, last_o, last_x, small_d, small_q, small_u = results[10:]

    def home(grad, axis):
        if axis == 1:
            return lax.dynamic_slice(grad, (0, c * size.fine, 0), (1, size.fine, grad.shape[2]))[0]
        shape = (1, grad.shape[1] // 2, size.fine)
        return lax.dynamic_slice(grad, (0, 0, c * size.fine), shape)[0]

    def owned(own, last, axis):
        mine = own.astype(F32) + last[1].astype(F32)
        other = last[0].astype(F32) + last[2].astype(F32)
        return jnp.where(
            c == 0,
            jnp.concatenate([mine, other], axis=axis),
            jnp.concatenate([other, mine], axis=axis),
        )

    half = size.half
    home_x = home(grad_x, 1)
    inner = []
    for i in range(3):
        at = slice(i * half, (i + 1) * half)
        inner.append(owned(home_x[:, at], last_x[:, :, at], 1))
    small_d = small_d.transpose(1, 0, 2).reshape(8, size.dim)
    residual_size = size.dim // (fsdp * tp)
    ends = lax.dynamic_slice(small_d, (0, (f * tp + t) * residual_size), (8, residual_size))

    def split(table):
        row = lax.dynamic_slice_in_dim(table, 2 * t, 2).reshape(1, -1)
        part = row.shape[1] // fsdp
        return lax.dynamic_slice_in_dim(row, f * part, part, axis=1)

    return (
        layer_out,
        input_grad,
        inner[0],
        split(small_q[:, :half]),
        inner[1],
        inner[2],
        split(small_q[:, half:]),
        owned(home(grad_o, 0), last_o, 0),
        ends[3],
        ends[4],
        ends[5],
        owned(home(grad_u, 1), last_u, 1),
        split(small_u),
        owned(home(grad_d, 0), last_d, 0),
        ends[0],
        ends[1],
        ends[2],
    )


def solution(mesh):
    fsdp, tp = mesh.shape["fsdp"], mesh.shape["tp"]

    def body(*arrays):
        return shards(fsdp, tp, *arrays)

    tokens, inner, outer = P(AXES, None), P("fsdp", "tp"), P("tp", "fsdp")
    placed = (
        tokens,
        inner,
        P("tp"),
        inner,
        inner,
        P("tp"),
        outer,
        P(),
        P(),
        P(),
        inner,
        P("tp"),
        outer,
        P(),
        P(),
        P(),
        P("fsdp", None),
        tokens,
    )
    return jax.shard_map(
        body,
        mesh=mesh,
        in_specs=placed,
        out_specs=(
            tokens,
            tokens,
            inner,
            outer,
            inner,
            inner,
            outer,
            outer,
            P(AXES),
            P(AXES),
            P(AXES),
            inner,
            outer,
            outer,
            P(AXES),
            P(AXES),
            P(AXES),
        ),
        check_vma=False,
    )
```

```python
import functools

import jax
import jax.numpy as jnp
from jax import lax
from jax.experimental import pallas as pl
from jax.experimental.pallas import tpu as pltpu
from jax.sharding import PartitionSpec as P

HD = 128
EPS = 1e-06
NEG = -1000000000.0
AXES = ("fsdp", "tp")
F32 = jnp.float32
BF16 = jnp.bfloat16
MESH = pl.DeviceIdType.MESH
VMEM = 62 * 2**20


def gelu_tanh(values):
    return jax.nn.gelu(values, approximate=True)


def dot(left, right, dims=((1,), (0,))):
    return lax.dot_general(left, right, (dims, ((), ())), preferred_element_type=F32)


NN, NT, TN = ((1,), (0,)), ((1,), (1,)), ((0,), (0,))


class Sizes:
    def __init__(self, fsdp, tp, inputs, query_weight, up_weight, segments):
        self.fsdp, self.tp = fsdp, tp
        self.planes, self.n = fsdp // 2, tp // 2
        self.rows, self.dim = inputs.shape
        self.length = segments.shape[1]
        self.fine = query_weight.shape[0]
        self.wide = 2 * self.fine
        self.heads = query_weight.shape[1]
        self.half = self.heads // 2
        self.units = up_weight.shape[1]
        self.uhalf = self.units // 2


INNER = (True, True, True, False, True, False)


class Links:
    def __init__(self, size, send, recv):
        self.size, self.send, self.recv = size, send, recv
        f, t = lax.axis_index("fsdp"), lax.axis_index("tp")
        self.g, self.c = f // 2, f % 2
        self.h, self.l = t // size.n, t % size.n
        self.done = set()
        self.sent = []
        self.next = 0

    def device(self, g, c, h, l):
        return (g * 2 + c, h * self.size.n + l)

    def mate(self):
        return self.device(self.g, 1 - self.c, self.h, self.l)

    def across(self):
        return self.device(self.g, self.c, 1 - self.h, self.l)

    def corner(self):
        return self.device(self.g, 1 - self.c, 1 - self.h, self.l)

    def plane(self, mask):
        return self.device(self.g ^ mask, self.c, self.h, self.l)

    def along(self, step):
        return self.device(self.g, self.c, self.h, (self.l + step) % self.size.n)

    def barrier(self):
        size = self.size
        peers = [self.mate(), self.across(), self.corner()]
        mask = 1
        while mask < size.planes:
            peers.append(self.plane(mask))
            mask *= 2
        peers += [self.along(step) for step in range(1, size.n)]
        semaphore = pltpu.get_barrier_semaphore()
        for peer in peers:
            pl.semaphore_signal(semaphore, inc=1, device_id=peer, device_id_type=MESH)
        pl.semaphore_wait(semaphore, len(peers))

    def slots(self, count=1):
        first = self.next
        self.next += count
        return first

    def copy(self, slot, source, target, device):
        return pltpu.make_async_remote_copy(
            src_ref=source,
            dst_ref=target,
            send_sem=self.send.at[slot],
            recv_sem=self.recv.at[slot],
            device_id=device,
            device_id_type=MESH,
        )

    def go(self, slot, source, target, device):
        copy = self.copy(slot, source, target, device)
        copy.start()
        self.sent.append(copy)
        return copy


class Local:
    def __init__(self, semaphores):
        self.semaphores, self.next = semaphores, 0

    def start(self, source, target):
        copy = pltpu.make_async_copy(source, target, self.semaphores.at[self.next])
        self.next += 1
        copy.start()
        return copy


class Spread:
    def __init__(self, links, local, shard, full, inner, hold):
        self.links, self.local, self.hold = links, local, hold
        self.shard, self.full, self.inner = shard, full, inner
        self.base = links.slots(3 + 2 * (links.size.planes - 1))
        self.waited = set()

    def part(self, index):
        axis = 1 if self.inner else 0
        width = self.shard.shape[axis] // 2
        at = pl.multiple_of(index * width, width)
        return self.shard.at[:, pl.ds(at, width)] if self.inner else self.shard.at[pl.ds(at, width)]

    def home(self, e, c):
        fine = self.links.size.fine
        at = pl.ds(pl.multiple_of(c * fine, fine), fine)
        if self.inner:
            return self.full.at[e, at, :]
        width = self.full.shape[1] // 2
        return self.full.at[0, pl.ds(e * width, width), at]

    def block(self, m, e=None):
        wide = self.links.size.wide
        if self.inner:
            at = pl.ds(m * wide, wide)
            return self.full.at[:, at, :] if e is None else self.full.at[e, at, :]
        width = self.full.shape[1] // 2
        return self.full.at[m] if e is None else self.full.at[m, pl.ds(e * width, width)]

    def near(self):
        k = self.links
        self.own = self.local.start(self.part(k.c), self.hold)
        self.steps = [k.go(self.base, self.part(1 - k.c), self.home(0, k.c), k.mate())]
        self.pieces = {}

    def keep(self):
        self.own.wait()
        self.own = self.local.start(self.hold, self.home(0, self.links.c))

    def far(self):
        k = self.links
        self.steps += [
            k.go(self.base + 1, self.part(k.c), self.home(1, k.c), k.across()),
            k.go(self.base + 2, self.part(1 - k.c), self.home(1, k.c), k.corner()),
        ]

    def plane(self, e):
        k = self.links
        if e == 0:
            self.own.wait()
            self.steps[0].wait_recv()
        else:
            self.steps[1].wait_recv()
            self.steps[2].wait_recv()
        mask = 1
        while mask < k.size.planes:
            self.pieces[mask, e] = k.go(
                self.base + 1 + 2 * mask + e, self.block(0, e), self.block(mask, e), k.plane(mask)
            )
            mask *= 2

    def arrive(self, m, e):
        if m and (m, e) not in self.waited:
            self.waited.add((m, e))
            self.pieces[m, e].wait_recv()

    def relay(self, e):
        k = self.links
        for m in sorted(range(1, k.size.planes), key=lambda v: bin(v).count("1")):
            if bin(m).count("1") > 1:
                bit = m & -m if e else 1 << (m.bit_length() - 1)
                self.arrive(m ^ bit, e)
                self.pieces[m, e] = k.go(
                    self.base + 1 + 2 * m + e,
                    self.block(m ^ bit, e),
                    self.block(m, e),
                    k.plane(bit),
                )

    def finish(self):
        for m in range(1, self.links.size.planes):
            for e in range(2):
                self.arrive(m, e)


class Activations:
    def __init__(self, links, rows, give, take, out, came):
        self.links, self.rows = links, rows
        self.give, self.take, self.out, self.came = give, take, out, came
        size = links.size
        self.gather_slots = links.slots(2 * size.n)
        self.mate_slots = links.slots(size.n * size.planes)
        self.along_slots = links.slots(size.n * size.planes)

    def piece(self, index):
        size = self.links.size
        return self.rows.at[pl.ds(index * size.rows, size.rows)]

    def gather_start(self):
        k, base = self.links, self.gather_slots
        self.far = [
            k.go(base + step, self.piece(0), self.piece(2 * step), k.along(step))
            for step in range(1, k.size.n)
        ]
        self.near = [k.go(base + k.size.n, self.piece(0), self.piece(1), k.mate())]

    def gather_relay(self):
        k, base = self.links, self.gather_slots
        for step in range(1, k.size.n):
            self.far[step - 1].wait_recv()
            self.near.append(
                k.go(
                    base + k.size.n + step,
                    self.piece(2 * step),
                    self.piece(2 * step + 1),
                    k.mate(),
                )
            )

    def gather_wait(self, step):
        self.near[step].wait_recv()

    def gather_end(self):
        over = self.far + self.near
        for copy in over:
            copy.wait_send()
        self.links.sent = [c for c in self.links.sent if all(c is not o for o in over)]

    def near_copy(self, step, m):
        k = self.links
        at = step * k.size.planes + m
        return k.copy(self.mate_slots + at, self.give.at[m], self.take.at[at], k.mate())

    def far_copy(self, step, m):
        k = self.links
        at = (step - 1) * k.size.planes + m
        return k.copy(self.along_slots + at, self.out.at[at], self.came.at[at], k.along(step))

    def reduce_near(self, step, tile, low, high):
        n = self.links.size.n
        index = 2 * ((n - step) % n)

        @pl.loop(low, high)
        def _(m):
            value = tile(m, index + 1).astype(BF16)
            if step != 1 and n > 1:
                self.near_copy(step - 1 if step else n - 1, m).wait_send()
            self.give[m] = value
            self.near_copy(step, m).start()

    def reduce_far(self, step, tile, low, high):
        planes, n = self.links.size.planes, self.links.size.n
        index = 2 * ((n - step) % n)

        @pl.loop(low, high)
        def _(m):
            total = tile(m, index)
            self.near_copy(step, m).wait_recv()
            total = total + self.take[step * planes + m].astype(F32)
            self.out[(step - 1) * planes + m] = total.astype(BF16)
            self.far_copy(step, m).start()

    def reduce_begin(self, tile, low, high):
        for step in range(1, self.links.size.n):
            self.reduce_near(step, tile, low, high)
            self.reduce_far(step, tile, low, high)
        self.reduce_near(0, tile, low, high)

    def reduce_finish(self, base, put):
        planes, n = self.links.size.planes, self.links.size.n

        @pl.loop(0, planes)
        def _(m):
            total = base(m)
            self.near_copy(0, m).wait_recv()
            total = total + self.take[m].astype(F32)
            for other in range(1, n):
                self.far_copy(other, m).wait_recv()
                total = total + self.came[(other - 1) * planes + m].astype(F32)
            put(m, total)

        @pl.loop(0, planes)
        def _(m):
            self.near_copy(0, m).wait_send()
            for step in range(1, n):
                self.far_copy(step, m).wait_send()


class Chunked:
    def __init__(self, links, rows):
        self.links, self.rows = links, rows
        self.base = links.slots(2 * links.size.n * links.size.planes)
        self.far, self.near = {}, {}

    def piece(self, index, m):
        size = self.links.size
        return self.rows.at[pl.ds(index * size.rows, size.rows), pl.ds(m * size.wide, size.wide)]

    def start(self, m):
        k = self.links
        n = k.size.n
        base = self.base + 2 * n * m
        for step in range(1, n):
            self.far[step, m] = k.go(
                base + step, self.piece(0, m), self.piece(2 * step, m), k.along(step)
            )
        self.near[0, m] = k.go(base + n, self.piece(0, m), self.piece(1, m), k.mate())

    def relay(self, m):
        k = self.links
        n = k.size.n
        base = self.base + 2 * n * m
        for step in range(1, n):
            self.far[step, m].wait_recv()
            self.near[step, m] = k.go(
                base + n + step, self.piece(2 * step, m), self.piece(2 * step + 1, m), k.mate()
            )

    def wait(self):
        for copy in self.near.values():
            copy.wait_recv()

    def end(self):
        over = list(self.far.values()) + list(self.near.values())
        for copy in over:
            copy.wait_send()
        self.links.sent = [c for c in self.links.sent if all(c is not o for o in over)]


def mean_of(value):
    return jnp.mean(value, axis=-1, keepdims=True)


def forward_kernel(size, *refs):
    (
        inputs,
        cotangent,
        label_row,
        label_column,
        role_bias,
        residual,
        *shards_,
    ) = refs[:12]
    (
        fulls_q,
        fulls_k,
        fulls_v,
        fulls_o,
        fulls_u,
        fulls_d,
        rows_out,
        qkv_out,
        context_out,
        lse_out,
        mid_out,
        pre_out,
        hidden_out,
        normed_out,
        inverse_out,
        final_out,
        d_second_out,
        sums_out,
        label_row_out,
        label_column_out,
    ) = refs[12:32]
    (
        rows,
        wq,
        qkv,
        context,
        lse,
        wo,
        wu,
        wd,
        hidden,
        pre,
        give,
        take,
        out,
        came,
        cot,
        labels_r,
        labels_c,
        bias,
        vectors,
        send,
        recv,
        near_sem,
        *holds,
    ) = refs[32:]
    k = Links(size, send, recv)
    local = Local(near_sem)
    R, D, L, wide, half, uhalf = (
        size.rows,
        size.dim,
        size.length,
        size.wide,
        size.half,
        size.uhalf,
    )
    planes, n = size.planes, size.n
    k.barrier()
    stay = k.c == k.h

    fulls = (fulls_q, fulls_k, fulls_v, fulls_o, fulls_u, fulls_d)
    spread = [
        Spread(k, local, shard, full, inner, hold)
        for shard, full, inner, hold in zip(shards_, fulls, INNER, holds)
    ]
    act = Activations(k, rows, give, take, out, came)
    begin = Chunked(k, rows)

    def trade(source, target):
        base = k.slots(planes)
        first_local = local.next
        local.next += planes

        def pieces(m):
            at = pl.multiple_of((k.g ^ m) * wide, wide)
            return source.at[:, pl.ds(at, wide)], target(m)

        @pl.when(stay)
        def _():
            for m in range(planes):
                a, b = pieces(m)
                pltpu.make_async_copy(a, b, near_sem.at[first_local + m]).start()

        @pl.when(jnp.logical_not(stay))
        def _():
            for m in range(planes):
                a, b = pieces(m)
                k.copy(base + m, a, b, k.corner()).start()

        def wait(blocks=range(planes)):
            @pl.when(stay)
            def _():
                for m in blocks:
                    a, b = pieces(m)
                    pltpu.make_async_copy(a, b, near_sem.at[first_local + m]).wait()

            @pl.when(jnp.logical_not(stay))
            def _():
                for m in blocks:
                    a, b = pieces(m)
                    k.copy(base + m, a, b, k.corner()).wait()

        return wait

    for index in range(3):
        spread[index].near()
    spread[0].far()
    spread[1].far()
    for index in range(3, 6):
        spread[index].near()
    for index in range(6):
        spread[index].keep()
    for index in range(3):
        spread[index].plane(0)
    rows_ready = trade(inputs, lambda m: rows.at[pl.ds(0, R), pl.ds(m * wide, wide)])

    label_slots = k.slots(2)
    label_pairs = ((label_row, labels_r), (label_column, labels_c))

    @pl.when(stay)
    def _():
        for index, (a, b) in enumerate(label_pairs):
            k.copy(label_slots + index, a, b, k.mate()).start()

    label_local = local.next
    local.next += 2

    @pl.when(stay)
    def _():
        for index, (a, b) in enumerate(label_pairs):
            pltpu.make_async_copy(a, b, near_sem.at[label_local + index]).start()

    bias_slot = k.slots()
    bias_copy = k.go(bias_slot, role_bias.at[k.c], bias.at[1], k.across())
    bias_local = local.start(role_bias.at[k.c], bias.at[0])

    for m in range(planes):
        vectors[:, pl.ds(m * wide, wide)] = residual[k.g ^ m]

    saved = []
    loads = {}

    def load(index, buffer):
        spread[index].finish()
        loads[index] = local.start(fulls[index], buffer)

    spread[0].plane(1)
    spread[2].far()
    for index in range(3):
        spread[index].relay(0)
    spread[1].plane(1)
    spread[3].far()
    spread[0].relay(1)
    for m in range(planes):
        rows_ready([m])
        begin.start(m)
    spread[2].plane(1)
    spread[4].far()
    spread[1].relay(1)
    spread[4].plane(0)
    for m in range(planes):
        begin.relay(m)
    spread[2].relay(1)
    spread[3].plane(0)
    spread[3].plane(1)
    begin.wait()
    saved.append(local.start(rows, rows_out))
    bias_copy.wait_recv()
    bias_local.wait()

    @pl.when(stay)
    def _():
        for index, (a, b) in enumerate(label_pairs):
            pltpu.make_async_copy(a, b, near_sem.at[label_local + index]).wait()
            k.copy(label_slots + index, a, b, k.mate()).wait_send()

    @pl.when(jnp.logical_not(stay))
    def _():
        for index, (a, b) in enumerate(label_pairs):
            k.copy(label_slots + index, a, b, k.mate()).wait_recv()

    load(0, wq.at[0])
    load(1, wq.at[1])
    for index in range(3):
        loads[index].wait()
        for e in range(2):
            result = dot(rows[...], wq[index % 2, e])
            if index != 1:
                at = 0 if index == 0 else half
                result = result + bias[e, :, pl.ds(at, half)]
            qkv[index, :, pl.ds(e * half, half)] = result.astype(BF16)
        if index == 0:
            load(2, wq.at[0])
    saved.append(local.start(qkv, qkv_out))
    begin.end()

    spread[4].relay(0)
    spread[3].relay(0)
    spread[3].relay(1)
    spread[4].plane(1)
    spread[5].far()
    order = []
    for step in range(n):
        for core in (k.c, 1 - k.c):
            order.append(core * n + (k.l + n - step) % n)
    row = jnp.concatenate([labels_r[q] for q in order], axis=-1)
    label_row_out[...] = row
    for piece, q in enumerate(order):
        column = labels_c[pl.ds(pl.multiple_of(q * R, R), R), :]
        label_column_out[pl.ds(piece * R, R), :] = column
        same = column == row

        lane = lax.broadcasted_iota(jnp.int32, (R, HD), 1)
        where = pl.ds(piece * R, R)

        def one(head, kept, where=where, same=same):
            at = pl.ds(pl.multiple_of(head * HD, HD), HD)
            scores = dot(qkv[0, where, at], qkv[1, :, at], NT) * HD ** (-0.5)
            scores = jnp.where(same, scores, NEG)
            top = jnp.max(scores, axis=-1, keepdims=True)
            weights = jnp.exp(scores - top)
            summed = jnp.sum(weights, axis=-1, keepdims=True)
            probs = (weights * (1.0 / summed)).astype(BF16)
            context[where, at] = dot(probs, qkv[2, :, at]).astype(BF16)
            return jnp.where(lane == head, top + jnp.log(summed), kept)

        lse[where, :] = lax.fori_loop(0, size.heads // HD, one, jnp.zeros((R, HD), F32))
        if piece == size.tp // 2 - 1:
            spread[5].plane(0)

    saved.append(local.start(context, context_out))
    saved.append(local.start(lse, lse_out))

    load(3, wo)
    loads[3].wait()

    def attn_tile(m, index):
        return dot(context[pl.ds(index * R, R), :], wo[m])

    def attn_put(m, value):
        at = pl.ds(pl.multiple_of(m * wide, wide), wide)
        normed_out[:, at] = value + rows[pl.ds(0, R), at].astype(F32) + vectors[0:1, at]

    saved[0].wait()
    act.reduce_begin(attn_tile, 0, planes)
    spread[4].relay(1)
    act.reduce_finish(lambda m: attn_tile(m, 0), attn_put)

    @pl.loop(0, R // 16)
    def _(i):
        at = pl.ds(pl.multiple_of(i * 16, 16), 16)
        summed = normed_out[at, :]
        center = summed - mean_of(summed)
        scale = lax.rsqrt(mean_of(center * center) + EPS)
        normed = center * scale
        normed_out[at, :] = normed
        inverse_out[at, :] = scale
        rows[at, :] = (normed * vectors[1:2, :] + vectors[2:3, :]).astype(BF16)

    act.gather_start()
    spread[5].relay(0)
    spread[5].plane(1)
    act.gather_relay()
    load(4, wu)
    loads[4].wait()
    tile = min(512, uhalf)
    for step in range(n):
        act.gather_wait(step)
        if step == n - 1:
            cot_ready = trade(cotangent, lambda m: cot.at[:, pl.ds(m * wide, wide)])
        where = pl.ds(step * 2 * R, 2 * R)
        for e in range(2):

            @pl.loop(0, uhalf // tile)
            def _(j, e=e, where=where):
                at = pl.ds(pl.multiple_of(j * tile, tile), tile)
                to = pl.ds(pl.multiple_of(e * uhalf + j * tile, tile), tile)
                skip = pl.ds(pl.multiple_of(2 * half + j * tile, 128), tile)
                value = dot(rows[where, :], wu[e, :, at]) + bias[e, :, skip]
                pre[where, to] = value.astype(BF16)
                hidden[where, to] = gelu_tanh(value).astype(BF16)

    saved.append(local.start(rows, mid_out))
    saved.append(local.start(pre, pre_out))
    saved.append(local.start(hidden, hidden_out))
    act.gather_end()

    def ffn_tile(m, index):
        return dot(hidden[pl.ds(index * R, R), :], wd[m])

    def ffn_put(m, value):
        at = pl.ds(pl.multiple_of(m * wide, wide), wide)
        first = normed_out[:, at] * vectors[1:2, at] + vectors[2:3, at]
        d_second_out[:, at] = value + first + vectors[3:4, at]

    counts = [bin(m).count("1") for m in range(planes)]
    low = 0
    while low < planes:
        high = low + 1
        while high < planes and (counts[high] > 1) == (counts[low] > 1) and low:
            high += 1
        if low == 1:
            spread[5].relay(1)
        pieces = []
        for m in range(low, high):
            spread[5].arrive(m, 0)
            spread[5].arrive(m, 1)
            pieces.append(local.start(fulls[5].at[m], wd.at[m]))
        for piece in pieces:
            piece.wait()
        act.reduce_begin(ffn_tile, low, high)
        low = high
    act.reduce_finish(lambda m: ffn_tile(m, 0), ffn_put)
    cot_ready()
    sums_out[...] = jnp.zeros_like(sums_out)

    @pl.loop(0, R // 16)
    def _(i):
        at = pl.ds(pl.multiple_of(i * 16, 16), 16)
        summed = d_second_out[at, :]
        center = summed - mean_of(summed)
        scale = lax.rsqrt(mean_of(center * center) + EPS)
        normed = center * scale
        final_out[at, :] = (normed * vectors[4:5, :] + vectors[5:6, :]).astype(BF16)
        grad = cot[at, :].astype(F32)
        scaled = grad * vectors[4:5, :]
        d_second = scale * (scaled - mean_of(scaled) - normed * mean_of(scaled * normed))
        d_second_out[at, :] = d_second
        for index, value in enumerate((d_second, grad * normed, grad)):
            sums_out[index : index + 1, :] += jnp.sum(value, axis=0, keepdims=True)

    for copy in saved[1:]:
        copy.wait()
    for copy in k.sent:
        copy.wait_send()


def forward(size, arrays):
    R, D, L, T = size.rows, size.dim, size.length, size.tp
    P_, n, wide, half, uhalf = size.planes, size.n, size.wide, size.half, size.uhalf
    C, U = size.heads, size.units
    whole = [jax.ShapeDtypeStruct((2, D, half), BF16)] * 3 + [
        jax.ShapeDtypeStruct((P_, C, wide), BF16),
        jax.ShapeDtypeStruct((2, D, uhalf), BF16),
        jax.ShapeDtypeStruct((P_, U, wide), BF16),
    ]
    kept = [
        jax.ShapeDtypeStruct((L, D), BF16),
        jax.ShapeDtypeStruct((3, L, C), BF16),
        jax.ShapeDtypeStruct((L, C), BF16),
        jax.ShapeDtypeStruct((L, HD), F32),
        jax.ShapeDtypeStruct((L, D), BF16),
        jax.ShapeDtypeStruct((L, U), BF16),
        jax.ShapeDtypeStruct((L, U), BF16),
    ]
    ends = [
        jax.ShapeDtypeStruct((R, D), F32),
        jax.ShapeDtypeStruct((R, 1), F32),
        jax.ShapeDtypeStruct((R, D), BF16),
        jax.ShapeDtypeStruct((R, D), F32),
        jax.ShapeDtypeStruct((3, D), F32),
        jax.ShapeDtypeStruct((1, L), jnp.int32),
        jax.ShapeDtypeStruct((L, 1), jnp.int32),
    ]
    anywhere = pl.BlockSpec(memory_space=pl.ANY)
    vmem = pl.BlockSpec(memory_space=pltpu.VMEM)
    width = 2 * half + uhalf
    slots = 6 * (3 + 2 * (P_ - 1)) + 2 * P_ + 3 + 2 * n + 4 * n * P_
    scratch = [
        pltpu.VMEM((L, D), BF16),
        pltpu.VMEM((2, 2, D, half), BF16),
        pltpu.VMEM((3, L, C), BF16),
        pltpu.VMEM((L, C), BF16),
        pltpu.VMEM((L, HD), F32),
        pltpu.VMEM((P_, C, wide), BF16),
        pltpu.VMEM((2, D, uhalf), BF16),
        pltpu.VMEM((P_, U, wide), BF16),
        pltpu.VMEM((L, U), BF16),
        pltpu.VMEM((L, U), BF16),
        pltpu.VMEM((P_, R, wide), BF16),
        pltpu.VMEM((n * P_, R, wide), BF16),
        pltpu.VMEM((max(n - 1, 1) * P_, R, wide), BF16),
        pltpu.VMEM((max(n - 1, 1) * P_, R, wide), BF16),
        pltpu.VMEM((R, D), BF16),
        pltpu.VMEM((T, 1, R), jnp.int32),
        pltpu.VMEM((L, 1), jnp.int32),
        pltpu.VMEM((2, 1, width), F32),
        pltpu.VMEM((8, D), F32),
        pltpu.SemaphoreType.DMA((slots,)),
        pltpu.SemaphoreType.DMA((slots,)),
        pltpu.SemaphoreType.DMA((32 + 2 * P_,)),
        *[pltpu.VMEM((size.fine, half), BF16)] * 3,
        pltpu.VMEM((half, size.fine), BF16),
        pltpu.VMEM((size.fine, uhalf), BF16),
        pltpu.VMEM((uhalf, size.fine), BF16),
    ]
    return pl.pallas_call(
        functools.partial(forward_kernel, size),
        out_shape=whole + kept + ends,
        in_specs=[anywhere, anywhere, vmem, vmem, vmem, vmem] + [anywhere] * 6,
        out_specs=[anywhere] * 13 + [vmem] * 7,
        scratch_shapes=scratch,
        compiler_params=pltpu.CompilerParams(
            collective_id=0, has_side_effects=True, vmem_limit_bytes=VMEM
        ),
        name="forward",
    )(*arrays)


class Collect:
    def __init__(self, links, grad, came, last, inner):
        self.links, self.grad, self.came, self.last, self.inner = links, grad, came, last, inner
        self.planes = links.size.planes
        self.base = links.slots(2 * (self.planes - 1) + 3)
        self.flying, self.final = {}, []

    def block(self, m, e):
        wide = self.links.size.wide
        if self.inner:
            return self.grad.at[e, pl.ds(m * wide, wide), :]
        width = self.grad.shape[1] // 2
        return self.grad.at[m, pl.ds(e * width, width), :]

    def home(self, e, c):
        fine = self.links.size.fine
        at = pl.ds(pl.multiple_of(c * fine, fine), fine)
        if self.inner:
            return self.grad.at[e, at, :]
        width = self.grad.shape[1] // 2
        return self.grad.at[0, pl.ds(e * width, width), at]

    @staticmethod
    def bit(m, e):
        return m & -m if e else 1 << (m.bit_length() - 1)

    def sources(self, m, e):
        return [o for o in range(1, self.planes) if o != m and o ^ self.bit(o, e) == m]

    def send(self, m, e):
        self.flying[m, e] = self.links.go(
            self.base + 2 * (m - 1) + e,
            self.block(m, e),
            self.came.at[m - 1, e],
            self.links.plane(self.bit(m, e)),
        )

    def finish(self, e):
        k = self.links
        base = self.base + 2 * (self.planes - 1)
        if e == 0:
            self.final.append(k.go(base, self.home(0, 1 - k.c), self.last.at[0], k.mate()))
            return
        self.final += [
            k.go(base + 1, self.home(1, k.c), self.last.at[1], k.across()),
            k.go(base + 2, self.home(1, 1 - k.c), self.last.at[2], k.corner()),
        ]

    def arrive(self):
        for copy in self.final:
            copy.wait_recv()


def column_tile(width):
    for tile in (512, 384):
        if width % tile == 0:
            return tile
    return width


def gelu_slope(v):
    scale = 0.7978845608028654
    square = v * v
    t = jnp.tanh(scale * v * (1.0 + 0.044715 * square))
    return 0.5 * (1.0 + t) + 0.5 * v * (1.0 - t * t) * scale * (1.0 + 3 * 0.044715 * square)


def backward_kernel(size, *refs):
    (
        full_q,
        full_k,
        full_v,
        full_o,
        full_u,
        full_d,
        rows_in,
        qkv_in,
        context_in,
        lse_in,
        mid_in,
        pre_in,
        hidden_in,
        normed,
        inverse,
        final,
        d_second,
        sums,
        label_row,
        label_column,
        residual,
    ) = refs[:21]
    (
        layer_out,
        input_grad,
        grad_d,
        grad_u,
        grad_o,
        grad_x,
        came_d,
        came_u,
        came_o,
        came_x,
        last_d,
        last_u,
        last_o,
        last_x,
        small_d,
        small_q,
        small_u,
    ) = refs[21:38]
    (
        rows,
        wbuf,
        wbig,
        wo,
        abuf,
        dp,
        qkv,
        dqkv,
        context,
        d_context,
        lse,
        give,
        take,
        out,
        came,
        dfs,
        dk,
        dv,
        stage,
        parts,
        final_rows,
        got_d,
        got_q,
        got_u,
        gain,
        ends_acc,
        send,
        recv,
        near_sem,
        stage_sem,
        part_sem,
    ) = refs[38:]
    k = Links(size, send, recv)
    local = Local(near_sem)
    R, D, L, wide, half, uhalf, T = (
        size.rows,
        size.dim,
        size.length,
        size.wide,
        size.half,
        size.uhalf,
        size.tp,
    )
    planes, n, C, U = size.planes, size.n, size.heads, size.units
    width = 3 * half
    act = Activations(k, rows, give, take, out, came)
    down = Collect(k, grad_d, came_d, last_d, False)
    up = Collect(k, grad_u, came_u, last_u, True)
    outer = Collect(k, grad_o, came_o, last_o, False)
    inner = Collect(k, grad_x, came_x, last_x, True)
    k.barrier()
    stay = k.c == k.h

    def trade(source, target):
        base = k.slots(planes)
        first_local = local.next
        local.next += planes

        def pieces(m):
            at = pl.multiple_of((k.g ^ m) * wide, wide)
            return source.at[:, pl.ds(m * wide, wide)], target.at[:, pl.ds(at, wide)]

        def both(go):
            @pl.when(stay)
            def _():
                for m in range(planes):
                    copy = pltpu.make_async_copy(*pieces(m), near_sem.at[first_local + m])
                    copy.start() if go else copy.wait()

            @pl.when(jnp.logical_not(stay))
            def _():
                for m in range(planes):
                    copy = k.copy(base + m, *pieces(m), k.corner())
                    copy.start() if go else copy.wait()

        both(True)
        return lambda: both(False)

    loads = {}
    start = local.start(d_second, dfs)
    loads["pre"] = [local.start(pre_in, dp)]
    loads["down"] = [
        local.start(full_d.at[m], wbuf.at[pl.ds(0, U), pl.ds(m * wide, wide)])
        for m in range(planes)
    ]
    start.wait()
    rows[pl.ds(0, R), :] = dfs[...].astype(BF16)
    act.gather_start()
    loads["hidden"] = [local.start(hidden_in, abuf.at[:, pl.ds(0, U)])]
    loads["up"] = [
        local.start(full_u.at[e], wbig.at[pl.ds(0, D), pl.ds(e * uhalf, uhalf)]) for e in range(2)
    ]
    loads["final"] = [local.start(final, final_rows)]
    loads["attention"] = [
        local.start(qkv_in, qkv),
        local.start(context_in, context),
        local.start(lse_in, lse),
        local.start(full_o, wo),
    ]
    for m in range(planes):
        gain[:, pl.ds(m * wide, wide)] = residual[k.g ^ m]

    def loaded(name):
        for copy in loads[name]:
            copy.wait()

    small_d[...] = jnp.zeros_like(small_d)
    small_q[...] = jnp.zeros_like(small_q)
    small_u[...] = jnp.zeros_like(small_u)
    places = [(k.h * n + k.l) * 2 + k.c, ((1 - k.h) * n + k.l) * 2 + k.c]

    tile = min(512, U)
    loaded("pre")
    loaded("down")
    for step in range(n):
        if step == 1:
            act.gather_relay()
        if step == n - 1:
            loaded("final")
            layer_done = trade(final_rows, layer_out)
        act.gather_wait(step)
        where = pl.ds(step * 2 * R, 2 * R)

        @pl.loop(0, U // tile)
        def _(j, where=where):
            at = pl.ds(pl.multiple_of(j * tile, tile), tile)
            d_hidden = dot(rows[where, :], wbuf[at, pl.ds(0, D)], NT)
            value = (d_hidden * gelu_slope(dp[where, at].astype(F32))).astype(BF16)
            dp[where, at] = value

    if n == 1:
        act.gather_relay()
    act.gather_end()
    loads["weights"] = [
        local.start(
            full.at[e], wbuf.at[pl.ds(0, D), pl.ds(e * width + index * half, half)]
        )
        for index, full in enumerate((full_q, full_k, full_v))
        for e in range(2)
    ]

    def mid_tile(m, index):
        at = pl.ds(pl.multiple_of(m * wide, wide), wide)
        return dot(dp[pl.ds(index * R, R), :], wbig[at, pl.ds(0, U)], NT)

    pending = []
    turn = [0]

    def flush():
        for copies, work, m, e in pending:
            for copy in copies:
                copy.wait()
            if m:
                work.send(m, e)
        pending.clear()

    def unit(work, m, e, value, alone=False):
        block = work.block(m, e)
        a, b = block.shape
        if work.inner:
            cols = column_tile(b)
            count, shape = b // cols, (a, cols)
        else:
            lines = 512 if a % 512 == 0 else a
            count, shape = a // lines, (lines, b)

        def piece(ref, i):
            if work.inner:
                return ref.at[:, pl.ds(i * shape[1], shape[1])]
            return ref.at[pl.ds(i * shape[0], shape[0]), :]

        sources = [] if alone else work.sources(m, e)
        origins = [work.came.at[o - 1, e] for o in sources] + ([] if value else [block])

        def fetch(i):
            return [
                pltpu.make_async_copy(
                    piece(origin, i),
                    parts.at[i % 2, index, pl.ds(0, shape[0]), pl.ds(0, shape[1])],
                    part_sem.at[i % 2, index],
                )
                for index, origin in enumerate(origins)
            ]

        if any((o, e) not in work.flying for o in sources):
            flush()
        for o in sources:
            work.flying[o, e].wait_recv()
        for i in range(min(count, 2)):
            for copy in fetch(i):
                copy.start()
        copies = []
        for i in range(count):
            result = value(m, e, i, shape) if value else 0.0
            for index, copy in enumerate(fetch(i)):
                copy.wait()
                result = result + parts[
                    i % 2, index, pl.ds(0, shape[0]), pl.ds(0, shape[1])
                ].astype(F32)
            if i + 2 < count:
                for copy in fetch(i + 2):
                    copy.start()
            if i == 0:
                flush()
            slot = turn[0] % 2
            turn[0] += 1
            if len(copies) > 1:
                copies.pop(0).wait()
            stage[slot, pl.ds(0, shape[0]), pl.ds(0, shape[1])] = result.astype(BF16)
            copy = pltpu.make_async_copy(
                stage.at[slot, pl.ds(0, shape[0]), pl.ds(0, shape[1])],
                piece(block, i),
                stage_sem.at[slot],
            )
            copy.start()
            copies.append(copy)
        pending.append((copies, work, m, e))

    def units(work, pairs, value, alone=False):
        for m, e in pairs:
            unit(work, m, e, value, alone)

    def close_half(work, e, value):
        unit(work, 0, e, value)
        flush()
        work.finish(e)

    def close(work, value):
        for e in (1, 0):
            close_half(work, e, value)

    def down_value(m, e, i, shape):
        at = pl.ds(e * uhalf + i * shape[0], shape[0])
        return dot(hidden_ref[0][:, at], rows[:, pl.ds(m * wide, wide)], TN)

    def up_value(m, e, i, shape):
        at = pl.ds(e * uhalf + i * shape[1], shape[1])
        return dot(wbig[pl.ds(L, L), pl.ds(m * wide, wide)], dp[:, at], TN)

    def outer_value(m, e, i, shape):
        at = pl.ds(e * half + i * shape[0], shape[0])
        return dot(context[:, at], abuf[:, pl.ds(m * wide, wide)], TN)

    def inner_value(m, e, i, shape):
        at = pl.ds(e * width + i * shape[1], shape[1])
        return dot(rows[:, pl.ds(m * wide, wide)], dqkv[:, at], TN)

    everything = [(m, e) for m in range(planes) for e in range(2)]
    weight_of = lambda m: bin(m).count("1")
    free = sorted(
        [p for p in everything if p[0] and not down.sources(*p)], key=lambda p: (-weight_of(p[0]), -p[1])
    )
    first_free = [p for p in free if weight_of(p[0]) == weight_of(planes - 1)]
    more_free = [p for p in free if p not in first_free]
    later = sorted(
        [p for p in everything if p[0] and down.sources(*p)],
        key=lambda p: (-weight_of(p[0]), -p[1]),
    )
    last = [(0, 0), (0, 1)]
    hidden_ref = [abuf.at[:, pl.ds(0, U)]]

    loaded("hidden")
    units(down, first_free, down_value)

    loaded("up")
    act.reduce_begin(mid_tile, 0, planes)

    @pl.loop(0, planes)
    def _(m):
        at = pl.ds(pl.multiple_of(m * wide, wide), wide)
        dfs[:, at] += mid_tile(m, 0)

    flush()
    again = [
        local.start(hidden_in, wbig.at[pl.ds(0, L), pl.ds(0, U)]),
        local.start(mid_in, wbig.at[pl.ds(L, L), pl.ds(0, D)]),
    ]
    for copy in again:
        copy.wait()
    hidden_ref[0] = wbig.at[pl.ds(0, L), pl.ds(0, U)]
    units(down, more_free, down_value)

    def mid_base(m):
        return dfs[:, pl.ds(pl.multiple_of(m * wide, wide), wide)]

    def mid_put(m, value):
        dfs[:, pl.ds(pl.multiple_of(m * wide, wide), wide)] = value

    act.reduce_finish(mid_base, mid_put)
    ends_acc[...] = jnp.zeros_like(ends_acc)
    ends_acc[0:3, :] = sums[...]

    @pl.loop(0, R // 16)
    def _(i):
        at = pl.ds(pl.multiple_of(i * 16, 16), 16)
        grad = dfs[at, :]
        normal = normed[at, :]
        scaled = grad * gain[1:2, :]
        d_sum = inverse[at, :] * (
            scaled - mean_of(scaled) - normal * mean_of(scaled * normal)
        )
        abuf[at, :] = d_sum.astype(BF16)
        dfs[at, :] = d_sum
        for index, value in enumerate((d_sum, grad * normal, grad)):
            ends_acc[3 + index : 4 + index, :] += jnp.sum(value, axis=0, keepdims=True)

    act.rows = abuf
    act.gather_start()
    flush()
    for m in range(planes):
        small_d[k.g ^ m] = ends_acc[:, m * wide : (m + 1) * wide]

    units(down, later, down_value)
    units(down, last, down_value, True)
    units(up, last, up_value, True)
    flush()
    loads["rows"] = [local.start(rows_in, rows)]
    for e in range(2):
        value = jnp.sum(dp[:, pl.ds(e * uhalf, uhalf)].astype(F32), axis=0, keepdims=True)
        line = lax.broadcasted_iota(jnp.int32, small_u.shape, 0)
        small_u[...] = jnp.where(line == places[e], value, small_u[...])
    loaded("attention")
    for step in range(n):
        if step == 1:
            act.gather_relay()
        act.gather_wait(step)
        where = pl.ds(step * 2 * R, 2 * R)
        total = dot(abuf[where, pl.ds(0, wide)], wo[0], NT)
        for m in range(1, planes):
            total = total + dot(abuf[where, pl.ds(m * wide, wide)], wo[m], NT)
        d_context[where, :] = total.astype(BF16)
    if n == 1:
        act.gather_relay()
    flush()
    units(up, first_free, up_value)
    units(outer, first_free + more_free, outer_value)
    units(outer, last, outer_value, True)
    act.gather_end()
    close(down, None)

    lane = lax.broadcasted_iota(jnp.int32, (R, HD), 1)
    per_half = half // HD

    def attend_head(head):
        at = pl.ds(pl.multiple_of(head * HD, HD), HD)
        base = (head // per_half) * width + (head % per_half) * HD
        ats = [pl.ds(pl.multiple_of(base + index * half, HD), HD) for index in range(3)]
        dk[...] = jnp.zeros_like(dk)
        dv[...] = jnp.zeros_like(dv)

        @pl.loop(0, T)
        def _(piece):
            where = pl.ds(pl.multiple_of(piece * R, R), R)
            queries, keys, values = qkv[0, where, at], qkv[1, :, at], qkv[2, :, at]
            grads = d_context[where, at]
            scores = dot(queries, keys, NT) * HD ** (-0.5)
            same = label_column[where, :] == label_row[...]
            log_total = jnp.sum(jnp.where(lane == head, lse[where, :], 0.0), axis=-1, keepdims=True)
            probs = jnp.exp(jnp.where(same, scores, NEG) - log_total)
            d_probs = dot(grads, values, NT)
            inner_sum = jnp.sum(probs * d_probs, axis=-1, keepdims=True)
            d_scores = (probs * (d_probs - inner_sum)).astype(BF16)
            dqkv[where, ats[0]] = (dot(d_scores, keys) * HD ** (-0.5)).astype(BF16)
            dk[...] += dot(d_scores, queries, TN)
            dv[...] += dot(probs.astype(BF16), grads, TN)

        dqkv[:, ats[1]] = (dk[...] * HD ** (-0.5)).astype(BF16)
        dqkv[:, ats[2]] = dv[...].astype(BF16)

    count = C // HD

    @pl.loop(0, count // 2)
    def _(head):
        attend_head(head)

    units(up, [p for p in more_free if p[1] == 1], up_value)
    flush()

    @pl.loop(count // 2, count)
    def _(head):
        attend_head(head)

    units(up, [p for p in later if p[1] == 1], up_value)
    units(outer, later, outer_value)
    loaded("weights")

    def rows_tile(m, index):
        at = pl.ds(pl.multiple_of(m * wide, wide), wide)
        return dot(dqkv[pl.ds(index * R, R), :], wbuf[at, pl.ds(0, 2 * width)], NT)

    act.reduce_begin(rows_tile, 0, planes)
    loaded("rows")
    early = first_free + [p for p in more_free if p[1] == 1]
    units(inner, early, inner_value)
    flush()

    def rows_base(m):
        return rows_tile(m, 0) + dfs[:, pl.ds(pl.multiple_of(m * wide, wide), wide)]

    def rows_put(m, value):
        final_rows[:, pl.ds(pl.multiple_of(m * wide, wide), wide)] = value.astype(BF16)

    for e in range(2):
        for index, part in enumerate((0, 2)):
            at = pl.ds(e * width + part * half, half)
            value = jnp.sum(dqkv[:, at].astype(F32), axis=0, keepdims=True)
            to = pl.ds(index * half, half)
            line = lax.broadcasted_iota(jnp.int32, (2 * T, half), 0)
            small_q[:, to] = jnp.where(line == places[e], value, small_q[:, to])
    close_half(up, 1, None)
    rest = [p for p in more_free if p[1] == 0] + [p for p in later if p[1] == 0]
    units(up, rest, up_value)
    flush()
    layer_done()
    act.reduce_finish(rows_base, rows_put)
    flush()
    input_done = trade(final_rows, input_grad)

    smalls = ((small_d, got_d), (small_q, got_q), (small_u, got_u))
    rounds = [[k.along(step) for step in range(1, n)]] if n > 1 else []
    rounds += [[k.mate()], [k.across()]]
    mask = 1
    while mask < planes:
        rounds.append([k.plane(mask)])
        mask *= 2
    small_slot = k.slots(3 * (n + 1 + planes))
    small_turn = [0]

    flying = []

    def small_start():
        for peer in rounds.pop(0) if rounds else []:
            for index, (mine, other) in enumerate(smalls):
                at = small_turn[0]
                copy = k.copy(small_slot + 3 * at + index, mine, other.at[at], peer)
                copy.start()
                flying.append((copy, mine, other.at[at]))
            small_turn[0] += 1

    def small_finish():
        for copy, mine, other in flying:
            copy.wait()
        for copy, mine, other in flying:
            mine[...] += other[...]
        flying.clear()

    small_start()
    close(outer, None)
    small_finish()
    small_start()
    late = [p for p in later if p[1] == 1] + [p for p in more_free if p[1] == 0]
    late += [p for p in later if p[1] == 0]
    for m, e in late:
        unit(inner, m, e, inner_value)
        flush()
    small_finish()
    small_start()
    close_half(up, 0, None)
    small_finish()
    while rounds:
        small_start()
        small_finish()
    close(inner, inner_value)
    input_done()
    for work in (down, up, outer, inner):
        work.arrive()
    for copy in k.sent:
        copy.wait_send()


def backward(size, arrays):
    R, D, L, T = size.rows, size.dim, size.length, size.tp
    P_, n, wide, half, uhalf = size.planes, size.n, size.wide, size.half, size.uhalf
    C, U, fine = size.heads, size.units, size.fine
    width = 3 * half
    bits = P_.bit_length() - 1
    rounds = 2 + bits + n - 1
    shape = jax.ShapeDtypeStruct
    m = max(P_ - 1, 1)
    outs = [
        shape((R, D), BF16),
        shape((R, D), BF16),
        shape((P_, U, wide), BF16),
        shape((2, D, uhalf), BF16),
        shape((P_, C, wide), BF16),
        shape((2, D, width), BF16),
        shape((m, 2, uhalf, wide), BF16),
        shape((m, 2, wide, uhalf), BF16),
        shape((m, 2, half, wide), BF16),
        shape((m, 2, wide, width), BF16),
        shape((3, uhalf, fine), BF16),
        shape((3, fine, uhalf), BF16),
        shape((3, half, fine), BF16),
        shape((3, fine, width), BF16),
    ]
    smalls = [
        shape((P_, 8, wide), F32),
        shape((2 * T, 2 * half), F32),
        shape((2 * T, uhalf), F32),
    ]
    anywhere = pl.BlockSpec(memory_space=pl.ANY)
    vmem = pl.BlockSpec(memory_space=pltpu.VMEM)
    tall, broad = max(U, D), max(D, 2 * width)
    slots = 2 * n + 2 * n * P_ + 4 * (2 * P_ + 1) + 2 * P_ + 3 * (n + 1 + P_)
    far = max(n - 1, 1) * P_
    tile = (
        max(min(512, uhalf), wide, half),
        max(wide, column_tile(uhalf), column_tile(width)),
    )
    scratch = [
        pltpu.VMEM((L, D), BF16),
        pltpu.VMEM((tall, broad), BF16),
        pltpu.VMEM((max(D, 2 * L), max(U, D)), BF16),
        pltpu.VMEM((P_, C, wide), BF16),
        pltpu.VMEM((L, max(U, D)), BF16),
        pltpu.VMEM((L, U), BF16),
        pltpu.VMEM((3, L, C), BF16),
        pltpu.VMEM((L, 3 * C), BF16),
        pltpu.VMEM((L, C), BF16),
        pltpu.VMEM((L, C), BF16),
        pltpu.VMEM((L, HD), F32),
        pltpu.VMEM((P_, R, wide), BF16),
        pltpu.VMEM((n * P_, R, wide), BF16),
        pltpu.VMEM((far, R, wide), BF16),
        pltpu.VMEM((far, R, wide), BF16),
        pltpu.VMEM((R, D), F32),
        pltpu.VMEM((L, HD), F32),
        pltpu.VMEM((L, HD), F32),
        pltpu.VMEM((2,) + tile, BF16),
        pltpu.VMEM((2, bits + 1) + tile, BF16),
        pltpu.VMEM((R, D), BF16),
        pltpu.VMEM((rounds, P_, 8, wide), F32),
        pltpu.VMEM((rounds, 2 * T, 2 * half), F32),
        pltpu.VMEM((rounds, 2 * T, uhalf), F32),
        pltpu.VMEM((8, D), F32),
        pltpu.VMEM((8, D), F32),
        pltpu.SemaphoreType.DMA((slots,)),
        pltpu.SemaphoreType.DMA((slots,)),
        pltpu.SemaphoreType.DMA((32 + 3 * P_,)),
        pltpu.SemaphoreType.DMA((2,)),
        pltpu.SemaphoreType.DMA((2, bits + 1)),
    ]
    return pl.pallas_call(
        functools.partial(backward_kernel, size),
        out_shape=outs + smalls,
        in_specs=[anywhere] * 13 + [vmem, vmem, anywhere, anywhere] + [vmem] * 4,
        out_specs=[anywhere] * 14 + [vmem] * 3,
        scratch_shapes=scratch,
        compiler_params=pltpu.CompilerParams(
            collective_id=1, has_side_effects=True, vmem_limit_bytes=VMEM
        ),
        name="backward",
    )(*arrays)


def shards(
    fsdp,
    tp,
    inputs,
    query_weight,
    query_bias,
    key_weight,
    value_weight,
    value_bias,
    output_weight,
    output_bias,
    first_gain,
    first_shift,
    up_weight,
    up_bias,
    down_weight,
    down_bias,
    second_gain,
    second_shift,
    segments,
    cotangent,
):
    size = Sizes(fsdp, tp, inputs, query_weight, up_weight, segments)
    f, t = lax.axis_index("fsdp"), lax.axis_index("tp")
    c = f % 2
    residual = jnp.stack(
        [output_bias, first_gain, first_shift, down_bias, second_gain, second_shift]
        + [output_bias] * 2
    )
    residual = residual.reshape(8, size.planes, size.wide).transpose(1, 0, 2)
    role_bias = jnp.concatenate(
        [v.reshape(2, -1) for v in (query_bias, value_bias, up_bias)], axis=1
    )[:, None]
    kept = forward(
        size,
        (
            inputs,
            cotangent,
            segments.reshape(tp, 1, size.rows),
            segments.reshape(size.length, 1),
            role_bias,
            residual,
            query_weight,
            key_weight,
            value_weight,
            output_weight,
            up_weight,
            down_weight,
        ),
    )
    results = backward(size, tuple(kept) + (residual,))
    layer_out, input_grad = results[:2]
    grad_d, grad_u, grad_o, grad_x = results[2:6]
    last_d, last_u, last_o, last_x, small_d, small_q, small_u = results[10:]

    def home(grad, axis):
        if axis == 1:
            return lax.dynamic_slice(grad, (0, c * size.fine, 0), (1, size.fine, grad.shape[2]))[0]
        shape = (1, grad.shape[1] // 2, size.fine)
        return lax.dynamic_slice(grad, (0, 0, c * size.fine), shape)[0]

    def owned(own, last, axis):
        mine = own.astype(F32) + last[1].astype(F32)
        other = last[0].astype(F32) + last[2].astype(F32)
        first = c == 0
        halves = [jnp.where(first, mine, other), jnp.where(first, other, mine)]
        return jnp.concatenate(halves, axis=axis)

    half = size.half
    home_x = home(grad_x, 1)
    inner = []
    for i in range(3):
        at = slice(i * half, (i + 1) * half)
        inner.append(owned(home_x[:, at], last_x[:, :, at], 1))
    small_d = small_d.transpose(1, 0, 2).reshape(8, size.dim)
    residual_size = size.dim // (fsdp * tp)
    ends = lax.dynamic_slice(small_d, (0, (f * tp + t) * residual_size), (8, residual_size))

    def split(table):
        row = lax.dynamic_slice_in_dim(table, 2 * t, 2).reshape(1, -1)
        part = row.shape[1] // fsdp
        return lax.dynamic_slice_in_dim(row, f * part, part, axis=1)

    return (
        layer_out,
        input_grad,
        inner[0],
        split(small_q[:, :half]),
        inner[1],
        inner[2],
        split(small_q[:, half:]),
        owned(home(grad_o, 0), last_o, 0),
        ends[3],
        ends[4],
        ends[5],
        owned(home(grad_u, 1), last_u, 1),
        split(small_u),
        owned(home(grad_d, 0), last_d, 0),
        ends[0],
        ends[1],
        ends[2],
    )


def solution(mesh):
    fsdp, tp = mesh.shape["fsdp"], mesh.shape["tp"]

    def body(*arrays):
        return shards(fsdp, tp, *arrays)

    tokens, inner, outer = P(AXES, None), P("fsdp", "tp"), P("tp", "fsdp")
    placed = (
        tokens,
        inner,
        P("tp"),
        inner,
        inner,
        P("tp"),
        outer,
        P(),
        P(),
        P(),
        inner,
        P("tp"),
        outer,
        P(),
        P(),
        P(),
        P("fsdp", None),
        tokens,
    )
    return jax.shard_map(
        body,
        mesh=mesh,
        in_specs=placed,
        out_specs=(
            tokens,
            tokens,
            inner,
            outer,
            inner,
            inner,
            outer,
            outer,
            P(AXES),
            P(AXES),
            P(AXES),
            inner,
            outer,
            outer,
            P(AXES),
            P(AXES),
            P(AXES),
        ),
        check_vma=False,
    )
```

```python
import functools

import jax
import jax.numpy as jnp
from jax import lax
from jax.experimental import pallas as pl
from jax.experimental.pallas import tpu as pltpu
from jax.sharding import PartitionSpec as P

HD = 128
EPS = 1e-06
NEG = -1000000000.0
AXES = ("fsdp", "tp")
F32 = jnp.float32
BF16 = jnp.bfloat16
MESH = pl.DeviceIdType.MESH
VMEM = 62 * 2**20


def gelu_tanh(values):
    return jax.nn.gelu(values, approximate=True)


def dot(left, right, dims=((1,), (0,))):
    return lax.dot_general(left, right, (dims, ((), ())), preferred_element_type=F32)


NN, NT, TN = ((1,), (0,)), ((1,), (1,)), ((0,), (0,))


class Sizes:
    def __init__(self, fsdp, tp, inputs, query_weight, up_weight, segments):
        self.fsdp, self.tp = fsdp, tp
        self.planes, self.n = fsdp // 2, tp // 2
        self.rows, self.dim = inputs.shape
        self.length = segments.shape[1]
        self.fine = query_weight.shape[0]
        self.wide = 2 * self.fine
        self.heads = query_weight.shape[1]
        self.half = self.heads // 2
        self.units = up_weight.shape[1]
        self.uhalf = self.units // 2


INNER = (True, True, True, False, True, False)


class Links:
    def __init__(self, size, send, recv):
        self.size, self.send, self.recv = size, send, recv
        f, t = lax.axis_index("fsdp"), lax.axis_index("tp")
        self.g, self.c = f // 2, f % 2
        self.h, self.l = t // size.n, t % size.n
        self.done = set()
        self.sent = []
        self.next = 0

    def device(self, g, c, h, l):
        return (g * 2 + c, h * self.size.n + l)

    def mate(self):
        return self.device(self.g, 1 - self.c, self.h, self.l)

    def across(self):
        return self.device(self.g, self.c, 1 - self.h, self.l)

    def corner(self):
        return self.device(self.g, 1 - self.c, 1 - self.h, self.l)

    def plane(self, mask):
        return self.device(self.g ^ mask, self.c, self.h, self.l)

    def along(self, step):
        return self.device(self.g, self.c, self.h, (self.l + step) % self.size.n)

    def barrier(self):
        size = self.size
        peers = [self.mate(), self.across(), self.corner()]
        mask = 1
        while mask < size.planes:
            peers.append(self.plane(mask))
            mask *= 2
        peers += [self.along(step) for step in range(1, size.n)]
        semaphore = pltpu.get_barrier_semaphore()
        for peer in peers:
            pl.semaphore_signal(semaphore, inc=1, device_id=peer, device_id_type=MESH)
        pl.semaphore_wait(semaphore, len(peers))

    def slots(self, count=1):
        first = self.next
        self.next += count
        return first

    def copy(self, slot, source, target, device):
        return pltpu.make_async_remote_copy(
            src_ref=source,
            dst_ref=target,
            send_sem=self.send.at[slot],
            recv_sem=self.recv.at[slot],
            device_id=device,
            device_id_type=MESH,
        )

    def go(self, slot, source, target, device):
        copy = self.copy(slot, source, target, device)
        copy.start()
        self.sent.append(copy)
        return copy


class Local:
    def __init__(self, semaphores):
        self.semaphores, self.next = semaphores, 0

    def start(self, source, target):
        copy = pltpu.make_async_copy(source, target, self.semaphores.at[self.next])
        self.next += 1
        copy.start()
        return copy


class Spread:
    def __init__(self, links, local, shard, full, inner, hold):
        self.links, self.local, self.hold = links, local, hold
        self.shard, self.full, self.inner = shard, full, inner
        self.base = links.slots(3 + 2 * (links.size.planes - 1))
        self.waited = set()

    def part(self, index):
        axis = 1 if self.inner else 0
        width = self.shard.shape[axis] // 2
        at = pl.multiple_of(index * width, width)
        return self.shard.at[:, pl.ds(at, width)] if self.inner else self.shard.at[pl.ds(at, width)]

    def home(self, e, c):
        fine = self.links.size.fine
        at = pl.ds(pl.multiple_of(c * fine, fine), fine)
        if self.inner:
            return self.full.at[e, at, :]
        width = self.full.shape[1] // 2
        return self.full.at[0, pl.ds(e * width, width), at]

    def block(self, m, e=None):
        wide = self.links.size.wide
        if self.inner:
            at = pl.ds(m * wide, wide)
            return self.full.at[:, at, :] if e is None else self.full.at[e, at, :]
        width = self.full.shape[1] // 2
        return self.full.at[m] if e is None else self.full.at[m, pl.ds(e * width, width)]

    def near(self):
        k = self.links
        self.own = self.local.start(self.part(k.c), self.hold)
        self.steps = [k.go(self.base, self.part(1 - k.c), self.home(0, k.c), k.mate())]
        self.pieces = {}

    def keep(self):
        self.own.wait()
        self.own = self.local.start(self.hold, self.home(0, self.links.c))

    def far(self):
        k = self.links
        self.steps += [
            k.go(self.base + 1, self.part(k.c), self.home(1, k.c), k.across()),
            k.go(self.base + 2, self.part(1 - k.c), self.home(1, k.c), k.corner()),
        ]

    def plane(self, e):
        k = self.links
        if e == 0:
            self.own.wait()
            self.steps[0].wait_recv()
        else:
            self.steps[1].wait_recv()
            self.steps[2].wait_recv()
        mask = 1
        while mask < k.size.planes:
            self.pieces[mask, e] = k.go(
                self.base + 1 + 2 * mask + e, self.block(0, e), self.block(mask, e), k.plane(mask)
            )
            mask *= 2

    def arrive(self, m, e):
        if m and (m, e) not in self.waited:
            self.waited.add((m, e))
            self.pieces[m, e].wait_recv()

    def relay(self, e):
        k = self.links
        for m in sorted(range(1, k.size.planes), key=lambda v: bin(v).count("1")):
            if bin(m).count("1") > 1:
                bit = m & -m if e else 1 << (m.bit_length() - 1)
                self.arrive(m ^ bit, e)
                self.pieces[m, e] = k.go(
                    self.base + 1 + 2 * m + e,
                    self.block(m ^ bit, e),
                    self.block(m, e),
                    k.plane(bit),
                )

    def finish(self):
        for m in range(1, self.links.size.planes):
            for e in range(2):
                self.arrive(m, e)


class Activations:
    def __init__(self, links, rows, give, take, out, came):
        self.links, self.rows = links, rows
        self.give, self.take, self.out, self.came = give, take, out, came
        size = links.size
        self.gather_slots = links.slots(2 * size.n)
        self.mate_slots = links.slots(size.n * size.planes)
        self.along_slots = links.slots(size.n * size.planes)

    def piece(self, index):
        size = self.links.size
        return self.rows.at[pl.ds(index * size.rows, size.rows)]

    def gather_start(self):
        k, base = self.links, self.gather_slots
        self.far = [
            k.go(base + step, self.piece(0), self.piece(2 * step), k.along(step))
            for step in range(1, k.size.n)
        ]
        self.near = [k.go(base + k.size.n, self.piece(0), self.piece(1), k.mate())]

    def gather_relay(self):
        k, base = self.links, self.gather_slots
        for step in range(1, k.size.n):
            self.far[step - 1].wait_recv()
            self.near.append(
                k.go(
                    base + k.size.n + step,
                    self.piece(2 * step),
                    self.piece(2 * step + 1),
                    k.mate(),
                )
            )

    def gather_wait(self, step):
        self.near[step].wait_recv()

    def gather_end(self):
        over = self.far + self.near
        for copy in over:
            copy.wait_send()
        self.links.sent = [c for c in self.links.sent if all(c is not o for o in over)]

    def near_copy(self, step, m):
        k = self.links
        at = step * k.size.planes + m
        return k.copy(self.mate_slots + at, self.give.at[m], self.take.at[at], k.mate())

    def far_copy(self, step, m):
        k = self.links
        at = (step - 1) * k.size.planes + m
        return k.copy(self.along_slots + at, self.out.at[at], self.came.at[at], k.along(step))

    def reduce_near(self, step, tile, low, high):
        n = self.links.size.n
        index = 2 * ((n - step) % n)

        @pl.loop(low, high)
        def _(m):
            value = tile(m, index + 1).astype(BF16)
            if step != 1 and n > 1:
                self.near_copy(step - 1 if step else n - 1, m).wait_send()
            self.give[m] = value
            self.near_copy(step, m).start()

    def reduce_far(self, step, tile, low, high):
        planes, n = self.links.size.planes, self.links.size.n
        index = 2 * ((n - step) % n)

        @pl.loop(low, high)
        def _(m):
            total = tile(m, index)
            self.near_copy(step, m).wait_recv()
            total = total + self.take[step * planes + m].astype(F32)
            self.out[(step - 1) * planes + m] = total.astype(BF16)
            self.far_copy(step, m).start()

    def reduce_begin(self, tile, low, high):
        for step in range(1, self.links.size.n):
            self.reduce_near(step, tile, low, high)
            self.reduce_far(step, tile, low, high)
        self.reduce_near(0, tile, low, high)

    def reduce_finish(self, base, put):
        planes, n = self.links.size.planes, self.links.size.n

        @pl.loop(0, planes)
        def _(m):
            total = base(m)
            self.near_copy(0, m).wait_recv()
            total = total + self.take[m].astype(F32)
            for other in range(1, n):
                self.far_copy(other, m).wait_recv()
                total = total + self.came[(other - 1) * planes + m].astype(F32)
            put(m, total)

        @pl.loop(0, planes)
        def _(m):
            self.near_copy(0, m).wait_send()
            for step in range(1, n):
                self.far_copy(step, m).wait_send()


class Chunked:
    def __init__(self, links, rows):
        self.links, self.rows = links, rows
        self.base = links.slots(2 * links.size.n * links.size.planes)
        self.far, self.near = {}, {}

    def piece(self, index, m):
        size = self.links.size
        return self.rows.at[pl.ds(index * size.rows, size.rows), pl.ds(m * size.wide, size.wide)]

    def start(self, m):
        k = self.links
        n = k.size.n
        base = self.base + 2 * n * m
        for step in range(1, n):
            self.far[step, m] = k.go(
                base + step, self.piece(0, m), self.piece(2 * step, m), k.along(step)
            )
        self.near[0, m] = k.go(base + n, self.piece(0, m), self.piece(1, m), k.mate())

    def relay(self, m):
        k = self.links
        n = k.size.n
        base = self.base + 2 * n * m
        for step in range(1, n):
            self.far[step, m].wait_recv()
            self.near[step, m] = k.go(
                base + n + step, self.piece(2 * step, m), self.piece(2 * step + 1, m), k.mate()
            )

    def wait(self):
        for copy in self.near.values():
            copy.wait_recv()

    def end(self):
        over = list(self.far.values()) + list(self.near.values())
        for copy in over:
            copy.wait_send()
        self.links.sent = [c for c in self.links.sent if all(c is not o for o in over)]


def mean_of(value):
    return jnp.mean(value, axis=-1, keepdims=True)


def forward_kernel(size, *refs):
    (
        inputs,
        cotangent,
        label_row,
        label_column,
        role_bias,
        residual,
        *shards_,
    ) = refs[:12]
    (
        fulls_q,
        fulls_k,
        fulls_v,
        fulls_o,
        fulls_u,
        fulls_d,
        rows_out,
        qkv_out,
        context_out,
        lse_out,
        mid_out,
        pre_out,
        hidden_out,
        normed_out,
        inverse_out,
        final_out,
        d_second_out,
        sums_out,
        label_row_out,
        label_column_out,
    ) = refs[12:32]
    (
        rows,
        wq,
        qkv,
        context,
        lse,
        wo,
        wu,
        wd,
        hidden,
        pre,
        give,
        take,
        out,
        came,
        cot,
        labels_r,
        labels_c,
        bias,
        vectors,
        send,
        recv,
        near_sem,
        *holds,
    ) = refs[32:]
    k = Links(size, send, recv)
    local = Local(near_sem)
    R, D, L, wide, half, uhalf = (
        size.rows,
        size.dim,
        size.length,
        size.wide,
        size.half,
        size.uhalf,
    )
    planes, n = size.planes, size.n
    k.barrier()
    stay = k.c == k.h

    fulls = (fulls_q, fulls_k, fulls_v, fulls_o, fulls_u, fulls_d)
    spread = [
        Spread(k, local, shard, full, inner, hold)
        for shard, full, inner, hold in zip(shards_, fulls, INNER, holds)
    ]
    act = Activations(k, rows, give, take, out, came)
    begin = Chunked(k, rows)

    def trade(source, target):
        base = k.slots(planes)
        first_local = local.next
        local.next += planes

        def pieces(m):
            at = pl.multiple_of((k.g ^ m) * wide, wide)
            return source.at[:, pl.ds(at, wide)], target(m)

        @pl.when(stay)
        def _():
            for m in range(planes):
                a, b = pieces(m)
                pltpu.make_async_copy(a, b, near_sem.at[first_local + m]).start()

        @pl.when(jnp.logical_not(stay))
        def _():
            for m in range(planes):
                a, b = pieces(m)
                k.copy(base + m, a, b, k.corner()).start()

        def wait(blocks=range(planes)):
            @pl.when(stay)
            def _():
                for m in blocks:
                    a, b = pieces(m)
                    pltpu.make_async_copy(a, b, near_sem.at[first_local + m]).wait()

            @pl.when(jnp.logical_not(stay))
            def _():
                for m in blocks:
                    a, b = pieces(m)
                    k.copy(base + m, a, b, k.corner()).wait()

        return wait

    for index in range(3):
        spread[index].near()
    spread[0].far()
    spread[1].far()
    for index in range(3, 6):
        spread[index].near()
    for index in range(6):
        spread[index].keep()
    for index in range(3):
        spread[index].plane(0)
    rows_ready = trade(inputs, lambda m: rows.at[pl.ds(0, R), pl.ds(m * wide, wide)])

    label_slots = k.slots(2)
    label_pairs = ((label_row, labels_r), (label_column, labels_c))

    @pl.when(stay)
    def _():
        for index, (a, b) in enumerate(label_pairs):
            k.copy(label_slots + index, a, b, k.mate()).start()

    label_local = local.next
    local.next += 2

    @pl.when(stay)
    def _():
        for index, (a, b) in enumerate(label_pairs):
            pltpu.make_async_copy(a, b, near_sem.at[label_local + index]).start()

    bias_slot = k.slots()
    bias_copy = k.go(bias_slot, role_bias.at[k.c], bias.at[1], k.across())
    bias_local = local.start(role_bias.at[k.c], bias.at[0])

    for m in range(planes):
        vectors[:, pl.ds(m * wide, wide)] = residual[k.g ^ m]

    saved = []
    loads = {}

    def load(index, buffer):
        spread[index].finish()
        loads[index] = local.start(fulls[index], buffer)

    spread[0].plane(1)
    spread[2].far()
    for index in range(3):
        spread[index].relay(0)
    spread[1].plane(1)
    spread[3].far()
    spread[0].relay(1)
    for m in range(planes):
        rows_ready([m])
        begin.start(m)
    spread[2].plane(1)
    spread[4].far()
    spread[1].relay(1)
    spread[4].plane(0)
    for m in range(planes):
        begin.relay(m)
    spread[2].relay(1)
    spread[3].plane(0)
    spread[3].plane(1)
    begin.wait()
    saved.append(local.start(rows, rows_out))
    bias_copy.wait_recv()
    bias_local.wait()

    @pl.when(stay)
    def _():
        for index, (a, b) in enumerate(label_pairs):
            pltpu.make_async_copy(a, b, near_sem.at[label_local + index]).wait()
            k.copy(label_slots + index, a, b, k.mate()).wait_send()

    @pl.when(jnp.logical_not(stay))
    def _():
        for index, (a, b) in enumerate(label_pairs):
            k.copy(label_slots + index, a, b, k.mate()).wait_recv()

    load(0, wq.at[0])
    load(1, wq.at[1])
    for index in range(3):
        loads[index].wait()
        for e in range(2):
            result = dot(rows[...], wq[index % 2, e])
            if index != 1:
                at = 0 if index == 0 else half
                result = result + bias[e, :, pl.ds(at, half)]
            qkv[index, :, pl.ds(e * half, half)] = result.astype(BF16)
        if index == 0:
            load(2, wq.at[0])
    saved.append(local.start(qkv, qkv_out))
    begin.end()

    spread[4].relay(0)
    spread[3].relay(0)
    spread[3].relay(1)
    spread[4].plane(1)
    spread[5].far()
    order = []
    for step in range(n):
        for core in (k.c, 1 - k.c):
            order.append(core * n + (k.l + n - step) % n)
    row = jnp.concatenate([labels_r[q] for q in order], axis=-1)
    label_row_out[...] = row
    for piece, q in enumerate(order):
        column = labels_c[pl.ds(pl.multiple_of(q * R, R), R), :]
        label_column_out[pl.ds(piece * R, R), :] = column
        same = column == row

        lane = lax.broadcasted_iota(jnp.int32, (R, HD), 1)
        where = pl.ds(piece * R, R)

        def one(head, kept, where=where, same=same):
            at = pl.ds(pl.multiple_of(head * HD, HD), HD)
            scores = dot(qkv[0, where, at], qkv[1, :, at], NT) * HD ** (-0.5)
            scores = jnp.where(same, scores, NEG)
            top = jnp.max(scores, axis=-1, keepdims=True)
            weights = jnp.exp(scores - top)
            summed = jnp.sum(weights, axis=-1, keepdims=True)
            probs = (weights * (1.0 / summed)).astype(BF16)
            context[where, at] = dot(probs, qkv[2, :, at]).astype(BF16)
            return jnp.where(lane == head, top + jnp.log(summed), kept)

        lse[where, :] = lax.fori_loop(0, size.heads // HD, one, jnp.zeros((R, HD), F32))
        if piece == size.tp // 2 - 1:
            spread[5].plane(0)

    saved.append(local.start(context, context_out))
    saved.append(local.start(lse, lse_out))

    load(3, wo)
    loads[3].wait()

    def attn_tile(m, index):
        return dot(context[pl.ds(index * R, R), :], wo[m])

    def attn_put(m, value):
        at = pl.ds(pl.multiple_of(m * wide, wide), wide)
        normed_out[:, at] = value + rows[pl.ds(0, R), at].astype(F32) + vectors[0:1, at]

    saved[0].wait()
    act.reduce_begin(attn_tile, 0, planes)
    spread[4].relay(1)
    act.reduce_finish(lambda m: attn_tile(m, 0), attn_put)

    @pl.loop(0, R // 16)
    def _(i):
        at = pl.ds(pl.multiple_of(i * 16, 16), 16)
        summed = normed_out[at, :]
        center = summed - mean_of(summed)
        scale = lax.rsqrt(mean_of(center * center) + EPS)
        normed = center * scale
        normed_out[at, :] = normed
        inverse_out[at, :] = scale
        rows[at, :] = (normed * vectors[1:2, :] + vectors[2:3, :]).astype(BF16)

    act.gather_start()
    spread[5].relay(0)
    spread[5].plane(1)
    act.gather_relay()
    load(4, wu)
    loads[4].wait()
    tile = min(512, uhalf)
    for step in range(n):
        act.gather_wait(step)
        if step == n - 1:
            cot_ready = trade(cotangent, lambda m: cot.at[:, pl.ds(m * wide, wide)])
        where = pl.ds(step * 2 * R, 2 * R)
        for e in range(2):

            @pl.loop(0, uhalf // tile)
            def _(j, e=e, where=where):
                at = pl.ds(pl.multiple_of(j * tile, tile), tile)
                to = pl.ds(pl.multiple_of(e * uhalf + j * tile, tile), tile)
                skip = pl.ds(pl.multiple_of(2 * half + j * tile, 128), tile)
                value = dot(rows[where, :], wu[e, :, at]) + bias[e, :, skip]
                pre[where, to] = value.astype(BF16)
                hidden[where, to] = gelu_tanh(value).astype(BF16)

    saved.append(local.start(rows, mid_out))
    saved.append(local.start(pre, pre_out))
    saved.append(local.start(hidden, hidden_out))
    act.gather_end()

    def ffn_tile(m, index):
        return dot(hidden[pl.ds(index * R, R), :], wd[m])

    def ffn_put(m, value):
        at = pl.ds(pl.multiple_of(m * wide, wide), wide)
        first = normed_out[:, at] * vectors[1:2, at] + vectors[2:3, at]
        d_second_out[:, at] = value + first + vectors[3:4, at]

    counts = [bin(m).count("1") for m in range(planes)]
    low = 0
    while low < planes:
        high = low + 1
        while high < planes and (counts[high] > 1) == (counts[low] > 1) and low:
            high += 1
        if low == 1:
            spread[5].relay(1)
        pieces = []
        for m in range(low, high):
            spread[5].arrive(m, 0)
            spread[5].arrive(m, 1)
            pieces.append(local.start(fulls[5].at[m], wd.at[m]))
        for piece in pieces:
            piece.wait()
        act.reduce_begin(ffn_tile, low, high)
        low = high
    act.reduce_finish(lambda m: ffn_tile(m, 0), ffn_put)
    cot_ready()
    sums_out[...] = jnp.zeros_like(sums_out)

    @pl.loop(0, R // 16)
    def _(i):
        at = pl.ds(pl.multiple_of(i * 16, 16), 16)
        summed = d_second_out[at, :]
        center = summed - mean_of(summed)
        scale = lax.rsqrt(mean_of(center * center) + EPS)
        normed = center * scale
        final_out[at, :] = (normed * vectors[4:5, :] + vectors[5:6, :]).astype(BF16)
        grad = cot[at, :].astype(F32)
        scaled = grad * vectors[4:5, :]
        d_second = scale * (scaled - mean_of(scaled) - normed * mean_of(scaled * normed))
        d_second_out[at, :] = d_second
        for index, value in enumerate((d_second, grad * normed, grad)):
            sums_out[index : index + 1, :] += jnp.sum(value, axis=0, keepdims=True)

    for copy in saved[1:]:
        copy.wait()
    for copy in k.sent:
        copy.wait_send()


def forward(size, arrays):
    R, D, L, T = size.rows, size.dim, size.length, size.tp
    P_, n, wide, half, uhalf = size.planes, size.n, size.wide, size.half, size.uhalf
    C, U = size.heads, size.units
    whole = [jax.ShapeDtypeStruct((2, D, half), BF16)] * 3 + [
        jax.ShapeDtypeStruct((P_, C, wide), BF16),
        jax.ShapeDtypeStruct((2, D, uhalf), BF16),
        jax.ShapeDtypeStruct((P_, U, wide), BF16),
    ]
    kept = [
        jax.ShapeDtypeStruct((L, D), BF16),
        jax.ShapeDtypeStruct((3, L, C), BF16),
        jax.ShapeDtypeStruct((L, C), BF16),
        jax.ShapeDtypeStruct((L, HD), F32),
        jax.ShapeDtypeStruct((L, D), BF16),
        jax.ShapeDtypeStruct((L, U), BF16),
        jax.ShapeDtypeStruct((L, U), BF16),
    ]
    ends = [
        jax.ShapeDtypeStruct((R, D), F32),
        jax.ShapeDtypeStruct((R, 1), F32),
        jax.ShapeDtypeStruct((R, D), BF16),
        jax.ShapeDtypeStruct((R, D), F32),
        jax.ShapeDtypeStruct((3, D), F32),
        jax.ShapeDtypeStruct((1, L), jnp.int32),
        jax.ShapeDtypeStruct((L, 1), jnp.int32),
    ]
    anywhere = pl.BlockSpec(memory_space=pl.ANY)
    vmem = pl.BlockSpec(memory_space=pltpu.VMEM)
    width = 2 * half + uhalf
    slots = 6 * (3 + 2 * (P_ - 1)) + 2 * P_ + 3 + 2 * n + 4 * n * P_
    scratch = [
        pltpu.VMEM((L, D), BF16),
        pltpu.VMEM((2, 2, D, half), BF16),
        pltpu.VMEM((3, L, C), BF16),
        pltpu.VMEM((L, C), BF16),
        pltpu.VMEM((L, HD), F32),
        pltpu.VMEM((P_, C, wide), BF16),
        pltpu.VMEM((2, D, uhalf), BF16),
        pltpu.VMEM((P_, U, wide), BF16),
        pltpu.VMEM((L, U), BF16),
        pltpu.VMEM((L, U), BF16),
        pltpu.VMEM((P_, R, wide), BF16),
        pltpu.VMEM((n * P_, R, wide), BF16),
        pltpu.VMEM((max(n - 1, 1) * P_, R, wide), BF16),
        pltpu.VMEM((max(n - 1, 1) * P_, R, wide), BF16),
        pltpu.VMEM((R, D), BF16),
        pltpu.VMEM((T, 1, R), jnp.int32),
        pltpu.VMEM((L, 1), jnp.int32),
        pltpu.VMEM((2, 1, width), F32),
        pltpu.VMEM((8, D), F32),
        pltpu.SemaphoreType.DMA((slots,)),
        pltpu.SemaphoreType.DMA((slots,)),
        pltpu.SemaphoreType.DMA((32 + 2 * P_,)),
        *[pltpu.VMEM((size.fine, half), BF16)] * 3,
        pltpu.VMEM((half, size.fine), BF16),
        pltpu.VMEM((size.fine, uhalf), BF16),
        pltpu.VMEM((uhalf, size.fine), BF16),
    ]
    return pl.pallas_call(
        functools.partial(forward_kernel, size),
        out_shape=whole + kept + ends,
        in_specs=[anywhere, anywhere, vmem, vmem, vmem, vmem] + [anywhere] * 6,
        out_specs=[anywhere] * 13 + [vmem] * 7,
        scratch_shapes=scratch,
        compiler_params=pltpu.CompilerParams(
            collective_id=0, has_side_effects=True, vmem_limit_bytes=VMEM
        ),
        name="forward",
    )(*arrays)


class Collect:
    def __init__(self, links, grad, came, last, inner):
        self.links, self.grad, self.came, self.last, self.inner = links, grad, came, last, inner
        self.planes = links.size.planes
        self.base = links.slots(2 * (self.planes - 1) + 3)
        self.flying, self.final = {}, []

    def block(self, m, e):
        wide = self.links.size.wide
        if self.inner:
            return self.grad.at[e, pl.ds(m * wide, wide), :]
        width = self.grad.shape[1] // 2
        return self.grad.at[m, pl.ds(e * width, width), :]

    def home(self, e, c):
        fine = self.links.size.fine
        at = pl.ds(pl.multiple_of(c * fine, fine), fine)
        if self.inner:
            return self.grad.at[e, at, :]
        width = self.grad.shape[1] // 2
        return self.grad.at[0, pl.ds(e * width, width), at]

    @staticmethod
    def bit(m, e):
        return m & -m if e else 1 << (m.bit_length() - 1)

    def sources(self, m, e):
        return [o for o in range(1, self.planes) if o != m and o ^ self.bit(o, e) == m]

    def send(self, m, e):
        self.flying[m, e] = self.links.go(
            self.base + 2 * (m - 1) + e,
            self.block(m, e),
            self.came.at[m - 1, e],
            self.links.plane(self.bit(m, e)),
        )

    def finish(self, e):
        k = self.links
        base = self.base + 2 * (self.planes - 1)
        if e == 0:
            self.final.append(k.go(base, self.home(0, 1 - k.c), self.last.at[0], k.mate()))
            return
        self.final += [
            k.go(base + 1, self.home(1, k.c), self.last.at[1], k.across()),
            k.go(base + 2, self.home(1, 1 - k.c), self.last.at[2], k.corner()),
        ]

    def arrive(self):
        for copy in self.final:
            copy.wait_recv()


def column_tile(width):
    for tile in (512, 384):
        if width % tile == 0:
            return tile
    return width


def gelu_slope(v):
    scale = 0.7978845608028654
    square = v * v
    t = jnp.tanh(scale * v * (1.0 + 0.044715 * square))
    return 0.5 * (1.0 + t) + 0.5 * v * (1.0 - t * t) * scale * (1.0 + 3 * 0.044715 * square)


def backward_kernel(size, *refs):
    (
        full_q,
        full_k,
        full_v,
        full_o,
        full_u,
        full_d,
        rows_in,
        qkv_in,
        context_in,
        lse_in,
        mid_in,
        pre_in,
        hidden_in,
        normed,
        inverse,
        final,
        d_second,
        sums,
        label_row,
        label_column,
        residual,
    ) = refs[:21]
    (
        layer_out,
        input_grad,
        grad_d,
        grad_u,
        grad_o,
        grad_x,
        came_d,
        came_u,
        came_o,
        came_x,
        last_d,
        last_u,
        last_o,
        last_x,
        small_d,
        small_q,
        small_u,
    ) = refs[21:38]
    (
        rows,
        wbuf,
        wbig,
        wo,
        abuf,
        dp,
        qkv,
        dqkv,
        context,
        d_context,
        lse,
        give,
        take,
        out,
        came,
        dfs,
        dk,
        dv,
        stage,
        parts,
        final_rows,
        got_d,
        got_q,
        got_u,
        gain,
        ends_acc,
        send,
        recv,
        near_sem,
        stage_sem,
        part_sem,
    ) = refs[38:]
    k = Links(size, send, recv)
    local = Local(near_sem)
    R, D, L, wide, half, uhalf, T = (
        size.rows,
        size.dim,
        size.length,
        size.wide,
        size.half,
        size.uhalf,
        size.tp,
    )
    planes, n, C, U = size.planes, size.n, size.heads, size.units
    width = 3 * half
    act = Activations(k, rows, give, take, out, came)
    down = Collect(k, grad_d, came_d, last_d, False)
    up = Collect(k, grad_u, came_u, last_u, True)
    outer = Collect(k, grad_o, came_o, last_o, False)
    inner = Collect(k, grad_x, came_x, last_x, True)
    k.barrier()
    stay = k.c == k.h

    def trade(source, target):
        base = k.slots(planes)
        first_local = local.next
        local.next += planes

        def pieces(m):
            at = pl.multiple_of((k.g ^ m) * wide, wide)
            return source.at[:, pl.ds(m * wide, wide)], target.at[:, pl.ds(at, wide)]

        def both(go):
            @pl.when(stay)
            def _():
                for m in range(planes):
                    copy = pltpu.make_async_copy(*pieces(m), near_sem.at[first_local + m])
                    copy.start() if go else copy.wait()

            @pl.when(jnp.logical_not(stay))
            def _():
                for m in range(planes):
                    copy = k.copy(base + m, *pieces(m), k.corner())
                    copy.start() if go else copy.wait()

        both(True)
        return lambda: both(False)

    loads = {}
    start = local.start(d_second, dfs)
    loads["pre"] = [local.start(pre_in, dp)]
    loads["down"] = [
        local.start(full_d.at[m], wbuf.at[pl.ds(0, U), pl.ds(m * wide, wide)])
        for m in range(planes)
    ]
    start.wait()
    rows[pl.ds(0, R), :] = dfs[...].astype(BF16)
    act.gather_start()
    loads["hidden"] = [local.start(hidden_in, abuf.at[:, pl.ds(0, U)])]
    loads["up"] = [
        local.start(full_u.at[e], wbig.at[pl.ds(0, D), pl.ds(e * uhalf, uhalf)]) for e in range(2)
    ]
    loads["final"] = [local.start(final, final_rows)]
    loads["attention"] = [
        local.start(qkv_in, qkv),
        local.start(context_in, context),
        local.start(lse_in, lse),
        local.start(full_o, wo),
    ]
    for m in range(planes):
        gain[:, pl.ds(m * wide, wide)] = residual[k.g ^ m]

    def loaded(name):
        for copy in loads[name]:
            copy.wait()

    small_d[...] = jnp.zeros_like(small_d)
    small_q[...] = jnp.zeros_like(small_q)
    small_u[...] = jnp.zeros_like(small_u)
    places = [(k.h * n + k.l) * 2 + k.c, ((1 - k.h) * n + k.l) * 2 + k.c]

    tile = min(512, U)
    loaded("pre")
    loaded("down")
    for step in range(n):
        if step == 1:
            act.gather_relay()
        if step == n - 1:
            loaded("final")
            layer_done = trade(final_rows, layer_out)
        act.gather_wait(step)
        where = pl.ds(step * 2 * R, 2 * R)

        @pl.loop(0, U // tile)
        def _(j, where=where):
            at = pl.ds(pl.multiple_of(j * tile, tile), tile)
            d_hidden = dot(rows[where, :], wbuf[at, pl.ds(0, D)], NT)
            value = (d_hidden * gelu_slope(dp[where, at].astype(F32))).astype(BF16)
            dp[where, at] = value

    if n == 1:
        act.gather_relay()
    act.gather_end()
    loads["weights"] = [
        local.start(
            full.at[e], wbuf.at[pl.ds(0, D), pl.ds(e * width + index * half, half)]
        )
        for index, full in enumerate((full_q, full_k, full_v))
        for e in range(2)
    ]

    def mid_tile(m, index):
        at = pl.ds(pl.multiple_of(m * wide, wide), wide)
        return dot(dp[pl.ds(index * R, R), :], wbig[at, pl.ds(0, U)], NT)

    pending = []
    turn = [0]

    def flush():
        for copies, work, m, e in pending:
            for copy in copies:
                copy.wait()
            if m:
                work.send(m, e)
        pending.clear()

    def unit(work, m, e, value, alone=False):
        block = work.block(m, e)
        a, b = block.shape
        if work.inner:
            cols = column_tile(b)
            count, shape = b // cols, (a, cols)
        else:
            lines = 512 if a % 512 == 0 else a
            count, shape = a // lines, (lines, b)

        def piece(ref, i):
            if work.inner:
                return ref.at[:, pl.ds(i * shape[1], shape[1])]
            return ref.at[pl.ds(i * shape[0], shape[0]), :]

        sources = [] if alone else work.sources(m, e)
        origins = [work.came.at[o - 1, e] for o in sources] + ([] if value else [block])

        def fetch(i):
            return [
                pltpu.make_async_copy(
                    piece(origin, i),
                    parts.at[i % 2, index, pl.ds(0, shape[0]), pl.ds(0, shape[1])],
                    part_sem.at[i % 2, index],
                )
                for index, origin in enumerate(origins)
            ]

        if any((o, e) not in work.flying for o in sources):
            flush()
        for o in sources:
            work.flying[o, e].wait_recv()
        for i in range(min(count, 2)):
            for copy in fetch(i):
                copy.start()
        copies = []
        for i in range(count):
            result = value(m, e, i, shape) if value else 0.0
            for index, copy in enumerate(fetch(i)):
                copy.wait()
                result = result + parts[
                    i % 2, index, pl.ds(0, shape[0]), pl.ds(0, shape[1])
                ].astype(F32)
            if i + 2 < count:
                for copy in fetch(i + 2):
                    copy.start()
            if i == 0:
                flush()
            slot = turn[0] % 2
            turn[0] += 1
            if len(copies) > 1:
                copies.pop(0).wait()
            stage[slot, pl.ds(0, shape[0]), pl.ds(0, shape[1])] = result.astype(BF16)
            copy = pltpu.make_async_copy(
                stage.at[slot, pl.ds(0, shape[0]), pl.ds(0, shape[1])],
                piece(block, i),
                stage_sem.at[slot],
            )
            copy.start()
            copies.append(copy)
        pending.append((copies, work, m, e))

    def units(work, pairs, value, alone=False):
        for m, e in pairs:
            unit(work, m, e, value, alone)

    def close_half(work, e, value):
        unit(work, 0, e, value)
        flush()
        work.finish(e)

    def close(work, value):
        for e in (1, 0):
            close_half(work, e, value)

    def down_value(m, e, i, shape):
        at = pl.ds(e * uhalf + i * shape[0], shape[0])
        return dot(hidden_ref[0][:, at], rows[:, pl.ds(m * wide, wide)], TN)

    def up_value(m, e, i, shape):
        at = pl.ds(e * uhalf + i * shape[1], shape[1])
        return dot(wbig[pl.ds(L, L), pl.ds(m * wide, wide)], dp[:, at], TN)

    def outer_value(m, e, i, shape):
        at = pl.ds(e * half + i * shape[0], shape[0])
        return dot(context[:, at], abuf[:, pl.ds(m * wide, wide)], TN)

    def inner_value(m, e, i, shape):
        at = pl.ds(e * width + i * shape[1], shape[1])
        return dot(rows[:, pl.ds(m * wide, wide)], dqkv[:, at], TN)

    everything = [(m, e) for m in range(planes) for e in range(2)]
    weight_of = lambda m: bin(m).count("1")
    free = sorted(
        [p for p in everything if p[0] and not down.sources(*p)], key=lambda p: (-weight_of(p[0]), -p[1])
    )
    first_free = [p for p in free if weight_of(p[0]) == weight_of(planes - 1)]
    more_free = [p for p in free if p not in first_free]
    later = sorted(
        [p for p in everything if p[0] and down.sources(*p)],
        key=lambda p: (-weight_of(p[0]), -p[1]),
    )
    last = [(0, 0), (0, 1)]
    hidden_ref = [abuf.at[:, pl.ds(0, U)]]

    loaded("hidden")
    units(down, first_free, down_value)

    loaded("up")
    act.reduce_begin(mid_tile, 0, planes)

    @pl.loop(0, planes)
    def _(m):
        at = pl.ds(pl.multiple_of(m * wide, wide), wide)
        dfs[:, at] += mid_tile(m, 0)

    flush()
    again = [
        local.start(hidden_in, wbig.at[pl.ds(0, L), pl.ds(0, U)]),
        local.start(mid_in, wbig.at[pl.ds(L, L), pl.ds(0, D)]),
    ]
    for copy in again:
        copy.wait()
    hidden_ref[0] = wbig.at[pl.ds(0, L), pl.ds(0, U)]
    units(down, more_free, down_value)

    def mid_base(m):
        return dfs[:, pl.ds(pl.multiple_of(m * wide, wide), wide)]

    def mid_put(m, value):
        dfs[:, pl.ds(pl.multiple_of(m * wide, wide), wide)] = value

    act.reduce_finish(mid_base, mid_put)
    ends_acc[...] = jnp.zeros_like(ends_acc)
    ends_acc[0:3, :] = sums[...]

    @pl.loop(0, R // 16)
    def _(i):
        at = pl.ds(pl.multiple_of(i * 16, 16), 16)
        grad = dfs[at, :]
        normal = normed[at, :]
        scaled = grad * gain[1:2, :]
        d_sum = inverse[at, :] * (
            scaled - mean_of(scaled) - normal * mean_of(scaled * normal)
        )
        abuf[at, :] = d_sum.astype(BF16)
        dfs[at, :] = d_sum
        for index, value in enumerate((d_sum, grad * normal, grad)):
            ends_acc[3 + index : 4 + index, :] += jnp.sum(value, axis=0, keepdims=True)

    act.rows = abuf
    act.gather_start()
    flush()
    for m in range(planes):
        small_d[k.g ^ m] = ends_acc[:, m * wide : (m + 1) * wide]

    units(down, later, down_value)
    units(down, last, down_value, True)
    units(up, last, up_value, True)
    flush()
    loads["rows"] = [local.start(rows_in, rows)]
    for e in range(2):
        value = jnp.sum(dp[:, pl.ds(e * uhalf, uhalf)].astype(F32), axis=0, keepdims=True)
        line = lax.broadcasted_iota(jnp.int32, small_u.shape, 0)
        small_u[...] = jnp.where(line == places[e], value, small_u[...])
    loaded("attention")
    for step in range(n):
        if step == 1:
            act.gather_relay()
        act.gather_wait(step)
        where = pl.ds(step * 2 * R, 2 * R)
        total = dot(abuf[where, pl.ds(0, wide)], wo[0], NT)
        for m in range(1, planes):
            total = total + dot(abuf[where, pl.ds(m * wide, wide)], wo[m], NT)
        d_context[where, :] = total.astype(BF16)
    if n == 1:
        act.gather_relay()
    flush()
    units(up, first_free, up_value)
    units(outer, first_free + more_free, outer_value)
    units(outer, last, outer_value, True)
    act.gather_end()
    close(down, None)

    lane = lax.broadcasted_iota(jnp.int32, (R, HD), 1)
    per_half = half // HD

    def attend_head(head):
        at = pl.ds(pl.multiple_of(head * HD, HD), HD)
        base = (head // per_half) * width + (head % per_half) * HD
        ats = [pl.ds(pl.multiple_of(base + index * half, HD), HD) for index in range(3)]
        dk[...] = jnp.zeros_like(dk)
        dv[...] = jnp.zeros_like(dv)

        @pl.loop(0, T)
        def _(piece):
            where = pl.ds(pl.multiple_of(piece * R, R), R)
            queries, keys, values = qkv[0, where, at], qkv[1, :, at], qkv[2, :, at]
            grads = d_context[where, at]
            scores = dot(queries, keys, NT) * HD ** (-0.5)
            same = label_column[where, :] == label_row[...]
            log_total = jnp.sum(jnp.where(lane == head, lse[where, :], 0.0), axis=-1, keepdims=True)
            probs = jnp.exp(jnp.where(same, scores, NEG) - log_total)
            d_probs = dot(grads, values, NT)
            inner_sum = jnp.sum(probs * d_probs, axis=-1, keepdims=True)
            d_scores = (probs * (d_probs - inner_sum)).astype(BF16)
            dqkv[where, ats[0]] = (dot(d_scores, keys) * HD ** (-0.5)).astype(BF16)
            dk[...] += dot(d_scores, queries, TN)
            dv[...] += dot(probs.astype(BF16), grads, TN)

        dqkv[:, ats[1]] = (dk[...] * HD ** (-0.5)).astype(BF16)
        dqkv[:, ats[2]] = dv[...].astype(BF16)

    count = C // HD

    @pl.loop(0, count // 2)
    def _(head):
        attend_head(head)

    units(up, [p for p in more_free if p[1] == 1], up_value)
    flush()

    @pl.loop(count // 2, count)
    def _(head):
        attend_head(head)

    units(up, [p for p in later if p[1] == 1], up_value)
    units(outer, later, outer_value)
    loaded("weights")

    def rows_tile(m, index):
        at = pl.ds(pl.multiple_of(m * wide, wide), wide)
        return dot(dqkv[pl.ds(index * R, R), :], wbuf[at, pl.ds(0, 2 * width)], NT)

    act.reduce_begin(rows_tile, 0, planes)
    loaded("rows")
    early = first_free + [p for p in more_free if p[1] == 1]
    units(inner, early, inner_value)
    flush()

    def rows_base(m):
        return rows_tile(m, 0) + dfs[:, pl.ds(pl.multiple_of(m * wide, wide), wide)]

    def rows_put(m, value):
        final_rows[:, pl.ds(pl.multiple_of(m * wide, wide), wide)] = value.astype(BF16)

    for e in range(2):
        for index, part in enumerate((0, 2)):
            at = pl.ds(e * width + part * half, half)
            value = jnp.sum(dqkv[:, at].astype(F32), axis=0, keepdims=True)
            to = pl.ds(index * half, half)
            line = lax.broadcasted_iota(jnp.int32, (2 * T, half), 0)
            small_q[:, to] = jnp.where(line == places[e], value, small_q[:, to])
    close_half(up, 1, None)
    rest = [p for p in more_free if p[1] == 0] + [p for p in later if p[1] == 0]
    units(up, rest, up_value)
    flush()
    layer_done()
    act.reduce_finish(rows_base, rows_put)
    flush()
    input_done = trade(final_rows, input_grad)

    smalls = ((small_d, got_d), (small_q, got_q), (small_u, got_u))
    rounds = [[k.along(step) for step in range(1, n)]] if n > 1 else []
    rounds += [[k.mate()], [k.across()]]
    mask = 1
    while mask < planes:
        rounds.append([k.plane(mask)])
        mask *= 2
    small_slot = k.slots(3 * (n + 1 + planes))
    small_turn = [0]

    flying = []

    def small_start():
        for peer in rounds.pop(0) if rounds else []:
            for index, (mine, other) in enumerate(smalls):
                at = small_turn[0]
                copy = k.copy(small_slot + 3 * at + index, mine, other.at[at], peer)
                copy.start()
                flying.append((copy, mine, other.at[at]))
            small_turn[0] += 1

    def small_finish():
        for copy, mine, other in flying:
            copy.wait()
        for copy, mine, other in flying:
            mine[...] += other[...]
        flying.clear()

    small_start()
    close(outer, None)
    small_finish()
    small_start()
    late = [p for p in later if p[1] == 1] + [p for p in more_free if p[1] == 0]
    late += [p for p in later if p[1] == 0]
    for m, e in late:
        unit(inner, m, e, inner_value)
        flush()
    small_finish()
    small_start()
    close_half(inner, 1, inner_value)
    close_half(up, 0, None)
    small_finish()
    while rounds:
        small_start()
        small_finish()
    close_half(inner, 0, inner_value)
    input_done()
    for work in (down, up, outer, inner):
        work.arrive()
    for copy in k.sent:
        copy.wait_send()


def backward(size, arrays):
    R, D, L, T = size.rows, size.dim, size.length, size.tp
    P_, n, wide, half, uhalf = size.planes, size.n, size.wide, size.half, size.uhalf
    C, U, fine = size.heads, size.units, size.fine
    width = 3 * half
    bits = P_.bit_length() - 1
    rounds = 2 + bits + n - 1
    shape = jax.ShapeDtypeStruct
    m = max(P_ - 1, 1)
    outs = [
        shape((R, D), BF16),
        shape((R, D), BF16),
        shape((P_, U, wide), BF16),
        shape((2, D, uhalf), BF16),
        shape((P_, C, wide), BF16),
        shape((2, D, width), BF16),
        shape((m, 2, uhalf, wide), BF16),
        shape((m, 2, wide, uhalf), BF16),
        shape((m, 2, half, wide), BF16),
        shape((m, 2, wide, width), BF16),
        shape((3, uhalf, fine), BF16),
        shape((3, fine, uhalf), BF16),
        shape((3, half, fine), BF16),
        shape((3, fine, width), BF16),
    ]
    smalls = [
        shape((P_, 8, wide), F32),
        shape((2 * T, 2 * half), F32),
        shape((2 * T, uhalf), F32),
    ]
    anywhere = pl.BlockSpec(memory_space=pl.ANY)
    vmem = pl.BlockSpec(memory_space=pltpu.VMEM)
    tall, broad = max(U, D), max(D, 2 * width)
    slots = 2 * n + 2 * n * P_ + 4 * (2 * P_ + 1) + 2 * P_ + 3 * (n + 1 + P_)
    far = max(n - 1, 1) * P_
    tile = (
        max(min(512, uhalf), wide, half),
        max(wide, column_tile(uhalf), column_tile(width)),
    )
    scratch = [
        pltpu.VMEM((L, D), BF16),
        pltpu.VMEM((tall, broad), BF16),
        pltpu.VMEM((max(D, 2 * L), max(U, D)), BF16),
        pltpu.VMEM((P_, C, wide), BF16),
        pltpu.VMEM((L, max(U, D)), BF16),
        pltpu.VMEM((L, U), BF16),
        pltpu.VMEM((3, L, C), BF16),
        pltpu.VMEM((L, 3 * C), BF16),
        pltpu.VMEM((L, C), BF16),
        pltpu.VMEM((L, C), BF16),
        pltpu.VMEM((L, HD), F32),
        pltpu.VMEM((P_, R, wide), BF16),
        pltpu.VMEM((n * P_, R, wide), BF16),
        pltpu.VMEM((far, R, wide), BF16),
        pltpu.VMEM((far, R, wide), BF16),
        pltpu.VMEM((R, D), F32),
        pltpu.VMEM((L, HD), F32),
        pltpu.VMEM((L, HD), F32),
        pltpu.VMEM((2,) + tile, BF16),
        pltpu.VMEM((2, bits + 1) + tile, BF16),
        pltpu.VMEM((R, D), BF16),
        pltpu.VMEM((rounds, P_, 8, wide), F32),
        pltpu.VMEM((rounds, 2 * T, 2 * half), F32),
        pltpu.VMEM((rounds, 2 * T, uhalf), F32),
        pltpu.VMEM((8, D), F32),
        pltpu.VMEM((8, D), F32),
        pltpu.SemaphoreType.DMA((slots,)),
        pltpu.SemaphoreType.DMA((slots,)),
        pltpu.SemaphoreType.DMA((32 + 3 * P_,)),
        pltpu.SemaphoreType.DMA((2,)),
        pltpu.SemaphoreType.DMA((2, bits + 1)),
    ]
    return pl.pallas_call(
        functools.partial(backward_kernel, size),
        out_shape=outs + smalls,
        in_specs=[anywhere] * 13 + [vmem, vmem, anywhere, anywhere] + [vmem] * 4,
        out_specs=[anywhere] * 14 + [vmem] * 3,
        scratch_shapes=scratch,
        compiler_params=pltpu.CompilerParams(
            collective_id=1, has_side_effects=True, vmem_limit_bytes=VMEM
        ),
        name="backward",
    )(*arrays)


def shards(
    fsdp,
    tp,
    inputs,
    query_weight,
    query_bias,
    key_weight,
    value_weight,
    value_bias,
    output_weight,
    output_bias,
    first_gain,
    first_shift,
    up_weight,
    up_bias,
    down_weight,
    down_bias,
    second_gain,
    second_shift,
    segments,
    cotangent,
):
    size = Sizes(fsdp, tp, inputs, query_weight, up_weight, segments)
    f, t = lax.axis_index("fsdp"), lax.axis_index("tp")
    c = f % 2
    residual = jnp.stack(
        [output_bias, first_gain, first_shift, down_bias, second_gain, second_shift]
        + [output_bias] * 2
    )
    residual = residual.reshape(8, size.planes, size.wide).transpose(1, 0, 2)
    role_bias = jnp.concatenate(
        [v.reshape(2, -1) for v in (query_bias, value_bias, up_bias)], axis=1
    )[:, None]
    kept = forward(
        size,
        (
            inputs,
            cotangent,
            segments.reshape(tp, 1, size.rows),
            segments.reshape(size.length, 1),
            role_bias,
            residual,
            query_weight,
            key_weight,
            value_weight,
            output_weight,
            up_weight,
            down_weight,
        ),
    )
    results = backward(size, tuple(kept) + (residual,))
    layer_out, input_grad = results[:2]
    grad_d, grad_u, grad_o, grad_x = results[2:6]
    last_d, last_u, last_o, last_x, small_d, small_q, small_u = results[10:]

    def home(grad, axis):
        if axis == 1:
            return lax.dynamic_slice(grad, (0, c * size.fine, 0), (1, size.fine, grad.shape[2]))[0]
        shape = (1, grad.shape[1] // 2, size.fine)
        return lax.dynamic_slice(grad, (0, 0, c * size.fine), shape)[0]

    def owned(own, last, axis):
        mine = own.astype(F32) + last[1].astype(F32)
        other = last[0].astype(F32) + last[2].astype(F32)
        first = c == 0
        halves = [jnp.where(first, mine, other), jnp.where(first, other, mine)]
        return jnp.concatenate(halves, axis=axis)

    half = size.half
    home_x = home(grad_x, 1)
    inner = []
    for i in range(3):
        at = slice(i * half, (i + 1) * half)
        inner.append(owned(home_x[:, at], last_x[:, :, at], 1))
    small_d = small_d.transpose(1, 0, 2).reshape(8, size.dim)
    residual_size = size.dim // (fsdp * tp)
    ends = lax.dynamic_slice(small_d, (0, (f * tp + t) * residual_size), (8, residual_size))

    def split(table):
        row = lax.dynamic_slice_in_dim(table, 2 * t, 2).reshape(1, -1)
        part = row.shape[1] // fsdp
        return lax.dynamic_slice_in_dim(row, f * part, part, axis=1)

    return (
        layer_out,
        input_grad,
        inner[0],
        split(small_q[:, :half]),
        inner[1],
        inner[2],
        split(small_q[:, half:]),
        owned(home(grad_o, 0), last_o, 0),
        ends[3],
        ends[4],
        ends[5],
        owned(home(grad_u, 1), last_u, 1),
        split(small_u),
        owned(home(grad_d, 0), last_d, 0),
        ends[0],
        ends[1],
        ends[2],
    )


def solution(mesh):
    fsdp, tp = mesh.shape["fsdp"], mesh.shape["tp"]

    def body(*arrays):
        return shards(fsdp, tp, *arrays)

    tokens, inner, outer = P(AXES, None), P("fsdp", "tp"), P("tp", "fsdp")
    placed = (
        tokens,
        inner,
        P("tp"),
        inner,
        inner,
        P("tp"),
        outer,
        P(),
        P(),
        P(),
        inner,
        P("tp"),
        outer,
        P(),
        P(),
        P(),
        P("fsdp", None),
        tokens,
    )
    return jax.shard_map(
        body,
        mesh=mesh,
        in_specs=placed,
        out_specs=(
            tokens,
            tokens,
            inner,
            outer,
            inner,
            inner,
            outer,
            outer,
            P(AXES),
            P(AXES),
            P(AXES),
            inner,
            outer,
            outer,
            P(AXES),
            P(AXES),
            P(AXES),
        ),
        check_vma=False,
    )
```
